32 devices in a mesh: tensor: 4 (over y, core), batch: 8 (over z, x).
Axes of the slice: x: 2, y: 2, z: 4, core: 2. Of those that a mesh axis runs over, the one named last changes fastest.
Arguments:
- layer_in: bfloat16 [3, 4096, 1024], P(None, 'batch', 'tensor'), may hold values from -6 to 6
- encoder_states: bfloat16 [4096, 1024], P('batch', 'tensor'), may hold values from -6 to 6
- w_self: bfloat16 [3, 1024, 1024], P(None, None, 'tensor'), may hold values from -0.1875 to 0.1875
- w_rel: bfloat16 [1024, 512], P(None, 'tensor'), may hold values from -0.1875 to 0.1875
- w_cross: bfloat16 [3, 1024, 1024], P(None, None, 'tensor'), may hold values from -0.1875 to 0.1875
- w_attn_out: bfloat16 [2, 1024, 1024], P(None, 'tensor'), may hold values from -0.75 to 0.75
- w_in: bfloat16 [1024, 4096], P(None, 'tensor'), may hold values from -0.1875 to 0.1875
- w_out: bfloat16 [4096, 1024], P('tensor'), may hold values from -0.09375 to 0.09375
- proj_bias: float32 [4, 1024], P(None, 'tensor'), may hold values from -3 to 3
- rel_bias: float32 [512], P('tensor'), may hold values from -4 to 4
- ffn_in_bias: float32 [4096], P('tensor'), may hold values from -3 to 3
- out_bias: float32 [3, 1024], P(None, 'tensor'), may hold values from -0.7 to 10.7
- norm_gain: float32 [3, 1024], P(None, 'tensor'), may hold values from 0.5 to 1.5
- norm_bias: float32 [3, 1024], P(None, 'tensor'), may hold values from -2 to 2
- rel_buckets: int32 [512], replicated, may hold values from 0 to 31
- slot_log: int32 [8], P('batch'), may hold values from 0 to 2
- tgt_fill: int32 [8, 4], P('batch'), may hold values from 0 to 511
- enc_fill: int32 [8, 4], P('batch'), may hold values from 0 to 511
- out_grad: bfloat16 [3, 4096, 1024], P(None, 'batch', 'tensor'), may hold values from -6 to 6
Outputs:
- layer_out: bfloat16 [3, 4096, 1024], P(None, 'batch', 'tensor')
- grad_layer_in: float32 [3, 4096, 1024], P(None, 'batch', 'tensor')
- grad_encoder: float32 [4096, 1024], P('batch', 'tensor')
- grad_w_self: float32 [3, 1024, 1024], P(None, 'batch', 'tensor')
- grad_w_rel: float32 [1024, 512], P('batch', 'tensor')
- grad_w_cross: float32 [3, 1024, 1024], P(None, 'batch', 'tensor')
- grad_w_attn_out: float32 [2, 1024, 1024], P(None, 'tensor', 'batch')
- grad_w_in: float32 [1024, 4096], P('batch', 'tensor')
- grad_w_out: float32 [4096, 1024], P('tensor', 'batch')
- grad_proj_bias: float32 [4, 1024], P(None, ('tensor', 'batch'))
- grad_rel_bias: float32 [512], P(('tensor', 'batch'))
- grad_ffn_in_bias: float32 [4096], P(('tensor', 'batch'))
- grad_out_bias: float32 [3, 1024], P(None, ('tensor', 'batch'))
- grad_norm_gain: float32 [3, 1024], P(None, ('tensor', 'batch'))
- grad_norm_bias: float32 [3, 1024], P(None, ('tensor', 'batch'))
The draws below stay inside these ranges and needn't reach their ends.
All inputs are finite; a program needn't handle non-finite values.
Results may differ from the reference program's by a relative error of at most 0.033.
Values may be sent and summed in bfloat16 or wider, within the bound.
A program may use at most 192 MiB of HBM per device.

```python
from functools import partial
import jax
import jax.numpy as jnp
from jax import lax

D = 1024
HEADS = 16
HEAD_DIM = 64
FF = 4096
BUCKETS = 32
NGRAM = 2
MAXLEN = 512
MAXENC = 512
SLAB_COUNT = 8
TOKENS = 4096
ENC_TOKENS = 4096


def draw_out_bias(key, part):
    key = jax.random.fold_in(key, 11)
    first_key, second_key = jax.random.split(key)
    place = jnp.arange(D, dtype=jnp.float32) / D
    rise = 0.5 + 2.5 * place
    factor = jnp.exp(jax.random.uniform(first_key, (3, D), jnp.float32, -0.69, 0.69))
    noise = jax.random.uniform(second_key, (3, D), jnp.float32, -0.7, 0.7)
    return (rise[None, :] * factor + noise).astype(jnp.float32)


def set_ends(drawn, stream_key, least, top_value):
    spot = [jax.random.randint(jax.random.fold_in(stream_key, axis), (), 0, length) for axis, length in enumerate(drawn.shape)]
    main_axis = drawn.shape.index(max(drawn.shape))
    neighbour = spot[:main_axis] + [(spot[main_axis] + 1) % drawn.shape[main_axis]] + spot[main_axis + 1:]
    return drawn.at[tuple(spot)].set(least).at[tuple(neighbour)].set(top_value)


def strengthened(values, key, source, target, blocks, factor):
    def block_of(position):
        return (jnp.arange(values.shape[position]) // (values.shape[position] // blocks)).reshape((-1,) + (1,) * (values.ndim - 1 - position))

    first = jax.random.permutation(key, blocks)[block_of(target)]
    far = (block_of(target) + blocks // 2) % blocks
    return jnp.where((block_of(source) == first) | (block_of(source) == far), factor * values, values)


def shard_levels(stream_key, shape, cuts, smallest, high):
    level, own = 1.0, jax.random.fold_in(stream_key, 6)
    for axis_at, blocks in cuts:
        steps = jnp.exp(jax.random.uniform(jax.random.fold_in(own, axis_at), (blocks,), jnp.float32, smallest / len(cuts), high / len(cuts)))
        level = level * jnp.repeat(steps, shape[axis_at] // blocks).reshape([-1 if axis == axis_at else 1 for axis in range(len(shape))])
    return level


def bell_draw(rng, shape, scale, limit, cuts=(), kind=jnp.bfloat16):
    values = scale * jax.random.normal(rng, shape, jnp.float32)
    if cuts:
        values = values * shard_levels(rng, shape, cuts, -0.22, 0.18)
    return jnp.clip(values, -limit, limit).astype(kind)


def noise_with(rng, shape, scale, reach, pieces, heavy, kind=jnp.bfloat16):
    values = scale * jax.random.normal(rng, shape, jnp.float32)
    if pieces:
        values = values * shard_levels(rng, shape, pieces, -0.22, 0.18)
    return jnp.clip(strengthened(values, jax.random.fold_in(rng, 3), *heavy), -reach, reach).astype(kind)


def setup_inputs(seed: int = 0) -> dict:
    keys = jax.random.split(jax.random.key(seed), 20)
    layer_in = bell_draw(keys[0], (NGRAM + 1, TOKENS, D), 1.0, 6.0, ((1, 8), (2, 4)))
    encoder_states = bell_draw(keys[1], (ENC_TOKENS, D), 1.0, 6.0, ((0, 8), (1, 4)))
    w_self = bell_draw(keys[2], (3, D, D), D ** -0.5, 0.1875, ((2, 4),))
    w_rel = bell_draw(keys[3], (D, HEADS * BUCKETS), D ** -0.5, 0.1875, ((1, 4),))
    w_cross = bell_draw(keys[4], (3, D, D), D ** -0.5, 0.1875, ((2, 4),))
    w_attn_out = bell_draw(keys[5], (2, D, D), (D // 16) ** -0.5, 0.75, ((1, 4),))
    w_in = bell_draw(keys[6], (D, FF), D ** -0.5, 0.1875, ((1, 4),))
    w_out = bell_draw(keys[7], (FF, D), FF ** -0.5, 0.09375, ((0, 4),))
    proj_bias = bell_draw(keys[8], (4, D), 0.5, 3.0, ((1, 4),), jnp.float32)
    rel_bias = bell_draw(keys[9], (HEADS * BUCKETS,), 1.0, 4.0, ((0, 4),), jnp.float32)
    ffn_in_bias = bell_draw(keys[10], (FF,), 0.5, 3.0, ((0, 4),), jnp.float32)
    out_bias = draw_out_bias(jax.random.fold_in(keys[19], 71), 0)
    norm_gain = jnp.clip(1.0 + 0.1 * jax.random.normal(keys[12], (3, D), jnp.float32), 0.5, 1.5)
    norm_bias = bell_draw(keys[13], (3, D), 0.3, 2.0, ((1, 4),), jnp.float32)
    rel_buckets = set_ends(jax.random.randint(keys[14], (MAXLEN,), 0, BUCKETS), jax.random.fold_in(keys[14], 1), 0, BUCKETS - 1).astype(jnp.int32)
    slot_log = set_ends(jax.random.randint(keys[15], (SLAB_COUNT,), 0, 3), jax.random.fold_in(keys[15], 1), 0, 2).astype(jnp.int32)
    tgt_fill = set_ends(jax.random.randint(keys[16], (SLAB_COUNT, 4), 0, MAXLEN), jax.random.fold_in(keys[16], 1), 0, MAXLEN - 1).astype(jnp.int32)
    enc_fill = set_ends(jax.random.randint(keys[17], (SLAB_COUNT, 4), 0, MAXENC), jax.random.fold_in(keys[17], 1), 0, MAXENC - 1).astype(jnp.int32)
    out_grad = noise_with(keys[18], (NGRAM + 1, TOKENS, D), 1.0, 6.0, ((1, 8), (2, 4)), (1, 2, 8, 2.0))
    return {"layer_in": layer_in, "encoder_states": encoder_states, "w_self": w_self, "w_rel": w_rel, "w_cross": w_cross, "w_attn_out": w_attn_out, "w_in": w_in, "w_out": w_out, "proj_bias": proj_bias, "rel_bias": rel_bias, "ffn_in_bias": ffn_in_bias, "out_bias": out_bias, "norm_gain": norm_gain, "norm_bias": norm_bias, "rel_buckets": rel_buckets, "slot_log": slot_log, "tgt_fill": tgt_fill, "enc_fill": enc_fill, "out_grad": out_grad}


@jax.custom_vjp
def low(v):
    return lax.optimization_barrier(v.astype(jnp.bfloat16)).astype(jnp.float32)

@jax.custom_vjp
def low_back(v):
    return v

def low_keep(v):
    return (low(v), None)

def low_pass(kept, grad):
    return (grad,)

def back_keep(v):
    return (v, None)

def back_low(kept, grad):
    return (low(grad),)
low.defvjp(low_keep, low_pass)
low_back.defvjp(back_keep, back_low)
norm_eps = 1e-05
best = lax.Precision.HIGHEST
neg_big = -1e+30

def matmul(left, right):
    return jnp.matmul(left, right, precision=best)

def grouping(code, span):
    place = jnp.arange(span, dtype=jnp.int32)
    width = jnp.right_shift(jnp.int32(span), code)
    return (place, place // width, width)

def layout(code, fill, span):
    place, group, width = grouping(code, span)
    half = jnp.maximum(width // 2, 1)
    lengths = width - fill % half
    valid = place % width < jnp.take(lengths, group)
    return (group, valid)

def layer_norm(resid, gain, shift):
    mean = lax.optimization_barrier(jnp.mean(resid, axis=-1, keepdims=True))
    centred = resid - mean
    var = lax.optimization_barrier(jnp.mean(centred * centred, axis=-1, keepdims=True))
    return centred * lax.rsqrt(var + norm_eps) * gain + shift

def masked_softmax(score):
    top = lax.optimization_barrier(jnp.max(score, axis=-1, keepdims=True))
    weight = jnp.exp(score - top)
    return weight / lax.optimization_barrier(jnp.sum(weight, axis=-1, keepdims=True))

def self_block(args, onehot, own_pick):
    query, key, value, rel, code, fill = args
    span = query.shape[1]
    spots = jnp.arange(span, dtype=jnp.int32)
    group, valid = layout(code, fill, span)
    allowed = (group[:, None] == group[None, :]) & valid[None, :]
    factor = HEAD_DIM ** (-0.5)
    bias = jnp.einsum('nthb,tsb->nhts', rel, onehot, precision=best)
    score = low_back(jnp.einsum('nthd,shd->nhts', query, key[0], precision=best)) * factor + bias
    prob_main = masked_softmax(jnp.where(allowed & (spots[:, None] >= spots[None, :]), score[0], neg_big))
    ahead = jnp.where(allowed & (spots[:, None] > spots[None, :]), score[1:], neg_big)
    own = low_back(jnp.einsum('nthd,nthd->nht', query[1:], key[1:], precision=best)) * factor
    own = own + jnp.einsum('nthb,b->nht', rel[1:], own_pick, precision=best)
    top = jnp.maximum(lax.optimization_barrier(jnp.max(ahead, axis=-1)), own)
    weight = jnp.exp(ahead - top[..., None])
    weight_own = jnp.exp(own - top)
    total = lax.optimization_barrier(jnp.sum(weight, axis=-1)) + weight_own
    probs = low(jnp.concatenate([prob_main[None], weight / total[..., None]], axis=0))
    mixed = jnp.einsum('nhts,shd->nthd', probs, value[0], precision=best)
    own_part = jnp.transpose(low(weight_own / total), (0, 2, 1))[..., None] * value[1:]
    return jnp.concatenate([mixed[:1], mixed[1:] + own_part], axis=0)

def cross_block(args):
    query, ckey, cvalue, code, fill = args
    span = query.shape[1]
    espan = ckey.shape[0]
    group = grouping(code, span)[1]
    egroup, evalid = layout(code, fill, espan)
    allowed = (group[:, None] == egroup[None, :]) & evalid[None, :]
    score = low_back(jnp.einsum('nthd,ehd->nhte', query, ckey, precision=best)) * HEAD_DIM ** (-0.5)
    prob = masked_softmax(jnp.where(allowed, score, neg_big))
    return jnp.einsum('nhte,ehd->nthd', low(prob), cvalue, precision=best)

def reference(layer_in, encoder_states, w_self, w_rel, w_cross, w_attn_out, w_in, w_out, proj_bias, rel_bias, ffn_in_bias, out_bias, norm_gain, norm_bias, rel_buckets, slot_log, tgt_fill, enc_fill, out_grad):
    slabs = slot_log.shape[0]
    span = layer_in.shape[1] // slabs
    espan = encoder_states.shape[0] // slabs
    spots = jnp.arange(span, dtype=jnp.int32)
    gap = jnp.clip(spots[:, None] - spots[None, :], 0, span - 1)
    codes = jnp.arange(BUCKETS, dtype=jnp.int32)
    onehot = (jnp.take(rel_buckets, gap)[..., None] == codes).astype(jnp.float32)
    own_pick = (codes == rel_buckets[0]).astype(jnp.float32)
    attend = jax.checkpoint(partial(self_block, onehot=onehot, own_pick=own_pick))
    across = jax.checkpoint(cross_block)

    def slab_heads(v):
        return jnp.moveaxis(v.reshape(v.shape[0], slabs, span, HEADS, -1), 1, 0)

    def slab_rows(v):
        return jnp.moveaxis(v, 0, 1).reshape(v.shape[1], slabs * span, -1)

    def enc_heads(v):
        return v.reshape(slabs, espan, HEADS, -1)

    def forward(inputs, encoded, w_self, w_rel, w_cross, w_attn_out, w_in, w_out, proj_bias, rel_bias, ffn_in_bias, out_bias, norm_gain, norm_bias):
        query = low(low_back(matmul(inputs, w_self[0])) + proj_bias[0])
        key = low(low_back(matmul(inputs, w_self[1])))
        value = low(low_back(matmul(inputs, w_self[2])) + proj_bias[1])
        rel = low_back(matmul(inputs, w_rel)) + rel_bias
        att = lax.map(attend, (slab_heads(query), slab_heads(key), slab_heads(value), slab_heads(rel), slot_log, tgt_fill))
        att = low(low_back(slab_rows(att)))
        first = layer_norm(inputs + low_back(matmul(att, w_attn_out[0])) + out_bias[0], norm_gain[0], norm_bias[0])
        cquery = low(low_back(matmul(low(first), w_cross[0])) + proj_bias[2])
        ckey = low(low_back(matmul(encoded, w_cross[1])))
        cvalue = low(low_back(matmul(encoded, w_cross[2])) + proj_bias[3])
        catt = lax.map(across, (slab_heads(cquery), enc_heads(ckey), enc_heads(cvalue), slot_log, enc_fill))
        catt = low(low_back(slab_rows(catt)))
        second = layer_norm(first + low_back(matmul(catt, w_attn_out[1])) + out_bias[1], norm_gain[1], norm_bias[1])
        pre = low_back(matmul(low(second), w_in)) + ffn_in_bias
        act = low(jax.nn.gelu(pre, approximate=False))
        return layer_norm(second + low_back(matmul(act, w_out)) + out_bias[2], norm_gain[2], norm_bias[2])
    floats = tuple((v.astype(jnp.float32) for v in (layer_in, encoder_states, w_self, w_rel, w_cross, w_attn_out, w_in, w_out, proj_bias, rel_bias, ffn_in_bias, out_bias, norm_gain, norm_bias)))
    result, pullback = jax.vjp(forward, *floats)
    grads = pullback(out_grad.astype(jnp.float32))
    return (result.astype(jnp.bfloat16), grads[0], grads[1], grads[2], grads[3], grads[4], grads[5], grads[6], grads[7], grads[8], grads[9], grads[10], grads[11], grads[12], grads[13])
```

```python
import jax
import jax.numpy as jnp
from jax import lax
from jax.sharding import PartitionSpec as P

HEAD_DIM = 64


norm_eps = 1e-05
best = lax.Precision.HIGHEST
neg_big = -1e30


def grouping(code, span):
    place = jnp.arange(span, dtype=jnp.int32)
    width = jnp.right_shift(jnp.int32(span), code)
    return (place, place // width, width)


def layout(code, fill, span):
    place, group, width = grouping(code, span)
    half = jnp.maximum(width // 2, 1)
    lengths = width - fill % half
    valid = place % width < jnp.take(lengths, group)
    return (group, valid)


def lowered(v):
    return lax.optimization_barrier(v.astype(jnp.bfloat16)).astype(jnp.float32)


def gelu_exact(v):
    return jax.nn.gelu(v, approximate=False)


def widen(rows_part):
    return lax.all_gather(rows_part, "tensor", axis=2, tiled=True)


def narrow(partial_rows):
    return lax.psum_scatter(
        partial_rows.astype(jnp.bfloat16), "tensor", scatter_dimension=2, tiled=True
    ).astype(jnp.float32)


def project(rows, weight):
    return jnp.dot(rows, weight, preferred_element_type=jnp.float32)


def back_project(grad, weight):
    return jnp.einsum("ntk,ck->ntc", grad, weight, preferred_element_type=jnp.float32)


def weight_grad(rows, grad):
    return jnp.einsum("...c,...k->ck", rows, grad, preferred_element_type=jnp.float32)


def norm_forward(resid, gain, shift, width):
    mean = lax.psum(jnp.sum(resid, axis=-1), "tensor") / width
    centred = resid - mean[..., None]
    var = lax.psum(jnp.sum(centred * centred, axis=-1), "tensor") / width
    scale_rows = lax.rsqrt(var + norm_eps)[..., None]
    normed = centred * scale_rows
    return (normed * gain + shift, normed, scale_rows)


def norm_backward(grad_out, normed, scale_rows, gain, width):
    scaled = grad_out * gain
    plain_sum, cross_sum = lax.psum(
        (jnp.sum(scaled, axis=-1), jnp.sum(scaled * normed, axis=-1)), "tensor"
    )
    grad_in = scale_rows * (
        scaled - plain_sum[..., None] / width - normed * (cross_sum[..., None] / width)
    )
    return (grad_in, jnp.sum(grad_out * normed, axis=(0, 1)), jnp.sum(grad_out, axis=(0, 1)))


def self_scores(query, key, bias, own_bias, allowed_main, allowed_ahead, factor):
    raw = jnp.einsum("nthd,shd->nhts", query, key[0], preferred_element_type=jnp.float32)
    score = raw * factor + bias
    own = (
        jnp.einsum("nthd,nthd->nht", query[1:], key[1:], preferred_element_type=jnp.float32)
        * factor
        + own_bias
    )
    main = jnp.where(allowed_main, score[0], neg_big)
    ahead = jnp.where(allowed_ahead, score[1:], neg_big)
    return (main, ahead, own)


def self_forward(query, key, value, bias, own_bias, allowed_main, allowed_ahead, factor):
    main, ahead, own = self_scores(query, key, bias, own_bias, allowed_main, allowed_ahead, factor)
    top_main = jnp.max(main, axis=-1)
    weight_main = jnp.exp(main - top_main[..., None])
    total_main = jnp.sum(weight_main, axis=-1)
    top = jnp.maximum(jnp.max(ahead, axis=-1), own)
    weight = jnp.exp(ahead - top[..., None])
    weight_own = jnp.exp(own - top)
    total = jnp.sum(weight, axis=-1) + weight_own
    probs = jnp.concatenate(
        [(weight_main / total_main[..., None])[None], weight / total[..., None]], axis=0
    ).astype(jnp.bfloat16)
    mixed = jnp.einsum("nhts,shd->nthd", probs, value[0], preferred_element_type=jnp.float32)
    own_part = jnp.transpose(lowered(weight_own / total), (0, 2, 1))[..., None] * value[1:].astype(
        jnp.float32
    )
    att = jnp.concatenate([mixed[:1], mixed[1:] + own_part], axis=0).astype(jnp.bfloat16)
    lse = jnp.concatenate([(top_main + jnp.log(total_main))[None], top + jnp.log(total)], axis=0)
    return (att, lse)


def self_backward(
    query,
    key,
    value,
    grad_att,
    lse,
    bias,
    own_bias,
    allowed_main,
    allowed_ahead,
    factor,
    onehot,
    own_pick,
):
    main, ahead, own = self_scores(query, key, bias, own_bias, allowed_main, allowed_ahead, factor)
    prob = jnp.exp(jnp.concatenate([main[None], ahead], axis=0) - lse[..., None])
    prob_own = jnp.exp(own - lse[1:])
    grad_prob = jnp.einsum("nthd,shd->nhts", grad_att, value[0], preferred_element_type=jnp.float32)
    grad_own_prob = jnp.einsum(
        "nthd,nthd->nht", grad_att[1:], value[1:], preferred_element_type=jnp.float32
    )
    delta = jnp.sum(prob * grad_prob, axis=-1)
    delta = jnp.concatenate([delta[:1], delta[1:] + prob_own * grad_own_prob], axis=0)
    grad_score = prob * (grad_prob - delta[..., None])
    grad_own = prob_own * (grad_own_prob - delta[1:])
    own_low = jnp.transpose(lowered(prob_own), (0, 2, 1))[..., None]
    value_main = jnp.einsum(
        "nhts,nthd->shd", prob.astype(jnp.bfloat16), grad_att, preferred_element_type=jnp.float32
    )
    grad_value = jnp.concatenate(
        [value_main[None], own_low * grad_att[1:].astype(jnp.float32)], axis=0
    )
    score_low = (grad_score * factor).astype(jnp.bfloat16)
    own_score = jnp.transpose(lowered(grad_own * factor), (0, 2, 1))[..., None]
    grad_query = jnp.einsum("nhts,shd->nthd", score_low, key[0], preferred_element_type=jnp.float32)
    grad_query = jnp.concatenate(
        [grad_query[:1], grad_query[1:] + own_score * key[1:].astype(jnp.float32)], axis=0
    )
    key_main = jnp.einsum("nhts,nthd->shd", score_low, query, preferred_element_type=jnp.float32)
    grad_key = jnp.concatenate([key_main[None], own_score * query[1:].astype(jnp.float32)], axis=0)
    grad_rel = jnp.einsum("nhts,tsb->nthb", grad_score, onehot, precision=best)
    own_rel = jnp.transpose(grad_own, (0, 2, 1))[..., None] * own_pick
    grad_rel = jnp.concatenate([grad_rel[:1], grad_rel[1:] + own_rel], axis=0)
    return (grad_query, grad_key, grad_value, grad_rel)


def cross_scores(query, ckey, allowed, factor):
    raw = jnp.einsum("nthd,ehd->nhte", query, ckey, preferred_element_type=jnp.float32) * factor
    return jnp.where(allowed, raw, neg_big)


def cross_forward(query, ckey, cvalue, allowed, factor):
    score = cross_scores(query, ckey, allowed, factor)
    top = jnp.max(score, axis=-1)
    weight = jnp.exp(score - top[..., None])
    total = jnp.sum(weight, axis=-1)
    probs = (weight / total[..., None]).astype(jnp.bfloat16)
    mixed = jnp.einsum("nhte,ehd->nthd", probs, cvalue, preferred_element_type=jnp.float32).astype(
        jnp.bfloat16
    )
    return (mixed, top + jnp.log(total))


def cross_backward(query, ckey, cvalue, grad_mixed, lse, allowed, factor):
    prob = jnp.exp(cross_scores(query, ckey, allowed, factor) - lse[..., None])
    grad_prob = jnp.einsum("nthd,ehd->nhte", grad_mixed, cvalue, preferred_element_type=jnp.float32)
    grad_value = jnp.einsum(
        "nhte,nthd->ehd", prob.astype(jnp.bfloat16), grad_mixed, preferred_element_type=jnp.float32
    )
    grad_score = prob * (grad_prob - jnp.sum(prob * grad_prob, axis=-1, keepdims=True))
    score_low = (grad_score * factor).astype(jnp.bfloat16)
    grad_query = jnp.einsum("nhte,ehd->nthd", score_low, ckey, preferred_element_type=jnp.float32)
    grad_key = jnp.einsum("nhte,nthd->ehd", score_low, query, preferred_element_type=jnp.float32)
    return (grad_query, grad_key, grad_value)


def per_device(
    layer_in,
    encoder_states,
    w_self,
    w_rel,
    w_cross,
    w_attn_out,
    w_in,
    w_out,
    proj_bias,
    rel_bias,
    ffn_in_bias,
    out_bias,
    norm_gain,
    norm_bias,
    rel_buckets,
    slot_log,
    tgt_fill,
    enc_fill,
    out_grad,
):
    slabs = slot_log.shape[0]
    span = layer_in.shape[1] // slabs
    espan = encoder_states.shape[0] // slabs
    width = w_self.shape[1]
    heads_here = w_self.shape[2] // HEAD_DIM
    buckets = w_rel.shape[1] // heads_here
    factor = HEAD_DIM ** (-0.5)
    spots = jnp.arange(span, dtype=jnp.int32)
    codes = jnp.arange(buckets, dtype=jnp.int32)
    lap = 2 * span
    turned = jnp.concatenate(
        [rel_buckets[:1], jnp.broadcast_to(rel_buckets[:1], (span,)), rel_buckets[:0:-1]]
    )
    table = jnp.tile(turned, span)[: span * (lap - 1)].reshape(span, lap - 1)[:, :span]
    onehot = (table[..., None] == codes).astype(jnp.float32)
    own_pick = (codes == rel_buckets[0]).astype(jnp.float32)

    def slab_heads(v):
        return jnp.moveaxis(v.reshape(v.shape[0], slabs, span, heads_here, -1), 1, 0)

    def slab_rows(v):
        return jnp.moveaxis(v, 0, 1).reshape(v.shape[1], slabs * span, -1)

    def enc_heads(v):
        return v.reshape(slabs, espan, heads_here, -1)

    def enc_rows(v):
        return v.reshape(slabs * espan, -1)

    def self_masks(code, fill):
        group, valid = layout(code, fill, span)
        allowed = (group[:, None] == group[None, :]) & valid[None, :]
        return (
            allowed & (spots[:, None] >= spots[None, :]),
            allowed & (spots[:, None] > spots[None, :]),
        )

    def cross_mask(code, fill):
        group = grouping(code, span)[1]
        egroup, evalid = layout(code, fill, espan)
        return (group[:, None] == egroup[None, :]) & evalid[None, :]

    def rel_terms(rel):
        bias = jnp.einsum("nthb,tsb->nhts", rel, onehot, precision=best)
        own_bias = jnp.einsum("nthb,b->nht", rel[1:], own_pick, precision=best)
        return (bias, own_bias)

    def self_forward_slab(args):
        query, key, value, rel, code, fill = args
        allowed_main, allowed_ahead = self_masks(code, fill)
        bias, own_bias = rel_terms(rel)
        return self_forward(query, key, value, bias, own_bias, allowed_main, allowed_ahead, factor)

    def self_backward_slab(args):
        query, key, value, rel, grad_att, lse, code, fill = args
        allowed_main, allowed_ahead = self_masks(code, fill)
        bias, own_bias = rel_terms(rel)
        return self_backward(
            query,
            key,
            value,
            grad_att,
            lse,
            bias,
            own_bias,
            allowed_main,
            allowed_ahead,
            factor,
            onehot,
            own_pick,
        )

    def cross_forward_slab(args):
        query, ckey, cvalue, code, fill = args
        return cross_forward(query, ckey, cvalue, cross_mask(code, fill), factor)

    def cross_backward_slab(args):
        query, ckey, cvalue, grad_mixed, lse, code, fill = args
        return cross_backward(query, ckey, cvalue, grad_mixed, lse, cross_mask(code, fill), factor)

    full_input = widen(layer_in)

    def add_norm(prev, partial_rows, index):
        resid = prev + narrow(partial_rows) + out_bias[index]
        out, normed, scale_rows = norm_forward(resid, norm_gain[index], norm_bias[index], width)
        return (out, normed, scale_rows, widen(out.astype(jnp.bfloat16)), out)

    query = (project(full_input, w_self[0]) + proj_bias[0]).astype(jnp.bfloat16)
    key = project(full_input, w_self[1]).astype(jnp.bfloat16)
    value = (project(full_input, w_self[2]) + proj_bias[1]).astype(jnp.bfloat16)
    rel = project(full_input, w_rel) + rel_bias
    att_heads, self_lse = lax.map(
        self_forward_slab,
        (
            slab_heads(query),
            slab_heads(key),
            slab_heads(value),
            slab_heads(rel),
            slot_log,
            tgt_fill,
        ),
    )
    att = slab_rows(att_heads)
    first, first_normed, first_scale, first_full, first_all = add_norm(
        layer_in.astype(jnp.float32), project(att, w_attn_out[0]), 0
    )
    full_encoder = lax.all_gather(encoder_states, "tensor", axis=1, tiled=True)
    cquery = (project(first_full, w_cross[0]) + proj_bias[2]).astype(jnp.bfloat16)
    ckey = project(full_encoder, w_cross[1]).astype(jnp.bfloat16)
    cvalue = (project(full_encoder, w_cross[2]) + proj_bias[3]).astype(jnp.bfloat16)
    catt_heads, cross_lse = lax.map(
        cross_forward_slab,
        (slab_heads(cquery), enc_heads(ckey), enc_heads(cvalue), slot_log, enc_fill),
    )
    catt = slab_rows(catt_heads)
    second, second_normed, second_scale, second_full, second_all = add_norm(
        first, project(catt, w_attn_out[1]), 1
    )
    pre = project(second_full, w_in) + ffn_in_bias
    act = gelu_exact(pre).astype(jnp.bfloat16)
    third, third_normed, third_scale, third_full, third_all = add_norm(
        second, project(act, w_out), 2
    )
    result = third.astype(jnp.bfloat16)
    grad_third, gain_three, shift_three = norm_backward(
        out_grad.astype(jnp.float32), third_normed, third_scale, norm_gain[2], width
    )
    ffn_full = widen(grad_third.astype(jnp.bfloat16))
    grad_w_out = weight_grad(act, ffn_full)
    grad_act = back_project(ffn_full, w_out)
    grad_pre = jax.vjp(gelu_exact, pre)[1](grad_act)[0]
    pre_low = grad_pre.astype(jnp.bfloat16)
    grad_w_in = weight_grad(second_full, pre_low)
    ffn_bias_grad = jnp.sum(grad_pre, axis=(0, 1))
    bias_two = jnp.sum(grad_third, axis=(0, 1))
    grad_second_out = grad_third + narrow(back_project(pre_low, w_in))
    grad_second, gain_two, shift_two = norm_backward(
        grad_second_out, second_normed, second_scale, norm_gain[1], width
    )
    cross_full = widen(grad_second.astype(jnp.bfloat16))
    grad_out_one = weight_grad(catt, cross_full)
    grad_catt = back_project(cross_full, w_attn_out[1]).astype(jnp.bfloat16)
    bias_one = jnp.sum(grad_second, axis=(0, 1))
    cquery_heads, ckey_heads, cvalue_heads = lax.map(
        cross_backward_slab,
        (
            slab_heads(cquery),
            enc_heads(ckey),
            enc_heads(cvalue),
            slab_heads(grad_catt),
            cross_lse,
            slot_log,
            enc_fill,
        ),
    )
    grad_cquery = slab_rows(cquery_heads)
    grad_ckey = enc_rows(ckey_heads)
    grad_cvalue = enc_rows(cvalue_heads)
    cquery_low = grad_cquery.astype(jnp.bfloat16)
    ckey_low = grad_ckey.astype(jnp.bfloat16)
    cvalue_low = grad_cvalue.astype(jnp.bfloat16)
    grad_w_cross = jnp.stack(
        [
            weight_grad(first_full, cquery_low),
            weight_grad(full_encoder, ckey_low),
            weight_grad(full_encoder, cvalue_low),
        ]
    )
    encoder_terms = jnp.einsum(
        "ek,ck->ec", ckey_low, w_cross[1], preferred_element_type=jnp.float32
    ) + jnp.einsum("ek,ck->ec", cvalue_low, w_cross[2], preferred_element_type=jnp.float32)
    grad_encoder = lax.psum_scatter(
        encoder_terms.astype(jnp.bfloat16), "tensor", scatter_dimension=1, tiled=True
    ).astype(jnp.float32)
    grad_first_out = grad_second + narrow(back_project(cquery_low, w_cross[0]))
    grad_first, gain_one, shift_one = norm_backward(
        grad_first_out, first_normed, first_scale, norm_gain[0], width
    )
    self_full = widen(grad_first.astype(jnp.bfloat16))
    grad_out_zero = weight_grad(att, self_full)
    grad_att = back_project(self_full, w_attn_out[0]).astype(jnp.bfloat16)
    bias_zero = jnp.sum(grad_first, axis=(0, 1))
    query_heads, key_heads, value_heads, rel_heads = lax.map(
        self_backward_slab,
        (
            slab_heads(query),
            slab_heads(key),
            slab_heads(value),
            slab_heads(rel),
            slab_heads(grad_att),
            self_lse,
            slot_log,
            tgt_fill,
        ),
    )
    grad_query = slab_rows(query_heads)
    grad_key = slab_rows(key_heads)
    grad_value = slab_rows(value_heads)
    grad_rel = slab_rows(rel_heads)
    query_low = grad_query.astype(jnp.bfloat16)
    key_low = grad_key.astype(jnp.bfloat16)
    value_low = grad_value.astype(jnp.bfloat16)
    rel_low = grad_rel.astype(jnp.bfloat16)
    grad_w_self = jnp.stack(
        [
            weight_grad(full_input, query_low),
            weight_grad(full_input, key_low),
            weight_grad(full_input, value_low),
        ]
    )
    grad_w_rel = weight_grad(full_input, rel_low)
    input_terms = (
        back_project(query_low, w_self[0])
        + back_project(key_low, w_self[1])
        + back_project(value_low, w_self[2])
        + back_project(rel_low, w_rel)
    )
    grad_input = grad_first + narrow(input_terms)
    grad_w_attn = jnp.stack([grad_out_zero, grad_out_one])
    proj_bias_grad = jnp.stack(
        [
            jnp.sum(grad_query, axis=(0, 1)),
            jnp.sum(grad_value, axis=(0, 1)),
            jnp.sum(grad_cquery, axis=(0, 1)),
            jnp.sum(grad_cvalue, axis=0),
        ]
    )
    rel_bias_grad = jnp.sum(grad_rel, axis=(0, 1))
    out_bias_grad = jnp.stack([bias_zero, bias_one, bias_two])
    gain_grad = jnp.stack([gain_one, gain_two, gain_three])
    shift_grad = jnp.stack([shift_one, shift_two, shift_three])
    def shared(part, axis, **how):
        return lax.psum_scatter(part.astype(jnp.bfloat16), axis, **how).astype(jnp.float32)

    sent = (
        shared(grad_w_self, "batch", scatter_dimension=1, tiled=True),
        shared(grad_w_rel, "batch", scatter_dimension=0, tiled=True),
        shared(grad_w_cross, "batch", scatter_dimension=1, tiled=True),
        shared(grad_w_attn, "batch", scatter_dimension=2, tiled=True),
        shared(grad_w_in, "batch", scatter_dimension=0, tiled=True),
        shared(grad_w_out, "batch", scatter_dimension=1, tiled=True),
        lax.psum_scatter(proj_bias_grad, "batch", scatter_dimension=1, tiled=True),
        lax.psum_scatter(rel_bias_grad, "batch", scatter_dimension=0, tiled=True),
        lax.psum_scatter(ffn_bias_grad, "batch", scatter_dimension=0, tiled=True),
        lax.psum_scatter(out_bias_grad, "batch", scatter_dimension=1, tiled=True),
        lax.psum_scatter(gain_grad, "batch", scatter_dimension=1, tiled=True),
        lax.psum_scatter(shift_grad, "batch", scatter_dimension=1, tiled=True),
    )
    return (result, grad_input, grad_encoder) + tuple(sent)


def solution(mesh):
    return jax.shard_map(
        per_device,
        mesh=mesh,
        in_specs=(
            P(None, "batch", "tensor"),
            P("batch", "tensor"),
            P(None, None, "tensor"),
            P(None, "tensor"),
            P(None, None, "tensor"),
            P(None, "tensor", None),
            P(None, "tensor"),
            P("tensor", None),
            P(None, "tensor"),
            P("tensor"),
            P("tensor"),
            P(None, "tensor"),
            P(None, "tensor"),
            P(None, "tensor"),
            P(),
            P("batch"),
            P("batch", None),
            P("batch", None),
            P(None, "batch", "tensor"),
        ),
        out_specs=(
            P(None, "batch", "tensor"),
            P(None, "batch", "tensor"),
            P("batch", "tensor"),
            P(None, "batch", "tensor"),
            P("batch", "tensor"),
            P(None, "batch", "tensor"),
            P(None, "tensor", "batch"),
            P("batch", "tensor"),
            P("tensor", "batch"),
            P(None, ("tensor", "batch")),
            P(("tensor", "batch")),
            P(("tensor", "batch")),
            P(None, ("tensor", "batch")),
            P(None, ("tensor", "batch")),
            P(None, ("tensor", "batch")),
        ),
        check_vma=False,
    )
```

```python
import functools

import jax
import jax.numpy as jnp
from jax import lax
from jax.experimental import pallas as pl
from jax.experimental.pallas import tpu as pltpu
from jax.sharding import PartitionSpec as P

HEAD_DIM = 64
norm_eps = 1e-05
neg_big = -1e30
MESH = pl.DeviceIdType.MESH
f32 = jnp.float32
bf16 = jnp.bfloat16
TILE = 128


def dot(a, b):
    return jnp.dot(a, b, preferred_element_type=f32)


def dot_nt(a, b):
    return lax.dot_general(a, b, (((1,), (1,)), ((), ())), preferred_element_type=f32)


def dot_tn(a, b):
    return lax.dot_general(a, b, (((0,), (0,)), ((), ())), preferred_element_type=f32)


def total(v):
    return jnp.sum(v, axis=1, keepdims=True)


def eight(v):
    return jnp.sum(v.reshape(v.shape[0] // 8, 8, v.shape[1]), axis=0)


def gelu_both(v):
    half = 0.5 * (1.0 + lax.erf(v * (0.5**0.5)))
    bell = jnp.exp(-0.5 * v * v) * 0.3989422804014327
    return v * half, half + v * bell


def layer_kernel(
    dims,
    x_in,
    e_in,
    og_in,
    par_in,
    ws_in,
    wr_in,
    wc_in,
    wa_in,
    wi_in,
    wo_in,
    pbias,
    rbias,
    fbias,
    smask,
    cmask,
    oh,
    oht,
    out_ref,
    gin_ref,
    genc_ref,
    vec_ref,
    gs_ref,
    gr_ref,
    gc_ref,
    ga0_ref,
    ga1_ref,
    gi_ref,
    go_ref,
    par,
    xf,
    ef,
    df,
    f1,
    f2,
    act,
    gp,
    qb,
    kb,
    vb,
    relb,
    att,
    catt,
    cq,
    ck,
    cv,
    lse,
    ws,
    wr,
    wc,
    wa,
    wi,
    wo,
    pbuf,
    crecv,
    yrecv,
    ga0,
    ga1,
    ecrecv,
    eyrecv,
    kacc,
    vacc,
    tile4,
    nacc,
    pacc,
    racc,
    facc,
    vec,
    vrecv,
    vquarter,
    xs,
    xr,
    xc,
    xa0,
    xa1,
    xi,
    xo,
    zs,
    zr,
    zc,
    za0,
    za1,
    zi,
    zo,
    lsem,
    ssem,
    rsem,
    csem,
    dsem,
    bsem,
):
    lanes, span, espan, cols, width, hidden, heads, buckets, parts = dims
    tiles = span // TILE
    tensor = lax.axis_index("tensor")
    yy = tensor // 2
    cc = lax.rem(tensor, 2)
    y_peer = {"tensor": (1 - yy) * 2 + cc}
    c_peer = {"tensor": yy * 2 + (1 - cc)}
    mine = tensor
    y_other = (1 - yy) * 2 + cc
    c_other = yy * 2 + (1 - cc)
    both_other = (1 - yy) * 2 + (1 - cc)

    batch = lax.axis_index("batch")
    ring = parts // 2
    at_ring = batch // 2
    at_pair = lax.rem(batch, 2)
    x_peer = {"batch": at_ring * 2 + (1 - at_pair)}

    def z_peer(step):
        return {"batch": lax.rem(at_ring + step, ring) * 2 + at_pair}

    barrier = pltpu.get_barrier_semaphore()
    for peer in (y_peer, c_peer, x_peer):
        pl.semaphore_signal(barrier, inc=1, device_id=peer, device_id_type=MESH)

    @pl.loop(1, ring)
    def _(step):
        pl.semaphore_signal(barrier, inc=1, device_id=z_peer(step), device_id_type=MESH)

    counts = {"local": 0, "y": 0, "c": 0}

    def local(src, dst):
        at = counts["local"]
        counts["local"] += 1
        copy = pltpu.make_async_copy(src, dst, lsem.at[at])
        copy.start()
        return copy

    def send_y(src, dst):
        at = counts["y"]
        counts["y"] += 1
        copy = pltpu.make_async_remote_copy(
            src_ref=src,
            dst_ref=dst,
            send_sem=ssem.at[at],
            recv_sem=rsem.at[at],
            device_id=y_peer,
            device_id_type=MESH,
        )
        copy.start()
        return copy

    def send_c(src, dst):
        at = counts["c"]
        counts["c"] += 1
        copy = pltpu.make_async_remote_copy(
            src_ref=src,
            dst_ref=dst,
            send_sem=csem.at[at],
            recv_sem=dsem.at[at],
            device_id=c_peer,
            device_id_type=MESH,
        )
        copy.start()
        return copy

    x_copies = [local(x_in.at[n], xf.at[n, mine]) for n in range(lanes)]
    ws_copy = local(ws_in, ws)
    wr_copy = local(wr_in, wr.at[0])
    wa_copy = local(wa_in, wa)
    e_copy = local(e_in, ef.at[0, mine])
    wc_copy = local(wc_in, wc)
    og_copies = [local(og_in.at[n], df.at[n, mine]) for n in range(lanes)]
    wi_copy = local(wi_in, wi.at[0])
    wo_copy = local(wo_in, wo.at[0])
    par[mine] = par_in[...]
    pl.semaphore_wait(barrier, 2 + ring)

    class Gather:
        def __init__(self, ref, at=None):
            def block(q):
                return ref.at[q] if at is None else ref.at[at, q]

            self.block = block
            self.by_y = send_y(block(mine), block(mine))
            self.by_c = send_c(block(mine), block(mine))

        def finish(self):
            self.by_y.wait_recv()
            self.on = send_c(self.block(y_other), self.block(y_other))
            self.by_c.wait_recv()
            self.on.wait_recv()

        def done(self):
            self.by_y.wait_send()
            self.by_c.wait_send()
            self.on.wait_send()

    x_gather = []
    for n in range(lanes):
        x_copies[n].wait()
        x_gather.append(Gather(xf, n))
        if n == 0:
            par_gather = Gather(par)

    for ref in (nacc, pacc, racc, facc, kacc, vacc):
        ref[...] = jnp.zeros(ref.shape, ref.dtype)

    lane_c = lax.broadcasted_iota(jnp.int32, (1, cols), 1)
    head_f = [(lane_c // HEAD_DIM == h).astype(f32) for h in range(heads)]
    head_b = [m.astype(bf16) for m in head_f]
    lane_w = lax.broadcasted_iota(jnp.int32, (1, 2 * heads * buckets), 1)
    word_b = [
        (lax.rem(lane_w, heads * buckets) // buckets == h).astype(f32).astype(bf16)
        for h in range(heads)
    ]
    lane_r = lax.broadcasted_iota(jnp.int32, (1, heads * buckets), 1)
    word_f = [(lane_r // buckets == h).astype(f32) for h in range(heads)]
    flip = (
        lax.broadcasted_iota(jnp.int32, (TILE, TILE), 0)
        + lax.broadcasted_iota(jnp.int32, (TILE, TILE), 1)
        == TILE - 1
    )
    flip = flip.astype(f32).astype(bf16)
    slot = lax.broadcasted_iota(jnp.int32, (TILE, 128), 1)

    def rows_of(i):
        return pl.ds(pl.multiple_of(i * TILE, TILE), TILE)

    def col_of(j):
        return pl.ds(pl.multiple_of(j * cols, cols), cols)

    def wide(ref, n, rows):
        return jnp.concatenate([ref[n, q, rows, :] for q in range(4)], axis=1)

    def summed(n, rows):
        places = [jnp.where(cc == q % 2, q, 4 + q // 2) for q in range(4)]
        return jnp.concatenate([pbuf[n, p, rows, :] for p in places], axis=1)

    def put_wide(ref, n, rows, v):
        for q in range(4):
            ref[n, q, rows, :] = v[:, q * cols : (q + 1) * cols].astype(ref.dtype)

    def param(k):
        return jnp.concatenate([par[q, k : k + 1, :] for q in range(4)], axis=1)

    def put_slot(ref, rows, k, v):
        ref[rows, :] = jnp.where(slot == k, v, ref[rows, :])

    class Reduce:
        def __init__(self, n, parity):
            self.n = n
            self.parity = parity
            self.first = [
                send_c(pbuf.at[n, 2 * k + 1 - cc], crecv.at[n, k]) for k in range(2)
            ]
            for copy in self.first:
                copy.wait_recv()
            for k in range(2):

                @pl.loop(0, tiles)
                def _(i, k=k):
                    rows = rows_of(i)
                    both = pbuf[n, 2 * k + cc, rows, :].astype(f32) + crecv[n, k, rows, :].astype(
                        f32
                    )
                    pbuf[n, 2 * k + cc, rows, :] = both.astype(bf16)

            self.second = [
                send_y(pbuf.at[n, 2 * k + cc], yrecv.at[parity, n, k]) for k in range(2)
            ]

        def finish(self):
            n = self.n
            for copy in self.first:
                copy.wait_send()
            for copy in self.second:
                copy.wait()
            for k in range(2):

                @pl.loop(0, tiles)
                def _(i, k=k):
                    rows = rows_of(i)
                    both = pbuf[n, 2 * k + cc, rows, :].astype(f32) + yrecv[
                        self.parity, n, k, rows, :
                    ].astype(f32)
                    pbuf[n, 2 * k + cc, rows, :] = both.astype(bf16)

            self.third = [send_c(pbuf.at[n, 2 * k + cc], pbuf.at[n, 4 + k]) for k in range(2)]
            for copy in self.third:
                copy.wait()

    class Scatter:
        def __init__(self, part, from_c, from_y):
            self.part = part
            self.from_y = from_y
            self.first = [send_c(part.at[2 * k + 1 - cc], from_c.at[k]) for k in range(2)]
            for copy in self.first:
                copy.wait_recv()
            for k in range(2):

                @pl.loop(0, tiles)
                def _(i, k=k):
                    rows = rows_of(i)
                    both = part[2 * k + cc, rows, :].astype(f32) + from_c[k, rows, :].astype(f32)
                    part[2 * k + cc, rows, :] = both.astype(bf16)

            self.second = send_y(part.at[y_other], from_y)

        def finish(self, store):
            self.second.wait_recv()

            @pl.loop(0, tiles)
            def _(i):
                rows = rows_of(i)
                store(
                    rows,
                    self.part[mine, rows, :].astype(f32) + self.from_y[rows, :].astype(f32),
                )

            for copy in self.first:
                copy.wait_send()
            self.second.wait_send()

    class Share:
        def __init__(self, grad, pair, far, out, at):
            self.grad, self.pair, self.far, self.out, self.at = grad, pair, far, out, at
            self.block = width // parts

            @pl.loop(0, ring)
            def _(z):
                self.near(self.rows(z, 1 - at_pair), pair.at[z]).start()

        def rows(self, z, x):
            start = pl.multiple_of((z * 2 + x) * self.block, self.block)
            return self.grad.at[:, pl.ds(start, self.block), :]

        def near(self, src, dst):
            return pltpu.make_async_remote_copy(
                src_ref=src,
                dst_ref=dst,
                send_sem=bsem.at[self.at, 0],
                recv_sem=bsem.at[self.at, 1],
                device_id=x_peer,
                device_id_type=MESH,
            )

        def away(self, src, dst, step):
            return pltpu.make_async_remote_copy(
                src_ref=src,
                dst_ref=dst,
                send_sem=bsem.at[self.at, 2],
                recv_sem=bsem.at[self.at, 3],
                device_id=z_peer(step),
                device_id_type=MESH,
            )

        def middle(self):
            self.near(self.pair, self.pair).wait()

            @pl.loop(0, ring)
            def _(z):
                for m in range(self.grad.shape[0]):
                    start = pl.multiple_of((z * 2 + at_pair) * self.block, self.block)
                    own = self.grad[m, pl.ds(start, self.block), :].astype(f32)
                    self.pair[z, m] = (own + self.pair[z, m].astype(f32)).astype(bf16)

            @pl.loop(1, ring)
            def _(step):
                self.away(
                    self.pair.at[lax.rem(at_ring + step, ring)], self.far.at[step - 1], step
                ).start()

        def last(self):
            self.away(self.far, self.far, 1).wait()
            self.out[...] = self.pair[at_ring].astype(f32)

            @pl.loop(1, ring)
            def _(step):
                self.out[...] += self.far[step - 1].astype(f32)

    def norm_rows(resid):
        mean = total(resid) * (1.0 / width)
        centred = resid - mean
        var = total(centred * centred) * (1.0 / width)
        rs = lax.rsqrt(var + norm_eps)
        return centred * rs, rs

    def norm_grad(grad, xh, rs, gain, k):
        q = grad * gain
        m1 = total(q) * (1.0 / width)
        m2 = total(q * xh) * (1.0 / width)
        back = rs * (q - m1 - xh * m2)
        nacc[k] += eight(grad * xh)
        nacc[3 + k] += eight(grad)
        nacc[6 + k] += eight(back)
        return back

    def self_score(n, i, h, q, rel_rows, key0, diag):
        rows = rows_of(i)
        qh = q * head_b[h]
        spread = dot(rel_rows * word_b[h], oh[i])
        bias = pltpu.roll(spread, 0, 1, stride=1, stride_axis=0)
        s = dot_nt(qh, key0) + smask[rows, :].astype(f32)
        if n > 0:
            s = jnp.where(diag, total(qh.astype(f32) * kb[n, rows, :].astype(f32)), s)
        return qh, s + bias

    def diagonal(i):
        r = lax.broadcasted_iota(jnp.int32, (TILE, span), 0)
        s = lax.broadcasted_iota(jnp.int32, (TILE, span), 1)
        return s == r + i * TILE

    def self_forward(n):
        @pl.loop(0, tiles)
        def _(i):
            rows = rows_of(i)
            x = wide(xf, n, rows)
            qb[n, rows, :] = ((dot(x, ws[0]) + pbias[0:1, :]).astype(bf16).astype(f32) * 0.125).astype(bf16)
            kb[n, rows, :] = dot(x, ws[1]).astype(bf16)
            vb[n, rows, :] = (dot(x, ws[2]) + pbias[1:2, :]).astype(bf16)
            rel = dot(x, wr[0]) + rbias[...]
            high = rel.astype(bf16)
            relb[n, rows, : heads * buckets] = high
            relb[n, rows, heads * buckets :] = (rel - high.astype(f32)).astype(bf16)

        @pl.loop(0, tiles)
        def _(i):
            rows = rows_of(i)
            diag = diagonal(i) if n > 0 else None
            q = qb[n, rows, :]
            rel_rows = relb[n, rows, :]
            mixed = jnp.zeros((TILE, cols), f32)
            for h in range(heads):
                qh, s = self_score(n, i, h, q, rel_rows, kb[0], diag)
                top = jnp.max(s, axis=1, keepdims=True)
                w = jnp.exp(s - top)
                sums = total(w)
                prob = w * (1.0 / sums)
                if n > 0:
                    own = total(jnp.where(diag, prob, 0.0)).astype(bf16).astype(f32)
                    prob = jnp.where(diag, 0.0, prob)
                part = dot(prob.astype(bf16), vb[0])
                if n > 0:
                    part = part + own * vb[n, rows, :].astype(f32)
                mixed = mixed + part * head_f[h]
                put_slot(lse, rows, n * heads + h, top + jnp.log(sums))
            low = mixed.astype(bf16)
            att[n, rows, :] = low
            put_wide(pbuf, n, rows, dot(low, wa[0]))

    def encoder_rows():
        @pl.loop(0, espan // TILE)
        def _(i):
            rows = rows_of(i)
            e = wide(ef, 0, rows)
            ck[rows, :] = dot(e, wc[1]).astype(bf16)
            cv[rows, :] = (dot(e, wc[2]) + pbias[3:4, :]).astype(bf16)

    def cross_forward(n):
        @pl.loop(0, tiles)
        def _(i):
            rows = rows_of(i)
            resid = wide(xf, n, rows).astype(f32) + summed(n, rows).astype(f32) + param(0)
            xh, rs = norm_rows(resid)
            put_slot(lse, rows, 2 * lanes * heads + n, rs)
            first = (xh * param(3) + param(6)).astype(bf16)
            put_wide(f1, n, rows, first)
            q = ((dot(first, wc[0]) + pbias[2:3, :]).astype(bf16).astype(f32) * 0.125).astype(bf16)
            cq[n, rows, :] = q
            mixed = jnp.zeros((TILE, cols), f32)
            for h in range(heads):
                s = dot_nt(q * head_b[h], ck[...]) + cmask[rows, :].astype(f32)
                top = jnp.max(s, axis=1, keepdims=True)
                w = jnp.exp(s - top)
                sums = total(w)
                mixed = mixed + dot((w * (1.0 / sums)).astype(bf16), cv[...]) * head_f[h]
                put_slot(lse, rows, (lanes + n) * heads + h, top + jnp.log(sums))
            low = mixed.astype(bf16)
            catt[n, rows, :] = low
            put_wide(pbuf, n, rows, dot(low, wa[1]))

    def ffn_forward(n):
        @pl.loop(0, tiles)
        def _(i):
            rows = rows_of(i)
            resid = wide(f1, n, rows).astype(f32) + summed(n, rows).astype(f32) + param(1)
            xh, rs = norm_rows(resid)
            put_slot(lse, rows, 2 * lanes * heads + lanes + n, rs)
            put_wide(f2, n, rows, xh * param(4) + param(7))

        every = pl.ds(0, span)

        @pl.loop(0, hidden // cols)
        def _(j):
            at = col_of(j)
            pre = dot(wide(f2, n, every), wi[0, :, at]) + fbias[:, at]
            value, slope = gelu_both(pre)
            act[n, :, at] = value.astype(bf16)
            gp[n, :, at] = slope.astype(bf16)

        @pl.loop(0, width // cols)
        def _(j):
            pbuf[n, j] = dot(act[n], wo[0, :, col_of(j)]).astype(bf16)

    def ffn_backward(n):
        @pl.loop(0, tiles)
        def _(i):
            rows = rows_of(i)
            resid = wide(f2, n, rows).astype(f32) + summed(n, rows).astype(f32) + param(2)
            xh, rs = norm_rows(resid)
            out = xh * param(5) + param(8)
            for q in range(4):
                tile4[q] = out[:, q * cols : (q + 1) * cols].astype(bf16)
            out_ref[n, rows, :] = tile4[mine]
            grad = wide(df, n, rows).astype(f32)
            put_wide(df, n, rows, norm_grad(grad, xh, rs, param(5), 2))

        every = pl.ds(0, span)

        @pl.loop(0, hidden // cols)
        def _(j):
            at = col_of(j)
            grad = dot_nt(wide(df, n, every), wo[0, at, :]) * gp[n, :, at].astype(f32)
            facc[:, at] += eight(grad)
            gp[n, :, at] = grad.astype(bf16)

        @pl.loop(0, width // cols)
        def _(j):
            pbuf[n, j] = dot_nt(gp[n], wi[0, col_of(j), :]).astype(bf16)

    def cross_backward(n):
        @pl.loop(0, tiles)
        def _(i):
            rows = rows_of(i)
            grad = wide(df, n, rows).astype(f32) + summed(n, rows).astype(f32)
            gain = param(4)
            xh = (wide(f2, n, rows).astype(f32) - param(7)) * (1.0 / gain)
            at = 2 * lanes * heads + lanes + n
            rs = lse[rows, at : at + 1]
            back = norm_grad(grad, xh, rs, gain, 1).astype(bf16)
            put_wide(df, n, rows, back)
            da = dot_nt(back, wa[1]).astype(bf16)
            q = cq[n, rows, :]
            dq = jnp.zeros((TILE, cols), f32)
            for h in range(heads):
                qh = q * head_b[h]
                dh = da * head_b[h]
                s = dot_nt(qh, ck[...]) + cmask[rows, :].astype(f32)
                at = (lanes + n) * heads + h
                p = jnp.exp(s - lse[rows, at : at + 1])
                dp = dot_nt(dh, cv[...])
                ds = (p * (dp - total(p * dp))).astype(bf16)
                vacc[...] += dot_tn(p.astype(bf16), dh)
                kacc[...] += dot_tn(ds, qh)
                dq = dq + dot(ds, ck[...]) * head_f[h]
            dq = dq * 0.125
            pacc[2] += eight(dq)
            low = dq.astype(bf16)
            cq[n, rows, :] = low
            put_wide(pbuf, n, rows, dot_nt(low, wc[0]))

    def encoder_backward():
        pacc[3] += eight(vacc[...])

        @pl.loop(0, espan // TILE)
        def _(i):
            rows = rows_of(i)
            dk = kacc[rows, :].astype(bf16)
            dv = vacc[rows, :].astype(bf16)
            ck[rows, :] = dk
            cv[rows, :] = dv
            part = dot_nt(dk, wc[1]) + dot_nt(dv, wc[2])
            for q in range(4):
                f2[0, q, rows, :] = part[:, q * cols : (q + 1) * cols].astype(bf16)

    def self_backward(n):
        @pl.loop(0, tiles)
        def _(i):
            rows = rows_of(i)
            grad = wide(df, n, rows).astype(f32) + summed(n, rows).astype(f32)
            gain = param(3)
            xh = (wide(f1, n, rows).astype(f32) - param(6)) * (1.0 / gain)
            at = 2 * lanes * heads + n
            rs = lse[rows, at : at + 1]
            back = norm_grad(grad, xh, rs, gain, 0).astype(bf16)
            put_wide(df, n, rows, back)
            da = dot_nt(back, wa[0]).astype(bf16)
            diag = diagonal(i) if n > 0 else None
            q = qb[n, rows, :]
            rel_rows = relb[n, rows, :]
            dq = jnp.zeros((TILE, cols), f32)
            drel = jnp.zeros((TILE, heads * buckets), f32)
            if n > 0:
                kn = kb[n, rows, :].astype(f32)
                vn = vb[n, rows, :].astype(f32)
                dk = jnp.zeros((TILE, cols), f32)
                dv = jnp.zeros((TILE, cols), f32)
            for h in range(heads):
                qh, s = self_score(n, i, h, q, rel_rows, kb[0], diag)
                at = n * heads + h
                p = jnp.exp(s - lse[rows, at : at + 1])
                dh = da * head_b[h]
                dp = dot_nt(dh, vb[0])
                if n > 0:
                    dp = jnp.where(diag, total(dh.astype(f32) * vn), dp)
                ds = p * (dp - total(p * dp))
                turned = pltpu.roll(dot(flip, ds.astype(bf16)), 0, 1, stride=1, stride_axis=0)
                drel = drel + dot(turned.astype(bf16), oht[i]) * word_f[h]
                if n > 0:
                    own_p = total(jnp.where(diag, p, 0.0)).astype(bf16).astype(f32)
                    own_s = total(jnp.where(diag, ds, 0.0)).astype(bf16).astype(f32)
                    p = jnp.where(diag, 0.0, p)
                    ds = jnp.where(diag, 0.0, ds)
                    dk = dk + own_s * qh.astype(f32)
                    dv = dv + own_p * dh.astype(f32)
                low = ds.astype(bf16)
                vacc[...] += dot_tn(p.astype(bf16), dh)
                kacc[...] += dot_tn(low, qh)
                part = dot(low, kb[0])
                if n > 0:
                    part = part + own_s * kn
                dq = dq + part * head_f[h]
            dq = dq * 0.125
            pacc[0] += eight(dq)
            racc[...] += eight(drel)
            qb[n, rows, :] = dq.astype(bf16)
            relb[n, rows, : heads * buckets] = dot(flip, drel.astype(bf16)).astype(bf16)
            if n > 0:
                pacc[1] += eight(dv)
                kb[n, rows, :] = dk.astype(bf16)
                vb[n, rows, :] = dv.astype(bf16)

        if n == 0:
            pacc[1] += eight(vacc[...])
            kb[0] = kacc[...].astype(bf16)
            vb[0] = vacc[...].astype(bf16)

        @pl.loop(0, width // cols)
        def _(j):
            at = col_of(j)
            part = dot_nt(qb[n], ws[0, at, :]) + dot_nt(kb[n], ws[1, at, :])
            part = part + dot_nt(vb[n], ws[2, at, :])
            part = part + dot_nt(relb[n, :, : heads * buckets], wr[0, at, :])
            pbuf[n, j] = part.astype(bf16)

    def weight_grad(rows_ref, pieces, lane_count):
        @pl.loop(0, 4)
        def _(j):
            left = jnp.concatenate([rows_ref[n, j] for n in range(lane_count)], axis=0)
            for load, target, size in pieces:
                for start in range(0, size, cols):
                    step = min(cols, size - start)
                    right = jnp.concatenate(
                        [load(n, start, step) for n in range(lane_count)], axis=0
                    )
                    target[col_of(j), start : start + step] = dot_tn(left, right).astype(bf16)

    def of(ref):
        return lambda n, start, step: ref[n, :, start : start + step]

    words = heads * buckets

    order = list(range(lanes))
    late = order[1:] + order[:1]
    reduces = {}
    ws_copy.wait()
    wr_copy.wait()
    wa_copy.wait()
    for n in order:
        x_gather[n].finish()
        self_forward(n)
        reduces[n] = Reduce(n, 0)
        if n == 0:
            e_copy.wait()
            e_gather = Gather(ef, 0)
            par_gather.finish()
    wc_copy.wait()
    e_gather.finish()
    encoder_rows()
    og_gather = []
    for n in order:
        og_copies[n].wait()
        reduces[n].finish()
        cross_forward(n)
        og_gather.append(Gather(df, n))
        reduces[n] = Reduce(n, 1)
    wi_copy.wait()
    wo_copy.wait()
    for n in order:
        reduces[n].finish()
        ffn_forward(n)
        reduces[n] = Reduce(n, 0)
    for n in order:
        reduces[n].finish()
        og_gather[n].finish()
        og_gather[n].done()
        ffn_backward(n)
        reduces[n] = Reduce(n, 1)
    weight_grad(df, [(of(act), wo.at[0], hidden)], lanes)
    share_o = Share(wo, xo, zo, go_ref, 0)
    weight_grad(f2, [(of(gp), wi.at[0], hidden)], lanes)
    share_i = Share(wi, xi, zi, gi_ref, 1)
    for n in late:
        reduces[n].finish()
        cross_backward(n)
        reduces[n] = Reduce(n, 0)
        if n == late[1]:
            share_o.middle()
    encoder_backward()
    e_scatter = Scatter(f2.at[0], ecrecv, eyrecv)
    weight_grad(df, [(of(catt), ga1.at[0], cols)], lanes)
    share_a1 = Share(ga1, xa1, za1, ga1_ref, 2)
    weight_grad(f1, [(of(cq), wc.at[0], cols)], lanes)
    weight_grad(
        ef,
        [
            (lambda n, a, b: ck[:, a : a + b], wc.at[1], cols),
            (lambda n, a, b: cv[:, a : a + b], wc.at[2], cols),
        ],
        1,
    )
    share_c = Share(wc, xc, zc, gc_ref, 4)
    share_i.middle()
    kacc[...] = jnp.zeros(kacc.shape, f32)
    vacc[...] = jnp.zeros(vacc.shape, f32)
    scatters = {}
    for n in late:
        reduces[n].finish()
        self_backward(n)
        scatters[n] = Scatter(pbuf.at[n], crecv.at[n], yrecv.at[1, n, 0])
        if n == late[0]:

            def store_enc(rows, v):
                genc_ref[rows, :] = v

            e_scatter.finish(store_enc)
            share_o.last()
            share_a1.middle()
        if n == late[1]:
            share_i.last()
            share_c.middle()
    def vec_copy(src, dst, k, peer):
        return pltpu.make_async_remote_copy(
            src_ref=src,
            dst_ref=dst,
            send_sem=bsem.at[7, k],
            recv_sem=bsem.at[7, k + 1],
            device_id=peer,
            device_id_type=MESH,
        )

    for k in range(9):
        row = jnp.sum(nacc[k], axis=0, keepdims=True)
        for q in range(4):
            vquarter[q, k : k + 1, :] = row[:, q * cols : (q + 1) * cols]
    vec[...] = jnp.zeros(vec.shape, f32)
    vec[0:9, :] = vquarter[mine, 0:9, :]
    for k in range(4):
        vec[9 + k : 10 + k, :] = jnp.sum(pacc[k], axis=0, keepdims=True)
    vec[13:14, :words] = jnp.sum(racc[...], axis=0, keepdims=True)
    row = jnp.sum(facc[...], axis=0, keepdims=True)
    for k in range(hidden // cols):
        vec[14 + k : 15 + k, :] = row[:, k * cols : (k + 1) * cols]
    vec_pair = vec_copy(vec, vrecv.at[0], 0, x_peer)
    vec_pair.start()
    weight_grad(df, [(of(att), ga0.at[0], cols)], lanes)
    share_a0 = Share(ga0, xa0, za0, ga0_ref, 3)
    weight_grad(
        xf,
        [
            (of(qb), ws.at[0], cols),
            (of(kb), ws.at[1], cols),
            (of(vb), ws.at[2], cols),
            (of(relb), wr.at[0], words),
        ],
        lanes,
    )
    share_r = Share(wr, xr, zr, gr_ref, 5)
    share_s = Share(ws, xs, zs, gs_ref, 6)
    for n in late:

        def store_in(rows, v, n=n):
            gin_ref[n, rows, :] = df[n, mine, rows, :].astype(f32) + v

        scatters[n].finish(store_in)
    share_a1.last()
    share_c.last()
    share_a0.middle()
    share_r.middle()
    share_s.middle()
    vec_pair.wait()
    vec[...] += vrecv[0]

    @pl.loop(1, ring)
    def _(step):
        vec_copy(vec, vrecv.at[step], 2, z_peer(step)).start()

    share_a0.last()
    share_r.last()
    share_s.last()
    every_vec = vrecv.at[pl.ds(1, ring - 1)]
    vec_copy(every_vec, every_vec, 2, z_peer(1)).wait()
    vec_ref[...] = vec[...]

    @pl.loop(1, ring)
    def _(step):
        vec_ref[...] += vrecv[step]

    for item in x_gather + [par_gather, e_gather]:
        item.done()


def grouping(code, span):
    place = jnp.arange(span, dtype=jnp.int32)
    width = jnp.right_shift(jnp.int32(span), code)
    return (place, place // width, width)


def layout(code, fill, span):
    place, group, width = grouping(code, span)
    half = jnp.maximum(width // 2, 1)
    lengths = width - fill % half
    slots = jnp.arange(fill.shape[0], dtype=jnp.int32)
    own = jnp.sum(jnp.where(group[:, None] == slots, lengths, 0), axis=1)
    return (group, place % width < own)


def per_device(
    layer_in,
    encoder_states,
    w_self,
    w_rel,
    w_cross,
    w_attn_out,
    w_in,
    w_out,
    proj_bias,
    rel_bias,
    ffn_in_bias,
    out_bias,
    norm_gain,
    norm_bias,
    rel_buckets,
    slot_log,
    tgt_fill,
    enc_fill,
    out_grad,
):
    lanes, span, cols = layer_in.shape
    espan = encoder_states.shape[0]
    width = w_self.shape[1]
    hidden = w_in.shape[1]
    heads = cols // HEAD_DIM
    words = w_rel.shape[1]
    buckets = words // heads
    spots = jnp.arange(span, dtype=jnp.int32)
    group, valid = layout(slot_log[0], tgt_fill[0], span)
    allowed = (group[:, None] == group[None, :]) & valid[None, :]
    allowed = allowed & (spots[:, None] >= spots[None, :])
    smask = jnp.where(allowed, 0.0, neg_big).astype(bf16)
    egroup, evalid = layout(slot_log[0], enc_fill[0], espan)
    cmask = jnp.where((group[:, None] == egroup[None, :]) & evalid[None, :], 0.0, neg_big)
    cmask = cmask.astype(bf16)
    turned = jnp.concatenate([rel_buckets[:1], rel_buckets[:0:-1]])
    turned = jnp.stack([jnp.roll(turned, r) for r in range(0, span, TILE)])
    codes = jnp.arange(buckets, dtype=jnp.int32)
    oh = (turned[:, None, :] == jnp.tile(codes, 2 * heads)[:, None]).astype(bf16)
    turned = jnp.roll(turned, TILE - 1, axis=1)
    oht = (turned[:, :, None] == jnp.tile(codes, heads)).astype(bf16)
    par = jnp.concatenate(
        [out_bias, norm_gain, norm_bias, jnp.zeros((7, cols), f32)], axis=0
    )
    parts = lax.axis_size("batch")
    ring = parts // 2
    block = width // parts
    shapes = [(3, cols), (1, words), (3, cols), (1, cols), (1, cols), (1, hidden), (1, hidden)]
    vec_rows = -(-(14 + hidden // cols) // 8) * 8
    dims = (lanes, span, espan, cols, width, hidden, heads, buckets, parts)
    any_spec = pl.BlockSpec(memory_space=pl.ANY)
    vmem = pl.BlockSpec(memory_space=pltpu.VMEM)
    V = pltpu.VMEM
    scratch = [
        V((4, 16, cols), f32),
        V((lanes, 4, span, cols), bf16),
        V((1, 4, espan, cols), bf16),
        V((lanes, 4, span, cols), bf16),
        V((lanes, 4, span, cols), bf16),
        V((lanes, 4, span, cols), bf16),
        V((lanes, span, hidden), bf16),
        V((lanes, span, hidden), bf16),
        V((lanes, span, cols), bf16),
        V((lanes, span, cols), bf16),
        V((lanes, span, cols), bf16),
        V((lanes, span, 2 * words), bf16),
        V((lanes, span, cols), bf16),
        V((lanes, span, cols), bf16),
        V((lanes, span, cols), bf16),
        V((espan, cols), bf16),
        V((espan, cols), bf16),
        V((span, 128), f32),
        V(w_self.shape, bf16),
        V((1,) + w_rel.shape, bf16),
        V(w_cross.shape, bf16),
        V(w_attn_out.shape, bf16),
        V((1,) + w_in.shape, bf16),
        V((1,) + w_out.shape, bf16),
        V((lanes, 6, span, cols), bf16),
        V((lanes, 2, span, cols), bf16),
        V((2, lanes, 2, span, cols), bf16),
        V((1, width, cols), bf16),
        V((1, width, cols), bf16),
        V((2, espan, cols), bf16),
        V((espan, cols), bf16),
        V((span, cols), f32),
        V((span, cols), f32),
        V((4, TILE, cols), bf16),
        V((9, 8, width), f32),
        V((4, 8, cols), f32),
        V((8, words), f32),
        V((8, hidden), f32),
        V((vec_rows, cols), f32),
        V((ring, vec_rows, cols), f32),
        V((4, 16, cols), f32),
        *[V((ring, m, block, w), bf16) for m, w in shapes],
        *[V((ring - 1, m, block, w), bf16) for m, w in shapes],
        pltpu.SemaphoreType.DMA((32,)),
        pltpu.SemaphoreType.DMA((64,)),
        pltpu.SemaphoreType.DMA((64,)),
        pltpu.SemaphoreType.DMA((128,)),
        pltpu.SemaphoreType.DMA((128,)),
        pltpu.SemaphoreType.DMA((8, 4)),
    ]
    result, g_in, g_enc, vec, g_self, g_rel, g_cross, g_att0, g_att1, g_win, g_wout = pl.pallas_call(
        functools.partial(layer_kernel, dims),
        out_shape=(
            jax.ShapeDtypeStruct((lanes, span, cols), bf16),
            jax.ShapeDtypeStruct((lanes, span, cols), f32),
            jax.ShapeDtypeStruct((espan, cols), f32),
            jax.ShapeDtypeStruct((vec_rows, cols), f32),
            *[jax.ShapeDtypeStruct((m, block, w), f32) for m, w in shapes],
        ),
        in_specs=[any_spec] * 3 + [vmem] + [any_spec] * 6 + [vmem] * 7,
        out_specs=(vmem,) * 11,
        scratch_shapes=scratch,
        compiler_params=pltpu.CompilerParams(
            collective_id=0, has_side_effects=True, vmem_limit_bytes=64 * 2**20
        ),
    )(
        layer_in,
        encoder_states,
        out_grad,
        par,
        w_self,
        w_rel,
        w_cross,
        w_attn_out,
        w_in,
        w_out,
        proj_bias,
        rel_bias[None],
        ffn_in_bias[None],
        smask,
        cmask,
        oh,
        oht,
    )
    each = cols // parts
    own = lax.axis_index("batch")
    rest = lax.dynamic_slice_in_dim(vec[:13], own * each, each, axis=1)
    rel_grad = lax.dynamic_slice_in_dim(vec[13, :words], own * (words // parts), words // parts)
    ffn_grad = vec[14 : 14 + hidden // cols].reshape(hidden)
    ffn_grad = lax.dynamic_slice_in_dim(ffn_grad, own * (hidden // parts), hidden // parts)
    return (
        result,
        g_in,
        g_enc,
        g_self,
        g_rel[0],
        g_cross,
        jnp.stack([g_att0[0].T, g_att1[0].T]),
        g_win[0],
        g_wout[0].T,
        rest[9:13],
        rel_grad,
        ffn_grad,
        rest[6:9],
        rest[0:3],
        rest[3:6],
    )


def solution(mesh):
    return jax.shard_map(
        per_device,
        mesh=mesh,
        in_specs=(
            P(None, "batch", "tensor"),
            P("batch", "tensor"),
            P(None, None, "tensor"),
            P(None, "tensor"),
            P(None, None, "tensor"),
            P(None, "tensor", None),
            P(None, "tensor"),
            P("tensor", None),
            P(None, "tensor"),
            P("tensor"),
            P("tensor"),
            P(None, "tensor"),
            P(None, "tensor"),
            P(None, "tensor"),
            P(),
            P("batch"),
            P("batch", None),
            P("batch", None),
            P(None, "batch", "tensor"),
        ),
        out_specs=(
            P(None, "batch", "tensor"),
            P(None, "batch", "tensor"),
            P("batch", "tensor"),
            P(None, "batch", "tensor"),
            P("batch", "tensor"),
            P(None, "batch", "tensor"),
            P(None, "tensor", "batch"),
            P("batch", "tensor"),
            P("tensor", "batch"),
            P(None, ("tensor", "batch")),
            P(("tensor", "batch")),
            P(("tensor", "batch")),
            P(None, ("tensor", "batch")),
            P(None, ("tensor", "batch")),
            P(None, ("tensor", "batch")),
        ),
        check_vma=False,
    )
```

```python
import functools

import jax
import jax.numpy as jnp
from jax import lax
from jax.experimental import pallas as pl
from jax.experimental.pallas import tpu as pltpu
from jax.sharding import PartitionSpec as P

HEAD_DIM = 64
norm_eps = 1e-05
neg_big = -1e30
MESH = pl.DeviceIdType.MESH
f32 = jnp.float32
bf16 = jnp.bfloat16
TILE = 128
HEAD_UNROLL = 2


def dot(a, b):
    return jnp.dot(a, b, preferred_element_type=f32)


def dot_nt(a, b):
    return lax.dot_general(a, b, (((1,), (1,)), ((), ())), preferred_element_type=f32)


def dot_tn(a, b):
    return lax.dot_general(a, b, (((0,), (0,)), ((), ())), preferred_element_type=f32)


def total(v):
    return jnp.sum(v, axis=1, keepdims=True)


def eight(v):
    return jnp.sum(v.reshape(v.shape[0] // 8, 8, v.shape[1]), axis=0)


def gelu_both(v):
    half = 0.5 * (1.0 + lax.erf(v * (0.5**0.5)))
    bell = jnp.exp(-0.5 * v * v) * 0.3989422804014327
    return v * half, half + v * bell


def layer_kernel(
    dims,
    x_in,
    e_in,
    og_in,
    par_in,
    ws_in,
    wr_in,
    wc_in,
    wa_in,
    wi_in,
    wo_in,
    pbias,
    rbias,
    fbias,
    smask,
    cmask,
    oh,
    oht,
    out_ref,
    gin_ref,
    genc_ref,
    vec_ref,
    gs_ref,
    gr_ref,
    gc_ref,
    ga0_ref,
    ga1_ref,
    gi_ref,
    go_ref,
    par,
    xf,
    ef,
    df,
    f1,
    f2,
    act,
    gp,
    qb,
    kb,
    vb,
    relb,
    att,
    catt,
    cq,
    ck,
    cv,
    lse,
    ws,
    wr,
    wc,
    wa,
    wi,
    wo,
    pbuf,
    crecv,
    yrecv,
    lout,
    lrecv,
    macc,
    ga0,
    ga1,
    ecrecv,
    eyrecv,
    kacc,
    vacc,
    dracc,
    dkacc,
    dvacc,
    tile4,
    nacc,
    pacc,
    racc,
    facc,
    vec,
    vrecv,
    vquarter,
    nsum,
    nrecv,
    xs,
    xr,
    xc,
    xa0,
    xa1,
    xi,
    xo,
    zs,
    zr,
    zc,
    za0,
    za1,
    zi,
    zo,
    lsem,
    ssem,
    rsem,
    csem,
    dsem,
    bsem,
    tsem,
    free,
):
    lanes, span, espan, cols, width, hidden, heads, buckets, parts = dims
    half = span // 2
    tiles = half // TILE
    tensor = lax.axis_index("tensor")
    yy = tensor // 2
    cc = lax.rem(tensor, 2)
    y_peer = {"tensor": (1 - yy) * 2 + cc}
    c_peer = {"tensor": yy * 2 + (1 - cc)}
    t_peer = {"tensor": (1 - yy) * 2 + (1 - cc)}
    mine = tensor
    y_other = (1 - yy) * 2 + cc
    c_other = yy * 2 + (1 - cc)
    both_other = (1 - yy) * 2 + (1 - cc)

    batch = lax.axis_index("batch")
    ring = parts // 2
    at_ring = batch // 2
    at_pair = lax.rem(batch, 2)
    x_peer = {"batch": at_ring * 2 + (1 - at_pair)}

    def z_peer(step):
        return {"batch": lax.rem(at_ring + step, ring) * 2 + at_pair}

    barrier = pltpu.get_barrier_semaphore()
    for peer in (y_peer, c_peer, t_peer, x_peer):
        pl.semaphore_signal(barrier, inc=1, device_id=peer, device_id_type=MESH)

    @pl.loop(1, ring)
    def _(step):
        pl.semaphore_signal(barrier, inc=1, device_id=z_peer(step), device_id_type=MESH)

    counts = {"local": 0, "y": 0, "c": 0, "t": 0}

    def local(src, dst):
        at = counts["local"]
        counts["local"] += 1
        copy = pltpu.make_async_copy(src, dst, lsem.at[at])
        copy.start()
        return copy

    def send_y(src, dst):
        at = counts["y"]
        counts["y"] += 1
        copy = pltpu.make_async_remote_copy(
            src_ref=src,
            dst_ref=dst,
            send_sem=ssem.at[at],
            recv_sem=rsem.at[at],
            device_id=y_peer,
            device_id_type=MESH,
        )
        copy.start()
        return copy

    def send_c(src, dst):
        at = counts["c"]
        counts["c"] += 1
        copy = pltpu.make_async_remote_copy(
            src_ref=src,
            dst_ref=dst,
            send_sem=csem.at[at],
            recv_sem=dsem.at[at],
            device_id=c_peer,
            device_id_type=MESH,
        )
        copy.start()
        return copy

    def send_t(src, dst):
        at = counts["t"]
        counts["t"] += 1
        copy = pltpu.make_async_remote_copy(
            src_ref=src,
            dst_ref=dst,
            send_sem=tsem.at[0, at],
            recv_sem=tsem.at[1, at],
            device_id=t_peer,
            device_id_type=MESH,
        )
        copy.start()
        return copy

    own_half = pl.ds(pl.multiple_of(cc * half, half), half)
    other_half = pl.ds(pl.multiple_of((1 - cc) * half, half), half)

    x_copies = [local(x_in.at[n], xf.at[n, mine]) for n in range(lanes)]
    ws_copy = local(ws_in, ws)
    wr_copy = local(wr_in, wr.at[0])
    wa_copy = local(wa_in, wa)
    e_copy = local(e_in, ef.at[0, mine])
    wc_copy = local(wc_in, wc)
    og_copies = [
        local(og_in.at[n, own_half], df.at[n, mine, own_half]) for n in range(lanes)
    ]
    wi_copy = local(wi_in, wi.at[0])
    wo_copy = local(wo_in, wo.at[0])
    par[mine] = par_in[...]
    pl.semaphore_wait(barrier, 3 + ring)

    class Gather:
        def __init__(self, ref, at=None):
            def block(q):
                return ref.at[q] if at is None else ref.at[at, q]

            self.block = block
            self.by_y = send_y(block(mine), block(mine))
            self.by_c = send_c(block(mine), block(mine))

        def finish(self):
            self.by_y.wait_recv()
            self.on = send_c(self.block(y_other), self.block(y_other))
            self.by_c.wait_recv()
            self.on.wait_recv()

        def done(self):
            self.by_y.wait_send()
            self.by_c.wait_send()
            self.on.wait_send()

    class Deal:
        def __init__(self, n):
            to_own = df.at[n, mine, own_half]
            to_other = df.at[n, mine, other_half]
            self.copies = [
                send_y(og_in.at[n, own_half], to_own),
                send_t(og_in.at[n, other_half], to_other),
                send_c(og_in.at[n, other_half], to_other),
            ]

        def finish(self):
            for copy in self.copies:
                copy.wait()

    x_gather = []
    for n in range(lanes):
        x_copies[n].wait()
        x_gather.append(Gather(xf, n))
        if n == 0:
            par_gather = Gather(par)

    for ref in (nacc, pacc, racc, facc, kacc, vacc):
        ref[...] = jnp.zeros(ref.shape, ref.dtype)

    lane_c = lax.broadcasted_iota(jnp.int32, (1, cols), 1)

    def head_f(h):
        return (lane_c // HEAD_DIM == h).astype(f32)

    def head_b(h):
        return head_f(h).astype(bf16)

    lane_w = lax.broadcasted_iota(jnp.int32, (1, 2 * heads * buckets), 1)

    def word_b(h):
        mask = lax.rem(lane_w, heads * buckets) // buckets == h
        return mask.astype(f32).astype(bf16)

    lane_r = lax.broadcasted_iota(jnp.int32, (1, heads * buckets), 1)

    def word_f(h):
        return (lane_r // buckets == h).astype(f32)

    flip = (
        lax.broadcasted_iota(jnp.int32, (half, half), 0)
        + lax.broadcasted_iota(jnp.int32, (half, half), 1)
        == half - 1
    )
    flip = flip.astype(f32).astype(bf16)
    slot = lax.broadcasted_iota(jnp.int32, (1, 128), 1)

    def rows_of(i):
        return pl.ds(pl.multiple_of(i * TILE, TILE), TILE)

    def own_tile(i):
        return pl.ds(pl.multiple_of(cc * half + i * TILE, TILE), TILE)

    def which_half(i):
        return lax.rem(i + cc, 2)

    def half_rows(which):
        return pl.ds(pl.multiple_of(which * half, half), half)

    def col_of(j):
        return pl.ds(pl.multiple_of(j * cols, cols), cols)

    def wide(ref, n, rows):
        return jnp.concatenate([ref[n, q, rows, :] for q in range(4)], axis=1)

    def summed(n, parity, i):
        rows = own_tile(i)
        mine_part = wide(pbuf, n, rows).astype(f32)
        return mine_part + wide(yrecv.at[parity], n, rows_of(i)).astype(f32)

    def put_wide(ref, n, rows, v):
        for q in range(4):
            ref[n, q, rows, :] = v[:, q * cols : (q + 1) * cols].astype(ref.dtype)

    def param(k):
        return jnp.concatenate([par[q, k : k + 1, :] for q in range(4)], axis=1)

    def put_slot(ref, rows, k, v):
        ref[rows, :] = jnp.where(slot == k, v, ref[rows, :])

    def get_slot(rows, k):
        return total(jnp.where(slot == k, lse[rows, :], 0.0))

    class Reduce:
        def __init__(self, n, parity):
            self.n = n
            self.parity = parity
            self.first = send_c(pbuf.at[n, :, other_half], crecv.at[n])

        def middle(self):
            n = self.n
            self.first.wait_recv()

            @pl.loop(0, tiles)
            def _(i):
                rows = own_tile(i)
                for q in range(4):
                    both = pbuf[n, q, rows, :].astype(f32)
                    both = both + crecv[n, q, rows_of(i), :].astype(f32)
                    pbuf[n, q, rows, :] = both.astype(bf16)

            self.second = send_y(pbuf.at[n, :, own_half], yrecv.at[self.parity, n])

        def finish(self):
            self.first.wait_send()
            self.second.wait()

    class Scatter:
        def __init__(self, part, from_c, from_y):
            self.part, self.from_c, self.from_y = part, from_c, from_y
            self.first = [
                send_c(part.at[2 * k + 1 - cc, pl.ds(r * half, half)], from_c.at[2 * k + r])
                for k in range(2)
                for r in range(2)
            ]

        def middle(self):
            for copy in self.first:
                copy.wait_recv()
            part = self.part
            for k in range(2):
                for r in range(2):

                    @pl.loop(0, tiles)
                    def _(i, k=k, r=r):
                        rows = rows_of(i + r * tiles)
                        both = part[2 * k + cc, rows, :].astype(f32)
                        both = both + self.from_c[2 * k + r, rows_of(i), :].astype(f32)
                        part[2 * k + cc, rows, :] = both.astype(bf16)

            self.second = [
                send_y(part.at[y_other, pl.ds(r * half, half)], self.from_y.at[r]) for r in range(2)
            ]

        def finish(self, store):
            for copy in self.second:
                copy.wait()
            for copy in self.first:
                copy.wait_send()
            for r in range(2):

                @pl.loop(0, tiles)
                def _(i, r=r):
                    rows = rows_of(i + r * tiles)
                    store(
                        rows,
                        self.part[mine, rows, :].astype(f32)
                        + self.from_y[r, rows_of(i), :].astype(f32),
                    )

    class Share:
        def __init__(self, grad, pair, far, out, at):
            self.grad, self.pair, self.far, self.out, self.at = grad, pair, far, out, at
            self.block = width // parts

            @pl.loop(0, ring)
            def _(z):
                self.near(self.rows(z, 1 - at_pair), pair.at[z]).start()

        def rows(self, z, x):
            start = pl.multiple_of((z * 2 + x) * self.block, self.block)
            return self.grad.at[:, pl.ds(start, self.block), :]

        def near(self, src, dst):
            return pltpu.make_async_remote_copy(
                src_ref=src,
                dst_ref=dst,
                send_sem=bsem.at[self.at, 0],
                recv_sem=bsem.at[self.at, 1],
                device_id=x_peer,
                device_id_type=MESH,
            )

        def away(self, src, dst, step):
            return pltpu.make_async_remote_copy(
                src_ref=src,
                dst_ref=dst,
                send_sem=bsem.at[self.at, 2],
                recv_sem=bsem.at[self.at, 3],
                device_id=z_peer(step),
                device_id_type=MESH,
            )

        def middle(self):
            self.near(self.pair, self.pair).wait()

            @pl.loop(0, ring)
            def _(z):
                for m in range(self.grad.shape[0]):
                    start = pl.multiple_of((z * 2 + at_pair) * self.block, self.block)
                    own = self.grad[m, pl.ds(start, self.block), :].astype(f32)
                    self.pair[z, m] = (own + self.pair[z, m].astype(f32)).astype(bf16)

            @pl.loop(1, ring)
            def _(step):
                self.away(
                    self.pair.at[lax.rem(at_ring + step, ring)], self.far.at[step - 1], step
                ).start()

        def last(self):
            self.away(self.far, self.far, 1).wait()
            self.out[...] = self.pair[at_ring].astype(f32)

            @pl.loop(1, ring)
            def _(step):
                self.out[...] += self.far[step - 1].astype(f32)

    def norm_rows(resid):
        mean = total(resid) * (1.0 / width)
        centred = resid - mean
        var = total(centred * centred) * (1.0 / width)
        rs = lax.rsqrt(var + norm_eps)
        return centred * rs, rs

    def norm_grad(grad, xh, rs, gain, k):
        q = grad * gain
        m1 = total(q) * (1.0 / width)
        m2 = total(q * xh) * (1.0 / width)
        back = rs * (q - m1 - xh * m2)
        nacc[k] += eight(grad * xh)
        nacc[3 + k] += eight(grad)
        nacc[6 + k] += eight(back)
        return back

    at_scale = 2 * lanes * heads

    def give(ref, n):
        return send_c(ref.at[n, :, own_half], ref.at[n, :, own_half])

    def norm_first(n):
        @pl.loop(0, tiles)
        def _(i):
            rows = own_tile(i)
            resid = wide(xf, n, rows).astype(f32) + summed(n, 1, i) + param(0)
            xh, rs = norm_rows(resid)
            put_slot(lse, rows, at_scale + n, rs)
            put_wide(f1, n, rows, xh * param(3) + param(6))

        return give(f1, n)

    def norm_second(n):
        @pl.loop(0, tiles)
        def _(i):
            rows = own_tile(i)
            resid = wide(f1, n, rows).astype(f32) + summed(n, 0, i) + param(1)
            xh, rs = norm_rows(resid)
            put_slot(lse, rows, at_scale + lanes + n, rs)
            put_wide(f2, n, rows, xh * param(4) + param(7))

        return give(f2, n)

    out_copies = []

    def norm_third(n):
        @pl.loop(0, tiles)
        def _(i):
            rows = own_tile(i)
            resid = wide(f2, n, rows).astype(f32) + summed(n, 1, i) + param(2)
            xh, rs = norm_rows(resid)
            out = xh * param(5) + param(8)
            for q in range(4):
                tile4[q] = out[:, q * cols : (q + 1) * cols].astype(bf16)
            out_ref[n, rows, :] = tile4[mine]
            lout[n, rows_of(i), :] = tile4[c_other]
            grad = wide(df, n, rows).astype(f32)
            put_wide(df, n, rows, norm_grad(grad, xh, rs, param(5), 2))

        out_copies.append(send_c(lout.at[n], lrecv.at[n]))
        return give(df, n)

    def norm_second_back(n):
        @pl.loop(0, tiles)
        def _(i):
            rows = own_tile(i)
            grad = wide(df, n, rows).astype(f32) + summed(n, 0, i)
            gain = param(4)
            xh = (wide(f2, n, rows).astype(f32) - param(7)) * (1.0 / gain)
            rs = get_slot(rows, at_scale + lanes + n)
            put_wide(df, n, rows, norm_grad(grad, xh, rs, gain, 1))

    def norm_first_back(n):
        @pl.loop(0, tiles)
        def _(i):
            rows = own_tile(i)
            grad = wide(df, n, rows).astype(f32) + summed(n, 1, i)
            gain = param(3)
            xh = (wide(f1, n, rows).astype(f32) - param(6)) * (1.0 / gain)
            rs = get_slot(rows, at_scale + n)
            put_wide(df, n, rows, norm_grad(grad, xh, rs, gain, 0))

    def halves(got, body):
        @pl.loop(0, 2)
        def _(i):
            if got is not None:

                @pl.when(i == 1)
                def _():
                    got.wait()

            which = which_half(i)
            body(which, half_rows(which))

    def each_head(body):
        pl.loop(0, heads, unroll=HEAD_UNROLL)(body)

    def self_score(n, which, rows, h, diag):
        qh = qb[n, rows, :] * head_b(h)
        spread = dot(relb[n, rows, :] * word_b(h), oh[which])
        bias = pltpu.roll(spread, 0, 1, stride=1, stride_axis=0)
        s = dot_nt(qh, kb[0]) + smask[rows, :].astype(f32)
        if n > 0:
            s = jnp.where(diag, total(qh.astype(f32) * kb[n, rows, :].astype(f32)), s)
        return qh, s + bias

    def diagonal(which):
        r = lax.broadcasted_iota(jnp.int32, (half, span), 0)
        s = lax.broadcasted_iota(jnp.int32, (half, span), 1)
        return s == r + which * half

    def project_rows(n):
        def body(which, rows):
            x = wide(xf, n, rows)
            q = (dot(x, ws[0]) + pbias[0:1, :]).astype(bf16)
            qb[n, rows, :] = (q.astype(f32) * 0.125).astype(bf16)
            kb[n, rows, :] = dot(x, ws[1]).astype(bf16)
            vb[n, rows, :] = (dot(x, ws[2]) + pbias[1:2, :]).astype(bf16)
            rel = dot(x, wr[0]) + rbias[...]
            high = rel.astype(bf16)
            relb[n, rows, : heads * buckets] = high
            relb[n, rows, heads * buckets :] = (rel - high.astype(f32)).astype(bf16)

        halves(None, body)

    def self_forward(n):
        project_rows(n)

        def body(which, rows):
            macc[...] = jnp.zeros(macc.shape, f32)

            @each_head
            def _(h):
                diag = diagonal(which) if n > 0 else None
                qh, s = self_score(n, which, rows, h, diag)
                top = jnp.max(s, axis=1, keepdims=True)
                w = jnp.exp(s - top)
                sums = total(w)
                inverse = 1.0 / sums
                put_slot(lse, rows, n * heads + h, top + jnp.log(sums))
                if n > 0:
                    own = total(jnp.where(diag, w, 0.0)) * inverse
                    w = jnp.where(diag, 0.0, w)
                part = dot(w.astype(bf16), vb[0]) * inverse
                if n > 0:
                    part = part + own.astype(bf16).astype(f32) * vb[n, rows, :].astype(f32)
                macc[...] += part * head_f(h)

            low = macc[...].astype(bf16)
            att[n, rows, :] = low
            put_wide(pbuf, n, rows, dot(low, wa[0]))

        halves(None, body)

    def encoder_rows():
        @pl.loop(0, espan // TILE)
        def _(i):
            rows = rows_of(i)
            e = wide(ef, 0, rows)
            ck[rows, :] = dot(e, wc[1]).astype(bf16)
            cv[rows, :] = (dot(e, wc[2]) + pbias[3:4, :]).astype(bf16)

    def cross_forward(n, got):
        def body(which, rows):
            q = (dot(wide(f1, n, rows), wc[0]) + pbias[2:3, :]).astype(bf16)
            cq[n, rows, :] = (q.astype(f32) * 0.125).astype(bf16)
            macc[...] = jnp.zeros(macc.shape, f32)

            @each_head
            def _(h):
                s = dot_nt(cq[n, rows, :] * head_b(h), ck[...]) + cmask[rows, :].astype(f32)
                top = jnp.max(s, axis=1, keepdims=True)
                w = jnp.exp(s - top)
                sums = total(w)
                put_slot(lse, rows, (lanes + n) * heads + h, top + jnp.log(sums))
                macc[...] += dot(w.astype(bf16), cv[...]) * (1.0 / sums) * head_f(h)

            low = macc[...].astype(bf16)
            catt[n, rows, :] = low
            put_wide(pbuf, n, rows, dot(low, wa[1]))

        halves(got, body)

    def ffn_forward(n, got):
        def body(which, rows):
            @pl.loop(0, hidden // cols)
            def _(j):
                at = col_of(j)
                pre = dot(wide(f2, n, rows), wi[0, :, at]) + fbias[:, at]
                value, slope = gelu_both(pre)
                act[n, rows, at] = value.astype(bf16)
                gp[n, rows, at] = slope.astype(bf16)

            @pl.loop(0, width // cols)
            def _(j):
                pbuf[n, j, rows, :] = dot(act[n, rows, :], wo[0, :, col_of(j)]).astype(bf16)

        halves(got, body)

    def ffn_backward(n, got):
        def body(which, rows):
            @pl.loop(0, hidden // cols)
            def _(j):
                at = col_of(j)
                grad = dot_nt(wide(df, n, rows), wo[0, at, :]) * gp[n, rows, at].astype(f32)
                facc[:, at] += eight(grad)
                gp[n, rows, at] = grad.astype(bf16)

            @pl.loop(0, width // cols)
            def _(j):
                pbuf[n, j, rows, :] = dot_nt(gp[n, rows, :], wi[0, col_of(j), :]).astype(bf16)

        halves(got, body)

    def spot(k, h, size):
        row = pl.ds(pl.multiple_of(lax.rem(h, 2) * half, half), half)
        col = pl.ds(pl.multiple_of(k * span + (h // 2) * size, size), size)
        return row, col

    def stacked(n, k, size):
        parts = [act[(n,) + spot(k, h, size)] for h in range(heads)]
        return jnp.concatenate(parts, axis=0)

    def keep_head(h, p, ds, dh, qh):
        act[(0,) + spot(0, h, span)] = p
        act[(1,) + spot(0, h, span)] = ds
        act[(2,) + spot(0, h, cols)] = dh
        act[(2,) + spot(1, h, cols)] = qh

    def add_heads():
        vacc[...] += dot_tn(stacked(0, 0, span), stacked(2, 0, cols))
        kacc[...] += dot_tn(stacked(1, 0, span), stacked(2, 1, cols))

    def cross_backward(n, got):
        def body(which, rows):
            da = dot_nt(wide(df, n, rows), wa[1]).astype(bf16)
            macc[...] = jnp.zeros(macc.shape, f32)

            @each_head
            def _(h):
                qh = cq[n, rows, :] * head_b(h)
                dh = da * head_b(h)
                s = dot_nt(qh, ck[...]) + cmask[rows, :].astype(f32)
                p = jnp.exp(s - get_slot(rows, (lanes + n) * heads + h))
                dp = dot_nt(dh, cv[...])
                ds = (p * (dp - total(p * dp))).astype(bf16)
                keep_head(h, p.astype(bf16), ds, dh, qh)
                macc[...] += dot(ds, ck[...]) * head_f(h)

            add_heads()
            dq = macc[...] * 0.125
            pacc[2] += eight(dq)
            low = dq.astype(bf16)
            cq[n, rows, :] = low
            put_wide(pbuf, n, rows, dot_nt(low, wc[0]))

        halves(got, body)

    def encoder_backward():
        pacc[3] += eight(vacc[...])

        @pl.loop(0, espan // TILE)
        def _(i):
            rows = rows_of(i)
            dk = kacc[rows, :].astype(bf16)
            dv = vacc[rows, :].astype(bf16)
            ck[rows, :] = dk
            cv[rows, :] = dv
            part = dot_nt(dk, wc[1]) + dot_nt(dv, wc[2])
            for q in range(4):
                f2[0, q, rows, :] = part[:, q * cols : (q + 1) * cols].astype(bf16)

    def self_backward(n, got):
        def body(which, rows):
            da = dot_nt(wide(df, n, rows), wa[0]).astype(bf16)
            macc[...] = jnp.zeros(macc.shape, f32)
            dracc[...] = jnp.zeros(dracc.shape, f32)
            if n > 0:
                dkacc[...] = jnp.zeros(dkacc.shape, f32)
                dvacc[...] = jnp.zeros(dvacc.shape, f32)

            @each_head
            def _(h):
                diag = diagonal(which) if n > 0 else None
                qh, s = self_score(n, which, rows, h, diag)
                p = jnp.exp(s - get_slot(rows, n * heads + h))
                dh = da * head_b(h)
                dp = dot_nt(dh, vb[0])
                if n > 0:
                    vn = vb[n, rows, :].astype(f32)
                    dp = jnp.where(diag, total(dh.astype(f32) * vn), dp)
                ds = p * (dp - total(p * dp))
                turned = pltpu.roll(dot(flip, ds.astype(bf16)), 0, 1, stride=1, stride_axis=0)
                dracc[...] += dot(turned.astype(bf16), oht[which]) * word_f(h)
                if n > 0:
                    own_p = total(jnp.where(diag, p, 0.0)).astype(bf16).astype(f32)
                    own_s = total(jnp.where(diag, ds, 0.0)).astype(bf16).astype(f32)
                    p = jnp.where(diag, 0.0, p)
                    ds = jnp.where(diag, 0.0, ds)
                    dkacc[...] += own_s * qh.astype(f32)
                    dvacc[...] += own_p * dh.astype(f32)
                low = ds.astype(bf16)
                keep_head(h, p.astype(bf16), low, dh, qh)
                part = dot(low, kb[0])
                if n > 0:
                    part = part + own_s * kb[n, rows, :].astype(f32)
                macc[...] += part * head_f(h)

            add_heads()
            dq = macc[...] * 0.125
            drel = dracc[...]
            pacc[0] += eight(dq)
            racc[...] += eight(drel)
            qb[n, rows, :] = dq.astype(bf16)
            relb[n, rows, : heads * buckets] = dot(flip, drel.astype(bf16)).astype(bf16)
            if n > 0:
                pacc[1] += eight(dvacc[...])
                kb[n, rows, :] = dkacc[...].astype(bf16)
                vb[n, rows, :] = dvacc[...].astype(bf16)

        halves(got, body)
        if n == 0:
            pacc[1] += eight(vacc[...])
            kb[0] = kacc[...].astype(bf16)
            vb[0] = vacc[...].astype(bf16)

        @pl.loop(0, width // cols)
        def _(j):
            at = col_of(j)
            part = dot_nt(qb[n], ws[0, at, :]) + dot_nt(kb[n], ws[1, at, :])
            part = part + dot_nt(vb[n], ws[2, at, :])
            part = part + dot_nt(relb[n, :, : heads * buckets], wr[0, at, :])
            pbuf[n, j] = part.astype(bf16)

    def weight_grad(rows_ref, pieces, lane_count):
        @pl.loop(0, 4)
        def _(j):
            left = jnp.concatenate([rows_ref[n, j] for n in range(lane_count)], axis=0)
            for load, target, size in pieces:
                for start in range(0, size, cols):
                    step = min(cols, size - start)
                    right = jnp.concatenate(
                        [load(n, start, step) for n in range(lane_count)], axis=0
                    )
                    target[col_of(j), start : start + step] = dot_tn(left, right).astype(bf16)

    def of(ref):
        return lambda n, start, step: ref[n, :, start : start + step]

    words = heads * buckets

    order = list(range(lanes))
    late = order[1:] + order[:1]
    ws_copy.wait()
    wr_copy.wait()
    wa_copy.wait()
    reduces = {}
    gots = {}

    def after(n, parity, following):
        reduce = Reduce(n, parity)
        if following is not None:
            following()
        reduce.middle()
        reduces[n] = reduce

    def ready(n, norm):
        def go():
            reduces[n].finish()
            gots[n] = norm(n)

        return go

    deals = []
    for n in order:
        x_gather[n].finish()
        if n == 0:
            par_gather.finish()
        self_forward(n)
        if n == 0:
            e_copy.wait()
            e_gather = Gather(ef, 0)
        after(n, 1, None)
    wc_copy.wait()
    e_gather.finish()
    encoder_rows()
    ready(order[0], norm_first)()
    for k, n in enumerate(order):
        cross_forward(n, gots[n])
        og_copies[n].wait()
        following = order[k + 1] if k + 1 < lanes else None
        norm = ready(following, norm_first) if following else ready(order[0], norm_second)
        after(n, 0, norm)
        deals.append(Deal(n))
    wi_copy.wait()
    wo_copy.wait()

    def third_of(n):
        def go():
            deals[n].finish()
            ready(n, norm_third)()

        return go

    for k, n in enumerate(order):
        ffn_forward(n, gots[n])
        norm = ready(order[k + 1], norm_second) if k + 1 < lanes else third_of(order[0])
        after(n, 1, norm)
    for k, n in enumerate(order):
        ffn_backward(n, gots[n])
        after(n, 0, third_of(order[k + 1]) if k + 1 < lanes else None)
    weight_grad(df, [(of(act), wo.at[0], hidden)], lanes)
    share_o = Share(wo, xo, zo, go_ref, 0)
    pl.semaphore_signal(free.at[0], inc=1, device_id=c_peer, device_id_type=MESH)
    waited = set()

    def back_of(n, norm, k):
        def go():
            reduces[n].finish()
            norm(n)
            if k not in waited:
                waited.add(k)
                pl.semaphore_wait(free.at[k], 1)
            gots[n] = give(df, n)

        return go

    back_of(late[0], norm_second_back, 0)()
    weight_grad(f2, [(of(gp), wi.at[0], hidden)], lanes)
    share_i = Share(wi, xi, zi, gi_ref, 1)
    for k, n in enumerate(late):
        cross_backward(n, gots[n])
        after(n, 1, back_of(late[k + 1], norm_second_back, 0) if k + 1 < lanes else None)
        if k == 1:
            share_o.middle()
    weight_grad(df, [(of(catt), ga1.at[0], cols)], lanes)
    share_a1 = Share(ga1, xa1, za1, ga1_ref, 2)
    pl.semaphore_signal(free.at[1], inc=1, device_id=c_peer, device_id_type=MESH)
    encoder_backward()
    e_scatter = Scatter(f2.at[0], ecrecv, eyrecv)
    back_of(late[0], norm_first_back, 1)()
    e_scatter.middle()
    weight_grad(f1, [(of(cq), wc.at[0], cols)], lanes)
    weight_grad(
        ef,
        [
            (lambda n, a, b: ck[:, a : a + b], wc.at[1], cols),
            (lambda n, a, b: cv[:, a : a + b], wc.at[2], cols),
        ],
        1,
    )
    share_c = Share(wc, xc, zc, gc_ref, 4)
    share_i.middle()
    kacc[...] = jnp.zeros(kacc.shape, f32)
    vacc[...] = jnp.zeros(vacc.shape, f32)
    scatters = {}
    for k, n in enumerate(late):
        self_backward(n, gots[n])
        scatters[n] = Scatter(pbuf.at[n], crecv.at[n], yrecv.at[0, n])
        if k + 1 < lanes:
            back_of(late[k + 1], norm_first_back, 1)()
        scatters[n].middle()
        if k == 0:

            def store_enc(rows, v):
                genc_ref[rows, :] = v

            e_scatter.finish(store_enc)
            share_o.last()
            share_a1.middle()
        if k == 1:
            share_i.last()
            share_c.middle()
    for n in order:
        out_copies[n].wait()

        @pl.loop(0, tiles)
        def _(i, n=n):
            rows = pl.ds(pl.multiple_of((1 - cc) * half + i * TILE, TILE), TILE)
            out_ref[n, rows, :] = lrecv[n, rows_of(i), :]

    def vec_copy(src, dst, k, peer):
        return pltpu.make_async_remote_copy(
            src_ref=src,
            dst_ref=dst,
            send_sem=bsem.at[7, k],
            recv_sem=bsem.at[7, k + 1],
            device_id=peer,
            device_id_type=MESH,
        )

    for k in range(9):
        nsum[k : k + 1, :] = jnp.sum(nacc[k], axis=0, keepdims=True)
    norm_sums = send_c(nsum, nrecv)
    norm_sums.wait()
    for k in range(9):
        row = nsum[k : k + 1, :] + nrecv[k : k + 1, :]
        for q in range(4):
            vquarter[q, k : k + 1, :] = row[:, q * cols : (q + 1) * cols]
    vec[...] = jnp.zeros(vec.shape, f32)
    vec[0:9, :] = vquarter[mine, 0:9, :]
    for k in range(4):
        vec[9 + k : 10 + k, :] = jnp.sum(pacc[k], axis=0, keepdims=True)
    vec[13:14, :words] = jnp.sum(racc[...], axis=0, keepdims=True)
    row = jnp.sum(facc[...], axis=0, keepdims=True)
    for k in range(hidden // cols):
        vec[14 + k : 15 + k, :] = row[:, k * cols : (k + 1) * cols]
    vec_pair = vec_copy(vec, vrecv.at[0], 0, x_peer)
    vec_pair.start()
    weight_grad(df, [(of(att), ga0.at[0], cols)], lanes)
    share_a0 = Share(ga0, xa0, za0, ga0_ref, 3)
    weight_grad(
        xf,
        [
            (of(qb), ws.at[0], cols),
            (of(kb), ws.at[1], cols),
            (of(vb), ws.at[2], cols),
            (of(relb), wr.at[0], words),
        ],
        lanes,
    )
    share_r = Share(wr, xr, zr, gr_ref, 5)
    share_s = Share(ws, xs, zs, gs_ref, 6)
    for n in late:

        def store_in(rows, v, n=n):
            gin_ref[n, rows, :] = df[n, mine, rows, :].astype(f32) + v

        scatters[n].finish(store_in)
    share_a1.last()
    share_c.last()
    share_a0.middle()
    share_r.middle()
    share_s.middle()
    vec_pair.wait()
    vec[...] += vrecv[0]

    @pl.loop(1, ring)
    def _(step):
        vec_copy(vec, vrecv.at[step], 2, z_peer(step)).start()

    share_a0.last()
    share_r.last()
    share_s.last()
    every_vec = vrecv.at[pl.ds(1, ring - 1)]
    vec_copy(every_vec, every_vec, 2, z_peer(1)).wait()
    vec_ref[...] = vec[...]

    @pl.loop(1, ring)
    def _(step):
        vec_ref[...] += vrecv[step]

    for item in x_gather + [par_gather, e_gather]:
        item.done()


def grouping(code, span):
    place = jnp.arange(span, dtype=jnp.int32)
    width = jnp.right_shift(jnp.int32(span), code)
    return (place, place // width, width)


def layout(code, fill, span):
    place, group, width = grouping(code, span)
    half = jnp.maximum(width // 2, 1)
    lengths = width - fill % half
    slots = jnp.arange(fill.shape[0], dtype=jnp.int32)
    own = jnp.sum(jnp.where(group[:, None] == slots, lengths, 0), axis=1)
    return (group, place % width < own)


def per_device(
    layer_in,
    encoder_states,
    w_self,
    w_rel,
    w_cross,
    w_attn_out,
    w_in,
    w_out,
    proj_bias,
    rel_bias,
    ffn_in_bias,
    out_bias,
    norm_gain,
    norm_bias,
    rel_buckets,
    slot_log,
    tgt_fill,
    enc_fill,
    out_grad,
):
    lanes, span, cols = layer_in.shape
    espan = encoder_states.shape[0]
    width = w_self.shape[1]
    hidden = w_in.shape[1]
    heads = cols // HEAD_DIM
    words = w_rel.shape[1]
    buckets = words // heads
    spots = jnp.arange(span, dtype=jnp.int32)
    group, valid = layout(slot_log[0], tgt_fill[0], span)
    allowed = (group[:, None] == group[None, :]) & valid[None, :]
    allowed = allowed & (spots[:, None] >= spots[None, :])
    smask = jnp.where(allowed, 0.0, neg_big).astype(bf16)
    egroup, evalid = layout(slot_log[0], enc_fill[0], espan)
    cmask = jnp.where((group[:, None] == egroup[None, :]) & evalid[None, :], 0.0, neg_big)
    cmask = cmask.astype(bf16)
    turned = jnp.concatenate([rel_buckets[:1], rel_buckets[:0:-1]])
    half = span // 2
    turned = jnp.stack([turned, jnp.roll(turned, half)])
    codes = jnp.arange(buckets, dtype=jnp.int32)
    oh = (turned[:, None, :] == jnp.tile(codes, 2 * heads)[:, None]).astype(bf16)
    turned = jnp.roll(turned, half - 1, axis=1)
    oht = (turned[:, :, None] == jnp.tile(codes, heads)).astype(bf16)
    par = jnp.concatenate(
        [out_bias, norm_gain, norm_bias, jnp.zeros((7, cols), f32)], axis=0
    )
    parts = lax.axis_size("batch")
    ring = parts // 2
    block = width // parts
    shapes = [(3, cols), (1, words), (3, cols), (1, cols), (1, cols), (1, hidden), (1, hidden)]
    vec_rows = -(-(14 + hidden // cols) // 8) * 8
    dims = (lanes, span, espan, cols, width, hidden, heads, buckets, parts)
    any_spec = pl.BlockSpec(memory_space=pl.ANY)
    vmem = pl.BlockSpec(memory_space=pltpu.VMEM)
    V = pltpu.VMEM
    scratch = [
        V((4, 16, cols), f32),
        V((lanes, 4, span, cols), bf16),
        V((1, 4, espan, cols), bf16),
        V((lanes, 4, span, cols), bf16),
        V((lanes, 4, span, cols), bf16),
        V((lanes, 4, span, cols), bf16),
        V((lanes, span, hidden), bf16),
        V((lanes, span, hidden), bf16),
        V((lanes, span, cols), bf16),
        V((lanes, span, cols), bf16),
        V((lanes, span, cols), bf16),
        V((lanes, span, 2 * words), bf16),
        V((lanes, span, cols), bf16),
        V((lanes, span, cols), bf16),
        V((lanes, span, cols), bf16),
        V((espan, cols), bf16),
        V((espan, cols), bf16),
        V((span, 128), f32),
        V(w_self.shape, bf16),
        V((1,) + w_rel.shape, bf16),
        V(w_cross.shape, bf16),
        V(w_attn_out.shape, bf16),
        V((1,) + w_in.shape, bf16),
        V((1,) + w_out.shape, bf16),
        V((lanes, 4, span, cols), bf16),
        V((lanes, 4, half, cols), bf16),
        V((2, lanes, 4, half, cols), bf16),
        V((lanes, half, cols), bf16),
        V((lanes, half, cols), bf16),
        V((half, cols), f32),
        V((1, width, cols), bf16),
        V((1, width, cols), bf16),
        V((4, espan // 2, cols), bf16),
        V((2, espan // 2, cols), bf16),
        V((span, cols), f32),
        V((span, cols), f32),
        V((half, words), f32),
        V((half, cols), f32),
        V((half, cols), f32),
        V((4, TILE, cols), bf16),
        V((9, 8, width), f32),
        V((4, 8, cols), f32),
        V((8, words), f32),
        V((8, hidden), f32),
        V((vec_rows, cols), f32),
        V((ring, vec_rows, cols), f32),
        V((4, 16, cols), f32),
        V((16, width), f32),
        V((16, width), f32),
        *[V((ring, m, block, w), bf16) for m, w in shapes],
        *[V((ring - 1, m, block, w), bf16) for m, w in shapes],
        pltpu.SemaphoreType.DMA((32,)),
        pltpu.SemaphoreType.DMA((64,)),
        pltpu.SemaphoreType.DMA((64,)),
        pltpu.SemaphoreType.DMA((128,)),
        pltpu.SemaphoreType.DMA((128,)),
        pltpu.SemaphoreType.DMA((8, 4)),
        pltpu.SemaphoreType.DMA((2, 4)),
        pltpu.SemaphoreType.REGULAR((2,)),
    ]
    result, g_in, g_enc, vec, g_self, g_rel, g_cross, g_att0, g_att1, g_win, g_wout = pl.pallas_call(
        functools.partial(layer_kernel, dims),
        out_shape=(
            jax.ShapeDtypeStruct((lanes, span, cols), bf16),
            jax.ShapeDtypeStruct((lanes, span, cols), f32),
            jax.ShapeDtypeStruct((espan, cols), f32),
            jax.ShapeDtypeStruct((vec_rows, cols), f32),
            *[jax.ShapeDtypeStruct((m, block, w), f32) for m, w in shapes],
        ),
        in_specs=[any_spec] * 3 + [vmem] + [any_spec] * 6 + [vmem] * 7,
        out_specs=(vmem,) * 11,
        scratch_shapes=scratch,
        compiler_params=pltpu.CompilerParams(
            collective_id=0, has_side_effects=True, vmem_limit_bytes=64 * 2**20
        ),
    )(
        layer_in,
        encoder_states,
        out_grad,
        par,
        w_self,
        w_rel,
        w_cross,
        w_attn_out,
        w_in,
        w_out,
        proj_bias,
        rel_bias[None],
        ffn_in_bias[None],
        smask,
        cmask,
        oh,
        oht,
    )
    each = cols // parts
    own = lax.axis_index("batch")
    rest = lax.dynamic_slice_in_dim(vec[:13], own * each, each, axis=1)
    rel_grad = lax.dynamic_slice_in_dim(vec[13, :words], own * (words // parts), words // parts)
    ffn_grad = vec[14 : 14 + hidden // cols].reshape(hidden)
    ffn_grad = lax.dynamic_slice_in_dim(ffn_grad, own * (hidden // parts), hidden // parts)
    return (
        result,
        g_in,
        g_enc,
        g_self,
        g_rel[0],
        g_cross,
        jnp.stack([g_att0[0].T, g_att1[0].T]),
        g_win[0],
        g_wout[0].T,
        rest[9:13],
        rel_grad,
        ffn_grad,
        rest[6:9],
        rest[0:3],
        rest[3:6],
    )


def solution(mesh):
    return jax.shard_map(
        per_device,
        mesh=mesh,
        in_specs=(
            P(None, "batch", "tensor"),
            P("batch", "tensor"),
            P(None, None, "tensor"),
            P(None, "tensor"),
            P(None, None, "tensor"),
            P(None, "tensor", None),
            P(None, "tensor"),
            P("tensor", None),
            P(None, "tensor"),
            P("tensor"),
            P("tensor"),
            P(None, "tensor"),
            P(None, "tensor"),
            P(None, "tensor"),
            P(),
            P("batch"),
            P("batch", None),
            P("batch", None),
            P(None, "batch", "tensor"),
        ),
        out_specs=(
            P(None, "batch", "tensor"),
            P(None, "batch", "tensor"),
            P("batch", "tensor"),
            P(None, "batch", "tensor"),
            P("batch", "tensor"),
            P(None, "batch", "tensor"),
            P(None, "tensor", "batch"),
            P("batch", "tensor"),
            P("tensor", "batch"),
            P(None, ("tensor", "batch")),
            P(("tensor", "batch")),
            P(("tensor", "batch")),
            P(None, ("tensor", "batch")),
            P(None, ("tensor", "batch")),
            P(None, ("tensor", "batch")),
        ),
        check_vma=False,
    )
```

```python
import functools

import jax
import jax.numpy as jnp
from jax import lax
from jax.experimental import pallas as pl
from jax.experimental.pallas import tpu as pltpu
from jax.sharding import PartitionSpec as P

HEAD_DIM = 64
norm_eps = 1e-05
neg_big = -1e30
MESH = pl.DeviceIdType.MESH
f32 = jnp.float32
bf16 = jnp.bfloat16
TILE = 128
HEAD_UNROLL = 2


def dot(a, b):
    return jnp.dot(a, b, preferred_element_type=f32)


def dot_nt(a, b):
    return lax.dot_general(a, b, (((1,), (1,)), ((), ())), preferred_element_type=f32)


def dot_tn(a, b):
    return lax.dot_general(a, b, (((0,), (0,)), ((), ())), preferred_element_type=f32)


def total(v):
    return jnp.sum(v, axis=1, keepdims=True)


def eight(v):
    return jnp.sum(v.reshape(v.shape[0] // 8, 8, v.shape[1]), axis=0)


def gelu_both(v):
    half = 0.5 * (1.0 + lax.erf(v * (0.5**0.5)))
    bell = jnp.exp(-0.5 * v * v) * 0.3989422804014327
    return v * half, half + v * bell


def layer_kernel(
    dims,
    x_in,
    e_in,
    og_in,
    ob_in,
    ng_in,
    nb_in,
    ws_in,
    wr_in,
    wc_in,
    wa_in,
    wi_in,
    wo_in,
    pbias,
    rbias,
    fbias,
    buckets_in,
    code_in,
    fill_in,
    efill_in,
    out_ref,
    gin_ref,
    genc_ref,
    vec_ref,
    gs_ref,
    gr_ref,
    gc_ref,
    ga0_ref,
    ga1_ref,
    gi_ref,
    go_ref,
    wgc,
    smask,
    cmask,
    oh_first,
    oh_second,
    oht_first,
    oht_second,
    par,
    xf,
    ef,
    df,
    f1,
    f2,
    act,
    gp,
    qb,
    kb,
    vb,
    relb,
    att,
    catt,
    cq,
    ck,
    cv,
    lse,
    ws,
    wr,
    wc,
    wa,
    wi,
    wo,
    pbuf,
    crecv,
    yrecv,
    lout,
    lrecv,
    macc,
    ga0,
    ga1,
    ecrecv,
    eyrecv,
    kacc,
    vacc,
    dracc,
    dkacc,
    dvacc,
    nacc,
    pacc,
    racc,
    facc,
    vec,
    vrecv,
    vquarter,
    nsum,
    nrecv,
    xq,
    xk,
    xv,
    xr,
    xc,
    xa0,
    xa1,
    xi,
    xo,
    zq,
    zk,
    zv,
    zr,
    zc,
    za0,
    za1,
    zi,
    zo,
    lsem,
    ssem,
    rsem,
    csem,
    dsem,
    bsem,
    tsem,
    wsem,
    free,
):
    lanes, span, espan, cols, width, hidden, heads, buckets, parts = dims
    half = span // 2
    tiles = half // TILE
    tensor = lax.axis_index("tensor")
    yy = tensor // 2
    cc = lax.rem(tensor, 2)
    y_peer = {"tensor": (1 - yy) * 2 + cc}
    c_peer = {"tensor": yy * 2 + (1 - cc)}
    t_peer = {"tensor": (1 - yy) * 2 + (1 - cc)}
    mine = tensor
    y_other = (1 - yy) * 2 + cc
    c_other = yy * 2 + (1 - cc)
    both_other = (1 - yy) * 2 + (1 - cc)

    batch = lax.axis_index("batch")
    ring = parts // 2
    at_ring = batch // 2
    at_pair = lax.rem(batch, 2)
    x_peer = {"batch": at_ring * 2 + (1 - at_pair)}

    def z_peer(step):
        return {"batch": lax.rem(at_ring + step, ring) * 2 + at_pair}

    barrier = pltpu.get_barrier_semaphore()
    for peer in (y_peer, c_peer, t_peer):
        pl.semaphore_signal(barrier, inc=1, device_id=peer, device_id_type=MESH)

    @pl.loop(1, parts)
    def _(step):
        peer = {"batch": lax.rem(batch + step, parts)}
        pl.semaphore_signal(barrier, inc=1, device_id=peer, device_id_type=MESH)

    counts = {"local": 0, "y": 0, "c": 0, "t": 0}

    def local(src, dst):
        at = counts["local"]
        counts["local"] += 1
        copy = pltpu.make_async_copy(src, dst, lsem.at[at])
        copy.start()
        return copy

    def send_y(src, dst):
        at = counts["y"]
        counts["y"] += 1
        copy = pltpu.make_async_remote_copy(
            src_ref=src,
            dst_ref=dst,
            send_sem=ssem.at[at],
            recv_sem=rsem.at[at],
            device_id=y_peer,
            device_id_type=MESH,
        )
        copy.start()
        return copy

    def send_c(src, dst):
        at = counts["c"]
        counts["c"] += 1
        copy = pltpu.make_async_remote_copy(
            src_ref=src,
            dst_ref=dst,
            send_sem=csem.at[at],
            recv_sem=dsem.at[at],
            device_id=c_peer,
            device_id_type=MESH,
        )
        copy.start()
        return copy

    def send_t(src, dst):
        at = counts["t"]
        counts["t"] += 1
        copy = pltpu.make_async_remote_copy(
            src_ref=src,
            dst_ref=dst,
            send_sem=tsem.at[0, at],
            recv_sem=tsem.at[1, at],
            device_id=t_peer,
            device_id_type=MESH,
        )
        copy.start()
        return copy

    own_half = pl.ds(pl.multiple_of(cc * half, half), half)
    other_half = pl.ds(pl.multiple_of((1 - cc) * half, half), half)

    x_copies = [local(x_in.at[n], xf.at[n, mine]) for n in range(lanes)]
    own_rows = pl.ds(pl.multiple_of(cc * cols, cols), cols)
    own_parts = [
        local(wa_in.at[0], act.at[yy, own_rows]),
        local(wa_in.at[1], gp.at[1 + yy, own_rows]),
    ]
    ws_copy = local(ws_in, ws)
    wr_copy = local(wr_in, wr.at[0])
    wa_copy = local(wa_in, wa)
    e_copy = local(e_in, ef.at[0, mine])
    wc_copy = local(wc_in, wc)
    og_copies = [
        local(og_in.at[n, own_half], df.at[n, mine, own_half]) for n in range(lanes)
    ]
    par[mine] = jnp.zeros(par.shape[1:], f32)
    par[mine, 0:3, :] = ob_in[...]
    par[mine, 3:6, :] = ng_in[...]
    par[mine, 6:9, :] = nb_in[...]
    pl.semaphore_wait(barrier, 2 + parts)

    class Gather:
        def __init__(self, ref, at=None):
            def block(q):
                return ref.at[q] if at is None else ref.at[at, q]

            self.block = block
            self.by_y = send_y(block(mine), block(mine))
            self.by_c = send_c(block(mine), block(mine))

        def finish(self):
            self.by_y.wait_recv()
            self.on = send_c(self.block(y_other), self.block(y_other))
            self.by_c.wait_recv()
            self.on.wait_recv()

        def done(self):
            self.by_y.wait_send()
            self.by_c.wait_send()
            self.on.wait_send()

    class Deal:
        def __init__(self, n):
            to_own = df.at[n, mine, own_half]
            to_other = df.at[n, mine, other_half]
            self.copies = [
                send_y(og_in.at[n, own_half], to_own),
                send_t(og_in.at[n, other_half], to_other),
                send_c(og_in.at[n, other_half], to_other),
            ]

        def finish(self):
            for copy in self.copies:
                copy.wait()

    class Weights:
        def __init__(self):
            self.group = min(parts, 16)
            self.base = batch // self.group * self.group
            self.place = lax.rem(batch, self.group)
            for copy in own_parts:
                copy.wait()
            self.fetch = [
                send_y(self.piece(self.source(k), k), self.piece(self.target(k, mine), k))
                for k in range(3)
            ]
            self.near = {}
            self.far = {}

        def source(self, k):
            return wc_in.at[0] if k == 2 else self.target(k, mine)

        def target(self, k, q):
            if k == 2:
                return wgc.at[q]
            rows = pl.ds(pl.multiple_of(lax.rem(q, 2) * cols, cols), cols)
            return gp.at[1 + q // 2, rows] if k else act.at[q // 2, rows]

        def piece(self, ref, k):
            size = (width if k == 2 else cols) // self.group
            return ref.at[pl.ds(pl.multiple_of(self.place * size, size), size)]

        def hand(self, src, k, step):
            peer = {"batch": self.base + lax.rem(self.place + step, self.group)}
            return pltpu.make_async_remote_copy(
                src_ref=src,
                dst_ref=src,
                send_sem=wsem.at[k, 0],
                recv_sem=wsem.at[k, 1],
                device_id=peer,
                device_id_type=MESH,
            )

        def hand_on(self, k):
            self.near[k] = send_c(self.source(k), self.target(k, mine))
            self.fetch[k].wait_recv()

            @pl.loop(1, self.group)
            def _(step):
                self.hand(self.piece(self.target(k, y_other), k), k, step).start()

        def across(self, k):
            size = width if k == 2 else cols
            rest = self.target(k, y_other).at[pl.ds(0, size - size // self.group)]
            self.hand(rest, k, 1).wait()
            self.far[k] = send_c(self.target(k, y_other), self.target(k, y_other))

        def finish(self, k):
            self.fetch[k].wait_send()
            self.near[k].wait()
            self.far[k].wait()

        def load_cross(self):
            copies = []
            for h in range(width // span):
                rows = pl.ds(h * span, span)
                for step in range(4):
                    q = lax.rem(mine + step, 4)
                    src = wgc.at[q, rows] if step else wc_in.at[0, rows]
                    copies.append(local(src, gp.at[h, :, col_of(q)]))
            return copies

    x_gather = []
    for n in range(lanes):
        x_copies[n].wait()
        x_gather.append(Gather(xf, n))
        if n == 0:
            par_gather = Gather(par)
            weights = Weights()

    for ref in (nacc, pacc, racc, facc, kacc, vacc):
        ref[...] = jnp.zeros(ref.shape, ref.dtype)

    lane_c = lax.broadcasted_iota(jnp.int32, (1, cols), 1)

    def head_f(h):
        return (lane_c // HEAD_DIM == h).astype(f32)

    def head_b(h):
        return head_f(h).astype(bf16)

    lane_w = lax.broadcasted_iota(jnp.int32, (1, 2 * heads * buckets), 1)

    def word_b(h):
        mask = lax.rem(lane_w, heads * buckets) // buckets == h
        return mask.astype(f32).astype(bf16)

    lane_r = lax.broadcasted_iota(jnp.int32, (1, heads * buckets), 1)

    def word_f(h):
        return (lane_r // buckets == h).astype(f32)

    flip = (
        lax.broadcasted_iota(jnp.int32, (half, half), 0)
        + lax.broadcasted_iota(jnp.int32, (half, half), 1)
        == half - 1
    )
    flip = flip.astype(f32).astype(bf16)
    slot = lax.broadcasted_iota(jnp.int32, (1, 128), 1)

    def rows_of(i):
        return pl.ds(pl.multiple_of(i * TILE, TILE), TILE)

    def own_tile(i):
        return pl.ds(pl.multiple_of(cc * half + i * TILE, TILE), TILE)

    def which_half(i):
        return lax.rem(i + cc, 2)

    def half_rows(which):
        return pl.ds(pl.multiple_of(which * half, half), half)

    def col_of(j):
        return pl.ds(pl.multiple_of(j * cols, cols), cols)

    def wide(ref, n, rows):
        return jnp.concatenate([ref[n, q, rows, :] for q in range(4)], axis=1)

    def summed(n, parity, i):
        rows = own_tile(i)
        mine_part = wide(pbuf, n, rows).astype(f32)
        return mine_part + wide(yrecv.at[parity], n, rows_of(i)).astype(f32)

    def put_wide(ref, n, rows, v):
        for q in range(4):
            ref[n, q, rows, :] = v[:, q * cols : (q + 1) * cols].astype(ref.dtype)

    def param(k):
        return jnp.concatenate([par[q, k : k + 1, :] for q in range(4)], axis=1)

    def put_slot(ref, rows, k, v):
        ref[rows, :] = jnp.where(slot == k, v, ref[rows, :])

    def get_slot(rows, k):
        return total(jnp.where(slot == k, lse[rows, :], 0.0))

    code = code_in[0]

    def pick(values):
        whole, two, four = values
        return jnp.where(code == 0, whole, jnp.where(code == 1, two, four))

    def group_of(spots, length):
        return pick((spots * 0, spots // (length // 2), spots // (length // 4)))

    def key_groups(fill, length):
        spots = lax.broadcasted_iota(jnp.int32, (1, length), 1)
        group = group_of(spots, length)
        long = pick((length, length // 2, length // 4))
        ends = spots * 0
        for g in range(fill.shape[1]):
            end = long - (fill[0, g] & (long // 2 - 1))
            ends = jnp.where(group == g, end, ends)
        return jnp.where(spots - group * long < ends, group, -1)

    def build_tables():
        keys = key_groups(fill_in, span)
        ekeys = key_groups(efill_in, espan)

        word = lax.broadcasted_iota(jnp.int32, (2 * heads * buckets, 1), 0)
        hot = (lax.rem(word, buckets) == buckets_in[...]).astype(f32).astype(bf16)

        def moves(size, shift):
            @pl.loop(0, size // TILE)
            def _(k):
                place = lax.broadcasted_iota(jnp.int32, (TILE, size), 0)
                place = place + lax.broadcasted_iota(jnp.int32, (TILE, size), 1)
                place = place + (2 * size + k * TILE - shift)
                smask[rows_of(k), :size] = ((place & (size - 1)) == 0).astype(f32).astype(bf16)

        for table, turned, size, shift in (
            (oh_first, oht_first, half, 0),
            (oh_second, oht_second, span, half),
        ):
            moves(size, shift)
            table[...] = dot(hot[:, :size], smask[:size, :size]).astype(bf16)
            moves(size, shift + half - 1)
            flat = hot[: heads * buckets, :size]
            turned[...] = dot_nt(smask[:size, :size], flat).astype(bf16)

        @pl.loop(0, span // TILE)
        def _(i):
            rows = rows_of(i)
            spots = lax.broadcasted_iota(jnp.int32, (TILE, 1), 0) + i * TILE
            group = group_of(spots, span)
            allowed = (group == keys) & (spots >= lax.broadcasted_iota(jnp.int32, (1, span), 1))
            smask[rows, :] = jnp.where(allowed, 0.0, neg_big).astype(bf16)
            cmask[rows, :] = jnp.where(group == ekeys, 0.0, neg_big).astype(bf16)

    build_tables()

    wi_copy = local(wi_in, wi.at[0])
    wo_copy = local(wo_in, wo.at[0])

    class Reduce:
        def __init__(self, n, parity):
            self.n = n
            self.parity = parity
            self.first = send_c(pbuf.at[n, :, other_half], crecv.at[n])

        def middle(self):
            n = self.n
            self.first.wait_recv()

            @pl.loop(0, tiles)
            def _(i):
                rows = own_tile(i)
                for q in range(4):
                    both = pbuf[n, q, rows, :].astype(f32)
                    both = both + crecv[n, q, rows_of(i), :].astype(f32)
                    pbuf[n, q, rows, :] = both.astype(bf16)

            self.second = send_y(pbuf.at[n, :, own_half], yrecv.at[self.parity, n])

        def finish(self):
            self.first.wait_send()
            self.second.wait()

    class Swap:
        def __init__(self, ref, n, parity):
            place = yrecv.at[parity, n, mine]
            self.copies = [
                send_y(ref.at[n, own_half], place),
                send_t(ref.at[n, other_half], place),
                send_c(ref.at[n, other_half], place),
            ]

        def middle(self):
            pass

        def finish(self):
            for copy in self.copies:
                copy.wait()

    def heads_of(n, parity):
        return jnp.concatenate([yrecv[parity, n, q] for q in range(4)], axis=1)

    def project_heads(n, parity, k):
        @pl.loop(0, 4)
        def _(j):
            rows = heads_of(n, parity)
            at = col_of(j)
            low, high = (gp[1, :, at], gp[2, :, at]) if k else (act[0, :, at], act[1, :, at])
            part = dot(rows[:, : 2 * cols], low) + dot(rows[:, 2 * cols :], high)
            pbuf[n, j, own_half, :] = part.astype(bf16)

    def project_back(n, parity):
        @pl.loop(0, 4)
        def _(j):
            rows = heads_of(n, parity)
            at = pl.ds(pl.multiple_of(lax.rem(j, 2) * cols, cols), cols)
            pbuf[n, j, own_half, :] = dot_nt(rows, gp[j // 2, at, :]).astype(bf16)

    class Scatter:
        def __init__(self, part, from_c, from_y):
            self.part, self.from_c, self.from_y = part, from_c, from_y
            self.first = [
                send_c(part.at[2 * k + 1 - cc, pl.ds(r * half, half)], from_c.at[2 * k + r])
                for k in range(2)
                for r in range(2)
            ]

        def middle(self):
            for copy in self.first:
                copy.wait_recv()
            part = self.part
            for k in range(2):
                for r in range(2):

                    @pl.loop(0, tiles)
                    def _(i, k=k, r=r):
                        rows = rows_of(i + r * tiles)
                        both = part[2 * k + cc, rows, :].astype(f32)
                        both = both + self.from_c[2 * k + r, rows_of(i), :].astype(f32)
                        part[2 * k + cc, rows, :] = both.astype(bf16)

            self.second = [
                send_y(part.at[y_other, pl.ds(r * half, half)], self.from_y.at[r]) for r in range(2)
            ]

        def finish(self, store):
            for copy in self.second:
                copy.wait()
            for copy in self.first:
                copy.wait_send()
            for r in range(2):

                @pl.loop(0, tiles)
                def _(i, r=r):
                    rows = rows_of(i + r * tiles)
                    store(
                        rows,
                        self.part[mine, rows, :].astype(f32)
                        + self.from_y[r, rows_of(i), :].astype(f32),
                    )

    class Share:
        def __init__(self, grad, pair, far, out, at):
            self.grad, self.pair, self.far, self.out, self.at = grad, pair, far, out, at
            self.block = width // parts

            @pl.loop(0, ring)
            def _(z):
                self.near(self.rows(z, 1 - at_pair), pair.at[z]).start()

        def rows(self, z, x):
            start = pl.multiple_of((z * 2 + x) * self.block, self.block)
            return self.grad.at[:, pl.ds(start, self.block), :]

        def near(self, src, dst):
            return pltpu.make_async_remote_copy(
                src_ref=src,
                dst_ref=dst,
                send_sem=bsem.at[self.at, 0],
                recv_sem=bsem.at[self.at, 1],
                device_id=x_peer,
                device_id_type=MESH,
            )

        def away(self, src, dst, step):
            return pltpu.make_async_remote_copy(
                src_ref=src,
                dst_ref=dst,
                send_sem=bsem.at[self.at, 2],
                recv_sem=bsem.at[self.at, 3],
                device_id=z_peer(step),
                device_id_type=MESH,
            )

        def middle(self):
            self.near(self.pair, self.pair).wait()

            @pl.loop(0, ring)
            def _(z):
                for m in range(self.grad.shape[0]):
                    start = pl.multiple_of((z * 2 + at_pair) * self.block, self.block)
                    own = self.grad[m, pl.ds(start, self.block), :].astype(f32)
                    self.pair[z, m] = (own + self.pair[z, m].astype(f32)).astype(bf16)

            @pl.loop(1, ring)
            def _(step):
                self.away(
                    self.pair.at[lax.rem(at_ring + step, ring)], self.far.at[step - 1], step
                ).start()

        def last(self):
            self.away(self.far, self.far, 1).wait()
            self.out[...] = self.pair[at_ring].astype(f32)

            @pl.loop(1, ring)
            def _(step):
                self.out[...] += self.far[step - 1].astype(f32)

    def norm_rows(resid):
        mean = total(resid) * (1.0 / width)
        centred = resid - mean
        var = total(centred * centred) * (1.0 / width)
        rs = lax.rsqrt(var + norm_eps)
        return centred * rs, rs

    def norm_grad(grad, xh, rs, gain, k):
        q = grad * gain
        m1 = total(q) * (1.0 / width)
        m2 = total(q * xh) * (1.0 / width)
        back = rs * (q - m1 - xh * m2)
        nacc[k] += eight(grad * xh)
        nacc[3 + k] += eight(grad)
        nacc[6 + k] += eight(back)
        return back

    at_scale = 2 * lanes * heads

    def give(ref, n):
        return send_c(ref.at[n, :, own_half], ref.at[n, :, own_half])

    def norm_first(n):
        project_heads(n, 1, 0)

        @pl.loop(0, tiles)
        def _(i):
            rows = own_tile(i)
            resid = wide(xf, n, rows).astype(f32) + wide(pbuf, n, rows).astype(f32) + param(0)
            xh, rs = norm_rows(resid)
            put_slot(lse, rows, at_scale + n, rs)
            put_wide(f1, n, rows, xh * param(3) + param(6))

        return give(f1, n)

    def norm_second(n):
        project_heads(n, 0, 1)

        @pl.loop(0, tiles)
        def _(i):
            rows = own_tile(i)
            resid = wide(f1, n, rows).astype(f32) + wide(pbuf, n, rows).astype(f32) + param(1)
            xh, rs = norm_rows(resid)
            put_slot(lse, rows, at_scale + lanes + n, rs)
            put_wide(f2, n, rows, xh * param(4) + param(7))

        return give(f2, n)

    out_copies = []

    def norm_third(n):
        @pl.loop(0, tiles)
        def _(i):
            rows = own_tile(i)
            resid = wide(f2, n, rows).astype(f32) + summed(n, 1, i) + param(2)
            xh, rs = norm_rows(resid)
            out = xh * param(5) + param(8)
            put_wide(pbuf, n, rows, out)
            out_ref[n, rows, :] = pbuf[n, mine, rows, :]
            lout[n, rows_of(i), :] = pbuf[n, c_other, rows, :]
            grad = wide(df, n, rows).astype(f32)
            put_wide(df, n, rows, norm_grad(grad, xh, rs, param(5), 2))

        out_copies.append(send_c(lout.at[n], lrecv.at[n]))
        return give(df, n)

    def norm_second_back(n):
        @pl.loop(0, tiles)
        def _(i):
            rows = own_tile(i)
            grad = wide(df, n, rows).astype(f32) + summed(n, 0, i)
            gain = param(4)
            xh = (wide(f2, n, rows).astype(f32) - param(7)) * (1.0 / gain)
            rs = get_slot(rows, at_scale + lanes + n)
            put_wide(df, n, rows, norm_grad(grad, xh, rs, gain, 1))

    def norm_first_back(n):
        project_back(n, 1)

        @pl.loop(0, tiles)
        def _(i):
            rows = own_tile(i)
            grad = wide(df, n, rows).astype(f32) + wide(pbuf, n, rows).astype(f32)
            gain = param(3)
            xh = (wide(f1, n, rows).astype(f32) - param(6)) * (1.0 / gain)
            rs = get_slot(rows, at_scale + n)
            put_wide(df, n, rows, norm_grad(grad, xh, rs, gain, 0))

    def halves(got, body):
        @pl.loop(0, 2)
        def _(i):
            if got is not None:

                @pl.when(i == 1)
                def _():
                    got.wait()

            which = which_half(i)
            body(which, half_rows(which))

    def keep_own(parity, n, which, v):
        @pl.when(which == cc)
        def _():
            yrecv[parity, n, mine] = v

    def each_head(body):
        pl.loop(0, heads, unroll=HEAD_UNROLL)(body)

    def self_score(n, which, rows, h, diag):
        reach = (which + 1) * half
        qh = qb[n, rows, :] * head_b(h)
        table = oh_second if which else oh_first
        spread = dot(relb[n, rows, :] * word_b(h), table[...])
        bias = pltpu.roll(spread, 0, 1, stride=1, stride_axis=0)
        s = dot_nt(qh, kb[0, :reach, :]) + smask[rows, :reach].astype(f32)
        if n > 0:
            s = jnp.where(diag, total(qh.astype(f32) * kb[n, rows, :].astype(f32)), s)
        return qh, s + bias

    def diagonal(which):
        r = lax.broadcasted_iota(jnp.int32, (half, (which + 1) * half), 0)
        s = lax.broadcasted_iota(jnp.int32, (half, (which + 1) * half), 1)
        return s == r + which * half

    def both_halves(body):
        for which in range(2):
            body(which, pl.ds(which * half, half), (which + 1) * half)

    def project_rows(n):
        def body(which, rows):
            x = wide(xf, n, rows)
            q = (dot(x, ws[0]) + pbias[0:1, :]).astype(bf16)
            qb[n, rows, :] = (q.astype(f32) * 0.125).astype(bf16)
            kb[n, rows, :] = dot(x, ws[1]).astype(bf16)
            vb[n, rows, :] = (dot(x, ws[2]) + pbias[1:2, :]).astype(bf16)
            rel = dot(x, wr[0]) + rbias[...]
            high = rel.astype(bf16)
            relb[n, rows, : heads * buckets] = high
            relb[n, rows, heads * buckets :] = (rel - high.astype(f32)).astype(bf16)

        halves(None, body)

    def self_forward(n):
        project_rows(n)

        def body(which, rows, reach):
            macc[...] = jnp.zeros(macc.shape, f32)

            @each_head
            def _(h):
                diag = diagonal(which) if n > 0 else None
                qh, s = self_score(n, which, rows, h, diag)
                top = jnp.max(s, axis=1, keepdims=True)
                w = jnp.exp(s - top)
                sums = total(w)
                inverse = 1.0 / sums
                put_slot(lse, rows, n * heads + h, top + jnp.log(sums))
                if n > 0:
                    own = total(jnp.where(diag, w, 0.0)) * inverse
                    w = jnp.where(diag, 0.0, w)
                part = dot(w.astype(bf16), vb[0, :reach, :]) * inverse
                if n > 0:
                    part = part + own.astype(bf16).astype(f32) * vb[n, rows, :].astype(f32)
                macc[...] += part * head_f(h)

            low = macc[...].astype(bf16)
            att[n, rows, :] = low
            keep_own(1, n, which, low)

        both_halves(body)

    def encoder_rows():
        @pl.loop(0, espan // TILE)
        def _(i):
            rows = rows_of(i)
            e = wide(ef, 0, rows)
            ck[rows, :] = dot(e, wc[1]).astype(bf16)
            cv[rows, :] = (dot(e, wc[2]) + pbias[3:4, :]).astype(bf16)

    def cross_forward(n, got):
        def body(which, rows):
            q = (dot(wide(f1, n, rows), wc[0]) + pbias[2:3, :]).astype(bf16)
            cq[n, rows, :] = (q.astype(f32) * 0.125).astype(bf16)
            macc[...] = jnp.zeros(macc.shape, f32)

            @each_head
            def _(h):
                s = dot_nt(cq[n, rows, :] * head_b(h), ck[...]) + cmask[rows, :].astype(f32)
                top = jnp.max(s, axis=1, keepdims=True)
                w = jnp.exp(s - top)
                sums = total(w)
                put_slot(lse, rows, (lanes + n) * heads + h, top + jnp.log(sums))
                macc[...] += dot(w.astype(bf16), cv[...]) * (1.0 / sums) * head_f(h)

            low = macc[...].astype(bf16)
            catt[n, rows, :] = low
            keep_own(0, n, which, low)

        halves(got, body)

    def ffn_forward(n, got):
        def body(which, rows):
            @pl.loop(0, hidden // cols)
            def _(j):
                at = col_of(j)
                pre = dot(wide(f2, n, rows), wi[0, :, at]) + fbias[:, at]
                value, slope = gelu_both(pre)
                act[n, rows, at] = value.astype(bf16)
                gp[n, rows, at] = slope.astype(bf16)

            @pl.loop(0, width // cols)
            def _(j):
                pbuf[n, j, rows, :] = dot(act[n, rows, :], wo[0, :, col_of(j)]).astype(bf16)

        halves(got, body)

    def ffn_backward(n, got):
        def body(which, rows):
            @pl.loop(0, hidden // cols)
            def _(j):
                at = col_of(j)
                grad = dot_nt(wide(df, n, rows), wo[0, at, :]) * gp[n, rows, at].astype(f32)
                facc[:, at] += eight(grad)
                gp[n, rows, at] = grad.astype(bf16)

            @pl.loop(0, width // cols)
            def _(j):
                pbuf[n, j, rows, :] = dot_nt(gp[n, rows, :], wi[0, col_of(j), :]).astype(bf16)

        halves(got, body)

    def spot(k, h, size, wide=None):
        row = pl.ds(pl.multiple_of(lax.rem(h, 2) * half, half), half)
        col = pl.ds(pl.multiple_of(k * span + (h // 2) * size, size), wide or size)
        return row, col

    def stacked(n, k, size, wide=None):
        parts = [act[(n,) + spot(k, h, size, wide)] for h in range(heads)]
        return jnp.concatenate(parts, axis=0)

    def keep_head(h, p, ds, dh, qh, reach):
        act[(0,) + spot(0, h, span, reach)] = p
        act[(1,) + spot(0, h, span, reach)] = ds
        act[(2,) + spot(0, h, cols)] = dh
        act[(2,) + spot(1, h, cols)] = qh

    def add_heads(reach):
        vacc[:reach, :] += dot_tn(stacked(0, 0, span, reach), stacked(2, 0, cols))
        kacc[:reach, :] += dot_tn(stacked(1, 0, span, reach), stacked(2, 1, cols))

    def cross_backward(n, got):
        def body(which, rows):
            da = dot_nt(wide(df, n, rows), wa[1]).astype(bf16)
            macc[...] = jnp.zeros(macc.shape, f32)

            @each_head
            def _(h):
                qh = cq[n, rows, :] * head_b(h)
                dh = da * head_b(h)
                s = dot_nt(qh, ck[...]) + cmask[rows, :].astype(f32)
                p = jnp.exp(s - get_slot(rows, (lanes + n) * heads + h))
                dp = dot_nt(dh, cv[...])
                ds = (p * (dp - total(p * dp))).astype(bf16)
                keep_head(h, p.astype(bf16), ds, dh, qh, espan)
                macc[...] += dot(ds, ck[...]) * head_f(h)

            add_heads(espan)
            dq = macc[...] * 0.125
            pacc[2] += eight(dq)
            low = dq.astype(bf16)
            cq[n, rows, :] = low
            keep_own(1, n, which, low)

        halves(got, body)

    def encoder_backward():
        pacc[3] += eight(vacc[...])

        @pl.loop(0, espan // TILE)
        def _(i):
            rows = rows_of(i)
            dk = kacc[rows, :].astype(bf16)
            dv = vacc[rows, :].astype(bf16)
            ck[rows, :] = dk
            cv[rows, :] = dv
            part = dot_nt(dk, wc[1]) + dot_nt(dv, wc[2])
            for q in range(4):
                f2[0, q, rows, :] = part[:, q * cols : (q + 1) * cols].astype(bf16)

    def self_backward(n):
        def body(which, rows, reach):
            da = dot_nt(wide(df, n, rows), wa[0]).astype(bf16)
            macc[...] = jnp.zeros(macc.shape, f32)
            dracc[...] = jnp.zeros(dracc.shape, f32)
            if n > 0:
                dkacc[...] = jnp.zeros(dkacc.shape, f32)
                dvacc[...] = jnp.zeros(dvacc.shape, f32)

            @each_head
            def _(h):
                diag = diagonal(which) if n > 0 else None
                qh, s = self_score(n, which, rows, h, diag)
                p = jnp.exp(s - get_slot(rows, n * heads + h))
                dh = da * head_b(h)
                dp = dot_nt(dh, vb[0, :reach, :])
                if n > 0:
                    vn = vb[n, rows, :].astype(f32)
                    dp = jnp.where(diag, total(dh.astype(f32) * vn), dp)
                ds = p * (dp - total(p * dp))
                turned = pltpu.roll(dot(flip, ds.astype(bf16)), 0, 1, stride=1, stride_axis=0)
                dracc[...] += dot(turned.astype(bf16), (oht_second if which else oht_first)[...]) * word_f(h)
                if n > 0:
                    own_p = total(jnp.where(diag, p, 0.0)).astype(bf16).astype(f32)
                    own_s = total(jnp.where(diag, ds, 0.0)).astype(bf16).astype(f32)
                    p = jnp.where(diag, 0.0, p)
                    ds = jnp.where(diag, 0.0, ds)
                    dkacc[...] += own_s * qh.astype(f32)
                    dvacc[...] += own_p * dh.astype(f32)
                low = ds.astype(bf16)
                keep_head(h, p.astype(bf16), low, dh, qh, reach)
                part = dot(low, kb[0, :reach, :])
                if n > 0:
                    part = part + own_s * kb[n, rows, :].astype(f32)
                macc[...] += part * head_f(h)

            add_heads(reach)
            dq = macc[...] * 0.125
            drel = dracc[...]
            pacc[0] += eight(dq)
            racc[...] += eight(drel)
            qb[n, rows, :] = dq.astype(bf16)
            relb[n, rows, : heads * buckets] = dot(flip, drel.astype(bf16)).astype(bf16)
            if n > 0:
                pacc[1] += eight(dvacc[...])
                kb[n, rows, :] = dkacc[...].astype(bf16)
                vb[n, rows, :] = dvacc[...].astype(bf16)

        both_halves(body)
        if n == 0:
            pacc[1] += eight(vacc[...])
            kb[0] = kacc[...].astype(bf16)
            vb[0] = vacc[...].astype(bf16)

        @pl.loop(0, width // cols)
        def _(j):
            at = col_of(j)
            part = dot_nt(qb[n], ws[0, at, :]) + dot_nt(kb[n], ws[1, at, :])
            part = part + dot_nt(vb[n], ws[2, at, :])
            part = part + dot_nt(relb[n, :, : heads * buckets], wr[0, at, :])
            pbuf[n, j] = part.astype(bf16)

    def weight_grad(rows_ref, pieces, lane_count):
        @pl.loop(0, 4)
        def _(j):
            left = jnp.concatenate([rows_ref[n, j] for n in range(lane_count)], axis=0)
            for load, target, size in pieces:
                for start in range(0, size, cols):
                    step = min(cols, size - start)
                    right = jnp.concatenate(
                        [load(n, start, step) for n in range(lane_count)], axis=0
                    )
                    target[col_of(j), start : start + step] = dot_tn(left, right).astype(bf16)

    def of(ref):
        return lambda n, start, step: ref[n, :, start : start + step]

    words = heads * buckets

    order = list(range(lanes))
    late = order[1:] + order[:1]
    ws_copy.wait()
    wr_copy.wait()
    wa_copy.wait()
    reduces = {}
    gots = {}

    def after(n, exchange, following):
        if following is not None:
            following()
        exchange.middle()
        reduces[n] = exchange

    def ready(n, norm):
        def go():
            reduces[n].finish()
            gots[n] = norm(n)

        return go

    deals = []
    for n in order:
        x_gather[n].finish()
        if n == 0:
            par_gather.finish()
            weights.hand_on(0)
        self_forward(n)
        if n == 0:
            e_copy.wait()
            e_gather = Gather(ef, 0)
        after(n, Swap(att, n, 1), None)
        if n == 0:
            weights.hand_on(1)
        if n == 1:
            weights.across(0)
    weights.finish(0)
    wc_copy.wait()
    e_gather.finish()
    encoder_rows()
    ready(order[0], norm_first)()

    def second_of(*those):
        def go():
            if those[0] == order[0]:
                weights.finish(1)
            for n in those:
                ready(n, norm_second)()

        return go

    for k, n in enumerate(order):
        cross_forward(n, gots[n])
        og_copies[n].wait()
        following = order[k + 1] if k + 1 < lanes else None
        norm = ready(following, norm_first) if following else second_of(order[0])
        after(n, Swap(catt, n, 0), norm)
        deals.append(Deal(n))
        if k == 0:
            weights.across(1)
            weights.hand_on(2)
    wi_copy.wait()
    wo_copy.wait()

    def third_of(n):
        def go():
            deals[n].finish()
            ready(n, norm_third)()

        return go

    for k, n in enumerate(order):
        ffn_forward(n, gots[n])
        if k == 0:
            norm = second_of(*order[1:])
        else:
            norm = third_of(order[0]) if k + 1 == lanes else None
        after(n, Reduce(n, 1), norm)
    for k, n in enumerate(order):
        ffn_backward(n, gots[n])
        after(n, Reduce(n, 0), third_of(order[k + 1]) if k + 1 < lanes else None)
        if k == 0:
            weights.across(2)
    weight_grad(df, [(of(act), wo.at[0], hidden)], lanes)
    share_o = Share(wo, xo, zo, go_ref, 0)
    pl.semaphore_signal(free.at[0], inc=1, device_id=c_peer, device_id_type=MESH)
    waited = set()

    def back_of(n, norm, k):
        def go():
            reduces[n].finish()
            norm(n)
            if k not in waited:
                waited.add(k)
                pl.semaphore_wait(free.at[k], 1)
            gots[n] = give(df, n)

        return go

    back_of(late[0], norm_second_back, 0)()
    weight_grad(f2, [(of(gp), wi.at[0], hidden)], lanes)
    share_i = Share(wi, xi, zi, gi_ref, 1)
    weights.finish(2)
    loads = weights.load_cross()
    for k, n in enumerate(late):
        cross_backward(n, gots[n])
        after(n, Swap(cq, n, 1), back_of(late[k + 1], norm_second_back, 0) if k + 1 < lanes else None)
        if k == 1:
            share_o.middle()
    weight_grad(df, [(of(catt), ga1.at[0], cols)], lanes)
    share_a1 = Share(ga1, xa1, za1, ga1_ref, 2)
    pl.semaphore_signal(free.at[1], inc=1, device_id=c_peer, device_id_type=MESH)
    encoder_backward()
    e_scatter = Scatter(f2.at[0], ecrecv, eyrecv)
    for copy in loads:
        copy.wait()
    back_of(late[0], norm_first_back, 1)()
    e_scatter.middle()
    weight_grad(f1, [(of(cq), wc.at[0], cols)], lanes)
    weight_grad(
        ef,
        [
            (lambda n, a, b: ck[:, a : a + b], wc.at[1], cols),
            (lambda n, a, b: cv[:, a : a + b], wc.at[2], cols),
        ],
        1,
    )
    share_c = Share(wc, xc, zc, gc_ref, 4)
    share_i.middle()
    kacc[...] = jnp.zeros(kacc.shape, f32)
    vacc[...] = jnp.zeros(vacc.shape, f32)
    scatters = {}
    for k, n in enumerate(late):
        gots[n].wait()
        if k + 1 == lanes:
            weight_grad(df, [(of(att), ga0.at[0], cols)], lanes)
            share_a0 = Share(ga0, xa0, za0, ga0_ref, 3)
        self_backward(n)
        scatters[n] = Scatter(pbuf.at[n], crecv.at[n], yrecv.at[0, n])
        if k + 1 < lanes:
            back_of(late[k + 1], norm_first_back, 1)()
            scatters[n].middle()
        if k == 0:

            def store_enc(rows, v):
                genc_ref[rows, :] = v

            e_scatter.finish(store_enc)
            share_o.last()
            share_a1.middle()
        if k == 1:
            share_i.last()
            share_c.middle()
    weight_grad(
        xf,
        [
            (of(vb), ws.at[2], cols),
            (of(kb), ws.at[1], cols),
            (of(qb), ws.at[0], cols),
            (of(relb), wr.at[0], words),
        ],
        lanes,
    )
    share_v = Share(ws.at[pl.ds(2, 1)], xv, zv, gs_ref.at[pl.ds(2, 1)], 6)
    share_k = Share(ws.at[pl.ds(1, 1)], xk, zk, gs_ref.at[pl.ds(1, 1)], 8)
    share_q = Share(ws.at[pl.ds(0, 1)], xq, zq, gs_ref.at[pl.ds(0, 1)], 9)
    share_r = Share(wr, xr, zr, gr_ref, 5)
    scatters[late[-1]].middle()
    share_a0.middle()
    for n in order:
        out_copies[n].wait()

        @pl.loop(0, tiles)
        def _(i, n=n):
            rows = pl.ds(pl.multiple_of((1 - cc) * half + i * TILE, TILE), TILE)
            out_ref[n, rows, :] = lrecv[n, rows_of(i), :]

    def vec_copy(src, dst, k, peer):
        return pltpu.make_async_remote_copy(
            src_ref=src,
            dst_ref=dst,
            send_sem=bsem.at[7, k],
            recv_sem=bsem.at[7, k + 1],
            device_id=peer,
            device_id_type=MESH,
        )

    for k in range(9):
        nsum[k : k + 1, :] = jnp.sum(nacc[k], axis=0, keepdims=True)
    norm_sums = send_c(nsum, nrecv)
    norm_sums.wait()
    for k in range(9):
        row = nsum[k : k + 1, :] + nrecv[k : k + 1, :]
        for q in range(4):
            vquarter[q, k : k + 1, :] = row[:, q * cols : (q + 1) * cols]
    vec[...] = jnp.zeros(vec.shape, f32)
    vec[0:9, :] = vquarter[mine, 0:9, :]
    for k in range(4):
        vec[9 + k : 10 + k, :] = jnp.sum(pacc[k], axis=0, keepdims=True)
    vec[13:14, :words] = jnp.sum(racc[...], axis=0, keepdims=True)
    row = jnp.sum(facc[...], axis=0, keepdims=True)
    for k in range(hidden // cols):
        vec[14 + k : 15 + k, :] = row[:, k * cols : (k + 1) * cols]
    vec_pair = vec_copy(vec, vrecv.at[0], 0, x_peer)
    vec_pair.start()
    share_v.middle()
    for n in late:

        def store_in(rows, v, n=n):
            gin_ref[n, rows, :] = df[n, mine, rows, :].astype(f32) + v

        scatters[n].finish(store_in)
    share_a1.last()
    share_c.last()
    share_k.middle()
    share_a0.last()
    share_q.middle()
    share_r.middle()
    vec_pair.wait()
    vec[...] += vrecv[0]

    @pl.loop(1, ring)
    def _(step):
        vec_copy(vec, vrecv.at[step], 2, z_peer(step)).start()

    share_v.last()
    share_k.last()
    share_q.last()
    share_r.last()
    every_vec = vrecv.at[pl.ds(1, ring - 1)]
    vec_copy(every_vec, every_vec, 2, z_peer(1)).wait()
    vec_ref[...] = vec[...]

    @pl.loop(1, ring)
    def _(step):
        vec_ref[...] += vrecv[step]

    for item in x_gather + [par_gather, e_gather]:
        item.done()


def per_device(
    layer_in,
    encoder_states,
    w_self,
    w_rel,
    w_cross,
    w_attn_out,
    w_in,
    w_out,
    proj_bias,
    rel_bias,
    ffn_in_bias,
    out_bias,
    norm_gain,
    norm_bias,
    rel_buckets,
    slot_log,
    tgt_fill,
    enc_fill,
    out_grad,
):
    lanes, span, cols = layer_in.shape
    espan = encoder_states.shape[0]
    width = w_self.shape[1]
    hidden = w_in.shape[1]
    heads = cols // HEAD_DIM
    words = w_rel.shape[1]
    buckets = words // heads
    half = span // 2
    parts = lax.axis_size("batch")
    ring = parts // 2
    block = width // parts
    shapes = [(1, cols)] * 3 + [(1, words), (3, cols), (1, cols), (1, cols), (1, hidden), (1, hidden)]
    vec_rows = -(-(14 + hidden // cols) // 8) * 8
    dims = (lanes, span, espan, cols, width, hidden, heads, buckets, parts)
    any_spec = pl.BlockSpec(memory_space=pl.ANY)
    vmem = pl.BlockSpec(memory_space=pltpu.VMEM)
    V = pltpu.VMEM
    smem = pl.BlockSpec(memory_space=pltpu.SMEM)
    scratch = [
        V((span, span), bf16),
        V((span, espan), bf16),
        V((2 * words, half), bf16),
        V((2 * words, span), bf16),
        V((half, words), bf16),
        V((span, words), bf16),
        V((4, 16, cols), f32),
        V((lanes, 4, span, cols), bf16),
        V((1, 4, espan, cols), bf16),
        V((lanes, 4, span, cols), bf16),
        V((lanes, 4, span, cols), bf16),
        V((lanes, 4, span, cols), bf16),
        V((lanes, span, hidden), bf16),
        V((lanes, span, hidden), bf16),
        V((lanes, span, cols), bf16),
        V((lanes, span, cols), bf16),
        V((lanes, span, cols), bf16),
        V((lanes, span, 2 * words), bf16),
        V((lanes, span, cols), bf16),
        V((lanes, span, cols), bf16),
        V((lanes, span, cols), bf16),
        V((espan, cols), bf16),
        V((espan, cols), bf16),
        V((span, 128), f32),
        V(w_self.shape, bf16),
        V((1,) + w_rel.shape, bf16),
        V(w_cross.shape, bf16),
        V(w_attn_out.shape, bf16),
        V((1,) + w_in.shape, bf16),
        V((1,) + w_out.shape, bf16),
        V((lanes, 4, span, cols), bf16),
        V((lanes, 4, half, cols), bf16),
        V((2, lanes, 4, half, cols), bf16),
        V((lanes, half, cols), bf16),
        V((lanes, half, cols), bf16),
        V((half, cols), f32),
        V((1, width, cols), bf16),
        V((1, width, cols), bf16),
        V((4, espan // 2, cols), bf16),
        V((2, espan // 2, cols), bf16),
        V((span, cols), f32),
        V((span, cols), f32),
        V((half, words), f32),
        V((half, cols), f32),
        V((half, cols), f32),
        V((9, 8, width), f32),
        V((4, 8, cols), f32),
        V((8, words), f32),
        V((8, hidden), f32),
        V((vec_rows, cols), f32),
        V((ring, vec_rows, cols), f32),
        V((4, 16, cols), f32),
        V((16, width), f32),
        V((16, width), f32),
        *[V((ring, m, block, w), bf16) for m, w in shapes],
        *[V((ring - 1, m, block, w), bf16) for m, w in shapes],
        pltpu.SemaphoreType.DMA((64,)),
        pltpu.SemaphoreType.DMA((64,)),
        pltpu.SemaphoreType.DMA((64,)),
        pltpu.SemaphoreType.DMA((128,)),
        pltpu.SemaphoreType.DMA((128,)),
        pltpu.SemaphoreType.DMA((10, 4)),
        pltpu.SemaphoreType.DMA((2, 16)),
        pltpu.SemaphoreType.DMA((3, 2)),
        pltpu.SemaphoreType.REGULAR((2,)),
    ]
    result, g_in, g_enc, vec, g_self, g_rel, g_cross, g_att0, g_att1, g_win, g_wout, _ = pl.pallas_call(
        functools.partial(layer_kernel, dims),
        out_shape=(
            jax.ShapeDtypeStruct((lanes, span, cols), bf16),
            jax.ShapeDtypeStruct((lanes, span, cols), f32),
            jax.ShapeDtypeStruct((espan, cols), f32),
            jax.ShapeDtypeStruct((vec_rows, cols), f32),
            jax.ShapeDtypeStruct((3, block, cols), f32),
            *[jax.ShapeDtypeStruct((m, block, w), f32) for m, w in shapes[3:]],
            jax.ShapeDtypeStruct((4, width, cols), bf16),
        ),
        in_specs=[any_spec] * 3 + [vmem] * 3 + [any_spec] * 6 + [vmem] * 4 + [smem] * 3,
        out_specs=(vmem,) * 11 + (any_spec,),
        scratch_shapes=scratch,
        compiler_params=pltpu.CompilerParams(
            collective_id=0, has_side_effects=True, vmem_limit_bytes=64 * 2**20
        ),
    )(
        layer_in,
        encoder_states,
        out_grad,
        out_bias,
        norm_gain,
        norm_bias,
        w_self,
        w_rel,
        w_cross,
        w_attn_out,
        w_in,
        w_out,
        proj_bias,
        rel_bias[None],
        ffn_in_bias[None],
        rel_buckets[None],
        slot_log,
        tgt_fill,
        enc_fill,
    )
    each = cols // parts
    own = lax.axis_index("batch")
    rest = lax.dynamic_slice_in_dim(vec[:13], own * each, each, axis=1)
    rel_grad = lax.dynamic_slice_in_dim(vec[13, :words], own * (words // parts), words // parts)
    ffn_grad = vec[14 : 14 + hidden // cols].reshape(hidden)
    ffn_grad = lax.dynamic_slice_in_dim(ffn_grad, own * (hidden // parts), hidden // parts)
    return (
        result,
        g_in,
        g_enc,
        g_self,
        g_rel[0],
        g_cross,
        jnp.stack([g_att0[0].T, g_att1[0].T]),
        g_win[0],
        g_wout[0].T,
        rest[9:13],
        rel_grad,
        ffn_grad,
        rest[6:9],
        rest[0:3],
        rest[3:6],
    )


def solution(mesh):
    return jax.shard_map(
        per_device,
        mesh=mesh,
        in_specs=(
            P(None, "batch", "tensor"),
            P("batch", "tensor"),
            P(None, None, "tensor"),
            P(None, "tensor"),
            P(None, None, "tensor"),
            P(None, "tensor", None),
            P(None, "tensor"),
            P("tensor", None),
            P(None, "tensor"),
            P("tensor"),
            P("tensor"),
            P(None, "tensor"),
            P(None, "tensor"),
            P(None, "tensor"),
            P(),
            P("batch"),
            P("batch", None),
            P("batch", None),
            P(None, "batch", "tensor"),
        ),
        out_specs=(
            P(None, "batch", "tensor"),
            P(None, "batch", "tensor"),
            P("batch", "tensor"),
            P(None, "batch", "tensor"),
            P("batch", "tensor"),
            P(None, "batch", "tensor"),
            P(None, "tensor", "batch"),
            P("batch", "tensor"),
            P("tensor", "batch"),
            P(None, ("tensor", "batch")),
            P(("tensor", "batch")),
            P(("tensor", "batch")),
            P(None, ("tensor", "batch")),
            P(None, ("tensor", "batch")),
            P(None, ("tensor", "batch")),
        ),
        check_vma=False,
    )
```

```python
import functools

import jax
import jax.numpy as jnp
from jax import lax
from jax.experimental import pallas as pl
from jax.experimental.pallas import tpu as pltpu
from jax.sharding import PartitionSpec as P

HEAD_DIM = 64
norm_eps = 1e-05
neg_big = -1e30
MESH = pl.DeviceIdType.MESH
f32 = jnp.float32
bf16 = jnp.bfloat16
TILE = 128
HEAD_UNROLL = 2


def dot(a, b):
    return jnp.dot(a, b, preferred_element_type=f32)


def dot_nt(a, b):
    return lax.dot_general(a, b, (((1,), (1,)), ((), ())), preferred_element_type=f32)


def dot_tn(a, b):
    return lax.dot_general(a, b, (((0,), (0,)), ((), ())), preferred_element_type=f32)


def total(v):
    return jnp.sum(v, axis=1, keepdims=True)


def eight(v):
    return jnp.sum(v.reshape(v.shape[0] // 8, 8, v.shape[1]), axis=0)


def gelu_both(v):
    half = 0.5 * (1.0 + lax.erf(v * (0.5**0.5)))
    bell = jnp.exp(-0.5 * v * v) * 0.3989422804014327
    return v * half, half + v * bell


def layer_kernel(
    dims,
    x_in,
    e_in,
    og_in,
    ob_in,
    ng_in,
    nb_in,
    ws_in,
    wr_in,
    wc_in,
    wa_in,
    wi_in,
    wo_in,
    pbias,
    rbias,
    fbias,
    buckets_in,
    code_in,
    fill_in,
    efill_in,
    out_ref,
    gin_ref,
    genc_ref,
    vec_ref,
    gs_ref,
    gr_ref,
    gc_ref,
    ga0_ref,
    ga1_ref,
    gi_ref,
    go_ref,
    wgc,
    pstore,
    smask,
    cmask,
    oh_first,
    oh_second,
    oht_first,
    oht_second,
    par,
    xf,
    ef,
    df,
    f1,
    f2,
    act,
    gp,
    qb,
    kb,
    vb,
    relb,
    att,
    catt,
    cq,
    ck,
    cv,
    lse,
    ws,
    wr,
    wc,
    wa,
    wi,
    wo,
    pbuf,
    crecv,
    yrecv,
    lout,
    lrecv,
    macc,
    ga0,
    ga1,
    ecrecv,
    eyrecv,
    kacc,
    vacc,
    dracc,
    dkacc,
    dvacc,
    nacc,
    pacc,
    racc,
    facc,
    vec,
    vrecv,
    vquarter,
    nsum,
    nrecv,
    xq,
    xk,
    xv,
    xr,
    xc,
    xa0,
    xa1,
    xi,
    xo,
    zq,
    zk,
    zv,
    zr,
    zc,
    za0,
    za1,
    zi,
    zo,
    lsem,
    ssem,
    rsem,
    csem,
    dsem,
    bsem,
    tsem,
    wsem,
    psem,
    qsem,
    free,
):
    lanes, span, espan, cols, width, hidden, heads, buckets, parts = dims
    half = span // 2
    tiles = half // TILE
    tensor = lax.axis_index("tensor")
    yy = tensor // 2
    cc = lax.rem(tensor, 2)
    y_peer = {"tensor": (1 - yy) * 2 + cc}
    c_peer = {"tensor": yy * 2 + (1 - cc)}
    t_peer = {"tensor": (1 - yy) * 2 + (1 - cc)}
    mine = tensor
    y_other = (1 - yy) * 2 + cc
    c_other = yy * 2 + (1 - cc)
    both_other = (1 - yy) * 2 + (1 - cc)

    batch = lax.axis_index("batch")
    ring = parts // 2
    at_ring = batch // 2
    at_pair = lax.rem(batch, 2)
    x_peer = {"batch": at_ring * 2 + (1 - at_pair)}

    def z_peer(step):
        return {"batch": lax.rem(at_ring + step, ring) * 2 + at_pair}

    barrier = pltpu.get_barrier_semaphore()
    for peer in (y_peer, c_peer, t_peer):
        pl.semaphore_signal(barrier, inc=1, device_id=peer, device_id_type=MESH)

    @pl.loop(1, parts)
    def _(step):
        peer = {"batch": lax.rem(batch + step, parts)}
        pl.semaphore_signal(barrier, inc=1, device_id=peer, device_id_type=MESH)

    counts = {"local": 0, "y": 0, "c": 0, "t": 0}

    def local(src, dst):
        at = counts["local"]
        counts["local"] += 1
        copy = pltpu.make_async_copy(src, dst, lsem.at[at])
        copy.start()
        return copy

    def send_y(src, dst):
        at = counts["y"]
        counts["y"] += 1
        copy = pltpu.make_async_remote_copy(
            src_ref=src,
            dst_ref=dst,
            send_sem=ssem.at[at],
            recv_sem=rsem.at[at],
            device_id=y_peer,
            device_id_type=MESH,
        )
        copy.start()
        return copy

    def send_c(src, dst):
        at = counts["c"]
        counts["c"] += 1
        copy = pltpu.make_async_remote_copy(
            src_ref=src,
            dst_ref=dst,
            send_sem=csem.at[at],
            recv_sem=dsem.at[at],
            device_id=c_peer,
            device_id_type=MESH,
        )
        copy.start()
        return copy

    def send_t(src, dst):
        at = counts["t"]
        counts["t"] += 1
        copy = pltpu.make_async_remote_copy(
            src_ref=src,
            dst_ref=dst,
            send_sem=tsem.at[0, at],
            recv_sem=tsem.at[1, at],
            device_id=t_peer,
            device_id_type=MESH,
        )
        copy.start()
        return copy

    own_half = pl.ds(pl.multiple_of(cc * half, half), half)
    other_half = pl.ds(pl.multiple_of((1 - cc) * half, half), half)

    x_copies = [local(x_in.at[n], xf.at[n, mine]) for n in range(lanes)]
    own_rows = pl.ds(pl.multiple_of(cc * cols, cols), cols)
    own_parts = [
        local(wa_in.at[0], act.at[yy, own_rows]),
        local(wa_in.at[1], gp.at[1 + yy, own_rows]),
    ]
    ws_copy = local(ws_in, ws)
    wr_copy = local(wr_in, wr.at[0])
    wa_copy = local(wa_in, wa)
    e_copy = local(e_in, ef.at[0, mine])
    wc_copy = local(wc_in, wc)
    og_copies = [
        local(og_in.at[n, own_half], df.at[n, mine, own_half]) for n in range(lanes)
    ]
    par[mine] = jnp.zeros(par.shape[1:], f32)
    par[mine, 0:3, :] = ob_in[...]
    par[mine, 3:6, :] = ng_in[...]
    par[mine, 6:9, :] = nb_in[...]
    pl.semaphore_wait(barrier, 2 + parts)

    class Gather:
        def __init__(self, ref, at=None, source=None):
            def block(q):
                return ref.at[q] if at is None else ref.at[at, q]

            self.block = block
            source = block(mine) if source is None else source
            self.by_y = send_y(source, block(mine))
            self.by_c = send_c(source, block(mine))

        def finish(self):
            self.by_y.wait_recv()
            self.on = send_c(self.block(y_other), self.block(y_other))
            self.by_c.wait_recv()
            self.on.wait_recv()

        def done(self):
            self.by_y.wait_send()
            self.by_c.wait_send()
            self.on.wait_send()

    class Deal:
        def __init__(self, n):
            to_own = df.at[n, mine, own_half]
            to_other = df.at[n, mine, other_half]
            self.copies = [
                send_y(og_in.at[n, own_half], to_own),
                send_t(og_in.at[n, other_half], to_other),
                send_c(og_in.at[n, other_half], to_other),
            ]

        def finish(self):
            for copy in self.copies:
                copy.wait()

    class Weights:
        def __init__(self):
            self.group = min(parts, 16)
            self.base = batch // self.group * self.group
            self.place = lax.rem(batch, self.group)
            for copy in own_parts:
                copy.wait()
            self.fetch = [
                send_y(self.piece(self.source(k), k), self.piece(self.target(k, mine), k))
                for k in range(3)
            ]
            self.near = {}
            self.far = {}

        def source(self, k):
            return wc_in.at[0] if k == 2 else self.target(k, mine)

        def target(self, k, q):
            if k == 2:
                return wgc.at[q]
            rows = pl.ds(pl.multiple_of(lax.rem(q, 2) * cols, cols), cols)
            return gp.at[1 + q // 2, rows] if k else act.at[q // 2, rows]

        def piece(self, ref, k):
            size = (width if k == 2 else cols) // self.group
            return ref.at[pl.ds(pl.multiple_of(self.place * size, size), size)]

        def hand(self, src, k, step):
            peer = {"batch": self.base + lax.rem(self.place + step, self.group)}
            return pltpu.make_async_remote_copy(
                src_ref=src,
                dst_ref=src,
                send_sem=wsem.at[k, 0],
                recv_sem=wsem.at[k, 1],
                device_id=peer,
                device_id_type=MESH,
            )

        def hand_on(self, k):
            self.near[k] = send_c(self.source(k), self.target(k, mine))
            self.fetch[k].wait_recv()

            @pl.loop(1, self.group)
            def _(step):
                self.hand(self.piece(self.target(k, y_other), k), k, step).start()

        def across(self, k):
            size = width if k == 2 else cols
            rest = self.target(k, y_other).at[pl.ds(0, size - size // self.group)]
            self.hand(rest, k, 1).wait()
            self.far[k] = send_c(self.target(k, y_other), self.target(k, y_other))

        def finish(self, k):
            self.fetch[k].wait_send()
            self.near[k].wait()
            self.far[k].wait()

        def load_cross(self):
            copies = []
            for h in range(width // span):
                rows = pl.ds(h * span, span)
                for step in range(4):
                    q = lax.rem(mine + step, 4)
                    src = wgc.at[q, rows] if step else wc_in.at[0, rows]
                    copies.append(local(src, gp.at[h, :, col_of(q)]))
            return copies

    x_gather = []
    for n in range(lanes):
        x_gather.append(Gather(xf, n, x_in.at[n]))
        if n == 0:
            par_gather = Gather(par)
            weights = Weights()

    for ref in (nacc, pacc, racc, facc, kacc, vacc):
        ref[...] = jnp.zeros(ref.shape, ref.dtype)
    act[2] = jnp.zeros(act.shape[1:], bf16)

    lane_c = lax.broadcasted_iota(jnp.int32, (1, cols), 1)

    def head_f(h):
        return (lane_c // HEAD_DIM == h).astype(f32)

    def head_b(h):
        return head_f(h).astype(bf16)

    lane_w = lax.broadcasted_iota(jnp.int32, (1, 2 * heads * buckets), 1)

    def word_b(h):
        mask = lax.rem(lane_w, heads * buckets) // buckets == h
        return mask.astype(f32).astype(bf16)

    lane_r = lax.broadcasted_iota(jnp.int32, (1, heads * buckets), 1)

    def word_f(h):
        return (lane_r // buckets == h).astype(f32)

    flip = (
        lax.broadcasted_iota(jnp.int32, (half, half), 0)
        + lax.broadcasted_iota(jnp.int32, (half, half), 1)
        == half - 1
    )
    flip = flip.astype(f32).astype(bf16)
    slot = lax.broadcasted_iota(jnp.int32, (1, 128), 1)

    def rows_of(i):
        return pl.ds(pl.multiple_of(i * TILE, TILE), TILE)

    def own_tile(i):
        return pl.ds(pl.multiple_of(cc * half + i * TILE, TILE), TILE)

    def which_half(i):
        return lax.rem(i + cc, 2)

    def half_rows(which):
        return pl.ds(pl.multiple_of(which * half, half), half)

    def col_of(j):
        return pl.ds(pl.multiple_of(j * cols, cols), cols)

    def wide(ref, n, rows):
        return jnp.concatenate([ref[n, q, rows, :] for q in range(4)], axis=1)

    def summed(n, parity, i):
        rows = own_tile(i)
        mine_part = wide(pbuf, n, rows).astype(f32)
        return mine_part + wide(yrecv.at[parity], n, rows_of(i)).astype(f32)

    def put_wide(ref, n, rows, v):
        for q in range(4):
            ref[n, q, rows, :] = v[:, q * cols : (q + 1) * cols].astype(ref.dtype)

    def param(k):
        return jnp.concatenate([par[q, k : k + 1, :] for q in range(4)], axis=1)

    def put_slot(ref, rows, k, v):
        ref[rows, :] = jnp.where(slot == k, v, ref[rows, :])

    def get_slot(rows, k):
        return total(jnp.where(slot == k, lse[rows, :], 0.0))

    code = code_in[0]

    def pick(values):
        whole, two, four = values
        return jnp.where(code == 0, whole, jnp.where(code == 1, two, four))

    def group_of(spots, length):
        return pick((spots * 0, spots // (length // 2), spots // (length // 4)))

    def key_groups(fill, length):
        spots = lax.broadcasted_iota(jnp.int32, (1, length), 1)
        group = group_of(spots, length)
        long = pick((length, length // 2, length // 4))
        ends = spots * 0
        for g in range(fill.shape[1]):
            end = long - (fill[0, g] & (long // 2 - 1))
            ends = jnp.where(group == g, end, ends)
        return jnp.where(spots - group * long < ends, group, -1)

    def build_tables():
        keys = key_groups(fill_in, span)
        ekeys = key_groups(efill_in, espan)

        word = lax.broadcasted_iota(jnp.int32, (2 * heads * buckets, 1), 0)
        hot = (lax.rem(word, buckets) == buckets_in[...]).astype(f32).astype(bf16)

        def moves(size, shift):
            @pl.loop(0, size // TILE)
            def _(k):
                place = lax.broadcasted_iota(jnp.int32, (TILE, size), 0)
                place = place + lax.broadcasted_iota(jnp.int32, (TILE, size), 1)
                place = place + (2 * size + k * TILE - shift)
                smask[rows_of(k), :size] = ((place & (size - 1)) == 0).astype(f32).astype(bf16)

        for table, turned, size, shift in (
            (oh_first, oht_first, half, 0),
            (oh_second, oht_second, span, half),
        ):
            moves(size, shift)
            table[...] = dot(hot[:, :size], smask[:size, :size]).astype(bf16)
            moves(size, shift + half - 1)
            flat = hot[: heads * buckets, :size]
            turned[...] = dot_nt(smask[:size, :size], flat).astype(bf16)

        @pl.loop(0, span // TILE)
        def _(i):
            rows = rows_of(i)
            spots = lax.broadcasted_iota(jnp.int32, (TILE, 1), 0) + i * TILE
            group = group_of(spots, span)
            allowed = (group == keys) & (spots >= lax.broadcasted_iota(jnp.int32, (1, span), 1))
            smask[rows, :] = jnp.where(allowed, 0.0, neg_big).astype(bf16)
            cmask[rows, :] = jnp.where(group == ekeys, 0.0, neg_big).astype(bf16)

    build_tables()

    wi_copy = local(wi_in, wi.at[0])
    wo_copy = local(wo_in, wo.at[0])

    class Reduce:
        def __init__(self, n, parity):
            self.n = n
            self.parity = parity
            self.first = send_c(pbuf.at[n, :, other_half], crecv.at[n])

        def middle(self):
            n = self.n
            self.first.wait_recv()

            @pl.loop(0, tiles)
            def _(i):
                rows = own_tile(i)
                for q in range(4):
                    both = pbuf[n, q, rows, :].astype(f32)
                    both = both + crecv[n, q, rows_of(i), :].astype(f32)
                    pbuf[n, q, rows, :] = both.astype(bf16)

            self.second = send_y(pbuf.at[n, :, own_half], yrecv.at[self.parity, n])

        def finish(self):
            self.first.wait_send()
            self.second.wait()

    class Swap:
        def __init__(self, ref, n, parity):
            place = yrecv.at[parity, n, mine]
            self.copies = [
                send_y(ref.at[n, own_half], place),
                send_t(ref.at[n, other_half], place),
                send_c(ref.at[n, other_half], place),
            ]

        def middle(self):
            pass

        def finish(self):
            for copy in self.copies:
                copy.wait()

    def heads_of(n, parity):
        return jnp.concatenate([yrecv[parity, n, q] for q in range(4)], axis=1)

    def project_heads(n, parity, k):
        @pl.loop(0, 4)
        def _(j):
            rows = heads_of(n, parity)
            at = col_of(j)
            low, high = (gp[1, :, at], gp[2, :, at]) if k else (act[0, :, at], act[1, :, at])
            part = dot(rows[:, : 2 * cols], low) + dot(rows[:, 2 * cols :], high)
            pbuf[n, j, own_half, :] = part.astype(bf16)

    def project_back(n, parity):
        @pl.loop(0, 4)
        def _(j):
            rows = heads_of(n, parity)
            at = pl.ds(pl.multiple_of(lax.rem(j, 2) * cols, cols), cols)
            pbuf[n, j, own_half, :] = dot_nt(rows, gp[j // 2, at, :]).astype(bf16)

    class Scatter:
        def __init__(self, part, from_c, from_y):
            self.part, self.from_c, self.from_y = part, from_c, from_y
            self.first = [
                send_c(part.at[2 * k + 1 - cc, pl.ds(r * half, half)], from_c.at[2 * k + r])
                for k in range(2)
                for r in range(2)
            ]

        def middle(self):
            for copy in self.first:
                copy.wait_recv()
            part = self.part
            for k in range(2):
                for r in range(2):

                    @pl.loop(0, tiles)
                    def _(i, k=k, r=r):
                        rows = rows_of(i + r * tiles)
                        both = part[2 * k + cc, rows, :].astype(f32)
                        both = both + self.from_c[2 * k + r, rows_of(i), :].astype(f32)
                        part[2 * k + cc, rows, :] = both.astype(bf16)

            self.second = [
                send_y(part.at[y_other, pl.ds(r * half, half)], self.from_y.at[r]) for r in range(2)
            ]

        def finish(self, store):
            for copy in self.second:
                copy.wait()
            for copy in self.first:
                copy.wait_send()
            for r in range(2):

                @pl.loop(0, tiles)
                def _(i, r=r):
                    rows = rows_of(i + r * tiles)
                    store(
                        rows,
                        self.part[mine, rows, :].astype(f32)
                        + self.from_y[r, rows_of(i), :].astype(f32),
                    )

    class Share:
        def __init__(self, grad, pair, far, out, at):
            self.grad, self.pair, self.far, self.out, self.at = grad, pair, far, out, at
            self.block = width // parts

            @pl.loop(0, ring)
            def _(z):
                self.near(self.rows(z, 1 - at_pair), pair.at[z]).start()

        def rows(self, z, x):
            start = pl.multiple_of((z * 2 + x) * self.block, self.block)
            return self.grad.at[:, pl.ds(start, self.block), :]

        def near(self, src, dst):
            return pltpu.make_async_remote_copy(
                src_ref=src,
                dst_ref=dst,
                send_sem=bsem.at[self.at, 0],
                recv_sem=bsem.at[self.at, 1],
                device_id=x_peer,
                device_id_type=MESH,
            )

        def away(self, src, dst, step):
            return pltpu.make_async_remote_copy(
                src_ref=src,
                dst_ref=dst,
                send_sem=bsem.at[self.at, 2],
                recv_sem=bsem.at[self.at, 3],
                device_id=z_peer(step),
                device_id_type=MESH,
            )

        def middle(self):
            self.near(self.pair, self.pair).wait()

            @pl.loop(0, ring)
            def _(z):
                for m in range(self.grad.shape[0]):
                    start = pl.multiple_of((z * 2 + at_pair) * self.block, self.block)
                    own = self.grad[m, pl.ds(start, self.block), :].astype(f32)
                    self.pair[z, m] = (own + self.pair[z, m].astype(f32)).astype(bf16)

            @pl.loop(1, ring)
            def _(step):
                self.away(
                    self.pair.at[lax.rem(at_ring + step, ring)], self.far.at[step - 1], step
                ).start()

        def last(self):
            self.away(self.far, self.far, 1).wait()
            self.out[...] = self.pair[at_ring].astype(f32)

            @pl.loop(1, ring)
            def _(step):
                self.out[...] += self.far[step - 1].astype(f32)

    def norm_rows(resid):
        mean = total(resid) * (1.0 / width)
        centred = resid - mean
        var = total(centred * centred) * (1.0 / width)
        rs = lax.rsqrt(var + norm_eps)
        return centred * rs, rs

    def norm_grad(grad, xh, rs, gain, k):
        q = grad * gain
        m1 = total(q) * (1.0 / width)
        m2 = total(q * xh) * (1.0 / width)
        back = rs * (q - m1 - xh * m2)
        nacc[k] += eight(grad * xh)
        nacc[3 + k] += eight(grad)
        nacc[6 + k] += eight(back)
        return back

    at_scale = 2 * lanes * heads

    def give(ref, n):
        return send_c(ref.at[n, :, own_half], ref.at[n, :, own_half])

    def norm_first(n):
        project_heads(n, 1, 0)

        @pl.loop(0, tiles)
        def _(i):
            rows = own_tile(i)
            resid = wide(xf, n, rows).astype(f32) + wide(pbuf, n, rows).astype(f32) + param(0)
            xh, rs = norm_rows(resid)
            put_slot(lse, rows, at_scale + n, rs)
            put_wide(f1, n, rows, xh * param(3) + param(6))

        return give(f1, n)

    def norm_second(n):
        project_heads(n, 0, 1)

        @pl.loop(0, tiles)
        def _(i):
            rows = own_tile(i)
            resid = wide(f1, n, rows).astype(f32) + wide(pbuf, n, rows).astype(f32) + param(1)
            xh, rs = norm_rows(resid)
            put_slot(lse, rows, at_scale + lanes + n, rs)
            put_wide(f2, n, rows, xh * param(4) + param(7))

        return give(f2, n)

    out_copies = []

    def norm_third(n):
        @pl.loop(0, tiles)
        def _(i):
            rows = own_tile(i)
            resid = wide(f2, n, rows).astype(f32) + summed(n, 1, i) + param(2)
            xh, rs = norm_rows(resid)
            out = xh * param(5) + param(8)
            put_wide(pbuf, n, rows, out)
            out_ref[n, rows, :] = pbuf[n, mine, rows, :]
            lout[n, rows_of(i), :] = pbuf[n, c_other, rows, :]
            grad = wide(df, n, rows).astype(f32)
            put_wide(df, n, rows, norm_grad(grad, xh, rs, param(5), 2))

        out_copies.append(send_c(lout.at[n], lrecv.at[n]))
        return give(df, n)

    def norm_second_back(n):
        @pl.loop(0, tiles)
        def _(i):
            rows = own_tile(i)
            grad = wide(df, n, rows).astype(f32) + summed(n, 0, i)
            gain = param(4)
            xh = (wide(f2, n, rows).astype(f32) - param(7)) * (1.0 / gain)
            rs = get_slot(rows, at_scale + lanes + n)
            put_wide(df, n, rows, norm_grad(grad, xh, rs, gain, 1))

    def norm_first_back(n):
        project_back(n, 1)

        @pl.loop(0, tiles)
        def _(i):
            rows = own_tile(i)
            grad = wide(df, n, rows).astype(f32) + wide(pbuf, n, rows).astype(f32)
            gain = param(3)
            xh = (wide(f1, n, rows).astype(f32) - param(6)) * (1.0 / gain)
            rs = get_slot(rows, at_scale + n)
            put_wide(df, n, rows, norm_grad(grad, xh, rs, gain, 0))

    def halves(got, body):
        @pl.loop(0, 2)
        def _(i):
            if got is not None:

                @pl.when(i == 1)
                def _():
                    got.wait()

            which = which_half(i)
            body(which, half_rows(which), i)

    def keep_own(parity, n, which, v):
        @pl.when(which == cc)
        def _():
            yrecv[parity, n, mine] = v

    def each_head(body):
        pl.loop(0, heads, unroll=HEAD_UNROLL)(body)

    def spot(k, h, size, wide=None):
        row = pl.ds(pl.multiple_of(lax.rem(h, 2) * half, half), half)
        col = pl.ds(pl.multiple_of(k * span + (h // 2) * size, size), wide or size)
        return row, col

    def put_head(kind, n, which, h):
        place = spot(0, h, span)
        return pltpu.make_async_copy(
            act.at[(2,) + place], pstore.at[(kind, n, which) + place], psem.at[h]
        )

    def fetch(kind, n, which, at):
        return pltpu.make_async_copy(pstore.at[kind, n, which], act.at[at], qsem.at[at])

    def self_score(n, which, rows, h, diag):
        reach = (which + 1) * half
        qh = qb[n, rows, :] * head_b(h)
        table = oh_second if which else oh_first
        spread = dot(relb[n, rows, :] * word_b(h), table[...])
        bias = pltpu.roll(spread, 0, 1, stride=1, stride_axis=0)
        s = dot_nt(qh, kb[0, :reach, :]) + smask[rows, :reach].astype(f32)
        if n > 0:
            s = jnp.where(diag, total(qh.astype(f32) * kb[n, rows, :].astype(f32)), s)
        return qh, s + bias

    def diagonal(which):
        r = lax.broadcasted_iota(jnp.int32, (half, (which + 1) * half), 0)
        s = lax.broadcasted_iota(jnp.int32, (half, (which + 1) * half), 1)
        return s == r + which * half

    def both_halves(body):
        for which in range(2):
            body(which, pl.ds(which * half, half), (which + 1) * half)

    def project_rows(n):
        def body(which, rows, i):
            x = wide(xf, n, rows)
            q = (dot(x, ws[0]) + pbias[0:1, :]).astype(bf16)
            qb[n, rows, :] = (q.astype(f32) * 0.125).astype(bf16)
            kb[n, rows, :] = dot(x, ws[1]).astype(bf16)
            vb[n, rows, :] = (dot(x, ws[2]) + pbias[1:2, :]).astype(bf16)
            rel = dot(x, wr[0]) + rbias[...]
            high = rel.astype(bf16)
            relb[n, rows, : heads * buckets] = high
            relb[n, rows, heads * buckets :] = (rel - high.astype(f32)).astype(bf16)

        halves(None, body)

    def self_forward(n):
        project_rows(n)

        def body(which, rows, reach):
            macc[...] = jnp.zeros(macc.shape, f32)

            @each_head
            def _(h):
                if n > 0 or which > 0:
                    put_head(0, n, which, h).wait()
                diag = diagonal(which) if n > 0 else None
                qh, s = self_score(n, which, rows, h, diag)
                w = jnp.exp(s - jnp.max(s, axis=1, keepdims=True))
                inverse = 1.0 / total(w)
                if n > 0:
                    own = total(jnp.where(diag, w, 0.0)) * inverse
                    put_slot(lse, rows, n * heads + h, own)
                    w = jnp.where(diag, 0.0, w)
                prob = (w * inverse).astype(bf16)
                act[(2,) + spot(0, h, span, reach)] = prob
                put_head(0, n, which, h).start()
                part = dot(prob, vb[0, :reach, :])
                if n > 0:
                    part = part + own.astype(bf16).astype(f32) * vb[n, rows, :].astype(f32)
                macc[...] += part * head_f(h)

            low = macc[...].astype(bf16)
            att[n, rows, :] = low
            keep_own(1, n, which, low)

        both_halves(body)

    def encoder_rows():
        @pl.loop(0, espan // TILE)
        def _(i):
            rows = rows_of(i)
            e = wide(ef, 0, rows)
            ck[rows, :] = dot(e, wc[1]).astype(bf16)
            cv[rows, :] = (dot(e, wc[2]) + pbias[3:4, :]).astype(bf16)

    def cross_forward(n, got):
        def body(which, rows, i):
            q = (dot(wide(f1, n, rows), wc[0]) + pbias[2:3, :]).astype(bf16)
            cq[n, rows, :] = (q.astype(f32) * 0.125).astype(bf16)
            macc[...] = jnp.zeros(macc.shape, f32)

            @each_head
            def _(h):
                put_head(1, n, which, h).wait()
                s = dot_nt(cq[n, rows, :] * head_b(h), ck[...]) + cmask[rows, :].astype(f32)
                w = jnp.exp(s - jnp.max(s, axis=1, keepdims=True))
                prob = (w * (1.0 / total(w))).astype(bf16)
                act[(2,) + spot(0, h, span)] = prob
                put_head(1, n, which, h).start()
                macc[...] += dot(prob, cv[...]) * head_f(h)

            low = macc[...].astype(bf16)
            catt[n, rows, :] = low
            keep_own(0, n, which, low)

        halves(got, body)

    def ffn_forward(n, got):
        def body(which, rows, i):
            @pl.loop(0, hidden // cols)
            def _(j):
                at = col_of(j)
                pre = dot(wide(f2, n, rows), wi[0, :, at]) + fbias[:, at]
                value, slope = gelu_both(pre)
                act[n, rows, at] = value.astype(bf16)
                gp[n, rows, at] = slope.astype(bf16)

            @pl.loop(0, width // cols)
            def _(j):
                pbuf[n, j, rows, :] = dot(act[n, rows, :], wo[0, :, col_of(j)]).astype(bf16)

        halves(got, body)

    def ffn_backward(n, got):
        def body(which, rows, i):
            @pl.loop(0, hidden // cols)
            def _(j):
                at = col_of(j)
                grad = dot_nt(wide(df, n, rows), wo[0, at, :]) * gp[n, rows, at].astype(f32)
                facc[:, at] += eight(grad)
                gp[n, rows, at] = grad.astype(bf16)

            @pl.loop(0, width // cols)
            def _(j):
                pbuf[n, j, rows, :] = dot_nt(gp[n, rows, :], wi[0, col_of(j), :]).astype(bf16)

        halves(got, body)

    def stacked(ref, n, k, size, wide=None):
        parts = [ref[(n,) + spot(k, h, size, wide)] for h in range(heads)]
        return jnp.concatenate(parts, axis=0)

    def keep_head(h, ds, dh, qh, reach):
        gp[(2,) + spot(0, h, span, reach)] = ds
        act[(2,) + spot(0, h, cols)] = dh
        act[(2,) + spot(1, h, cols)] = qh

    def add_heads(at, reach):
        vacc[:reach, :] += dot_tn(stacked(act, at, 0, span, reach), stacked(act, 2, 0, cols))
        kacc[:reach, :] += dot_tn(stacked(gp, 2, 0, span, reach), stacked(act, 2, 1, cols))

    def cross_backward(n, got, following):
        def body(which, rows, i):
            fetch(1, n, which, i).wait()
            da = dot_nt(wide(df, n, rows), wa[1]).astype(bf16)
            macc[...] = jnp.zeros(macc.shape, f32)

            @each_head
            def _(h):
                qh = cq[n, rows, :] * head_b(h)
                dh = da * head_b(h)
                p = act[(i,) + spot(0, h, span)].astype(f32)
                both = p * dot_nt(dh, cv[...])
                ds = (both - p * total(both)).astype(bf16)
                keep_head(h, ds, dh, qh, espan)
                macc[...] += dot(ds, ck[...]) * head_f(h)

            add_heads(i, espan)
            if following is None:
                fetch(0, late[0], i, i).start()
            else:
                fetch(1, following, which, i).start()
            dq = macc[...] * 0.125
            pacc[2] += eight(dq)
            low = dq.astype(bf16)
            cq[n, rows, :] = low
            keep_own(1, n, which, low)

        halves(got, body)

    def encoder_backward():
        pacc[3] += eight(vacc[...])

        @pl.loop(0, espan // TILE)
        def _(i):
            rows = rows_of(i)
            dk = kacc[rows, :].astype(bf16)
            dv = vacc[rows, :].astype(bf16)
            ck[rows, :] = dk
            cv[rows, :] = dv
            part = dot_nt(dk, wc[1]) + dot_nt(dv, wc[2])
            for q in range(4):
                f2[0, q, rows, :] = part[:, q * cols : (q + 1) * cols].astype(bf16)

    def self_backward(n, following):
        def body(which, rows, reach):
            fetch(0, n, which, which).wait()
            da = dot_nt(wide(df, n, rows), wa[0]).astype(bf16)
            macc[...] = jnp.zeros(macc.shape, f32)
            dracc[...] = jnp.zeros(dracc.shape, f32)
            if n > 0:
                dkacc[...] = jnp.zeros(dkacc.shape, f32)
                dvacc[...] = jnp.zeros(dvacc.shape, f32)

            @each_head
            def _(h):
                qh = qb[n, rows, :] * head_b(h)
                dh = da * head_b(h)
                p = act[(which,) + spot(0, h, span, reach)].astype(f32)
                both = p * dot_nt(dh, vb[0, :reach, :])
                delta = total(both)
                if n > 0:
                    own = get_slot(rows, n * heads + h)
                    own_dp = total(dh.astype(f32) * vb[n, rows, :].astype(f32))
                    delta = delta + own * own_dp
                    own_ds = own * (own_dp - delta)
                    put_slot(lse, rows, n * heads + h, own_ds)
                low = (both - p * delta).astype(bf16)
                keep_head(h, low, dh, qh, reach)
                turned = pltpu.roll(dot(flip, low), 0, 1, stride=1, stride_axis=0)
                table = oht_second if which else oht_first
                dracc[...] += dot(turned.astype(bf16), table[...]) * word_f(h)
                part = dot(low, kb[0, :reach, :])
                if n > 0:
                    own_s = own_ds.astype(bf16).astype(f32)
                    dkacc[...] += own_s * qh.astype(f32)
                    dvacc[...] += own.astype(bf16).astype(f32) * dh.astype(f32)
                    part = part + own_s * kb[n, rows, :].astype(f32)
                macc[...] += part * head_f(h)

            add_heads(which, reach)
            if following is not None:
                fetch(0, following, which, which).start()
            dq = macc[...] * 0.125
            pacc[0] += eight(dq)
            qb[n, rows, :] = dq.astype(bf16)
            drel = dot(flip, dracc[...].astype(bf16))
            racc[...] += eight(dracc[...])
            if n > 0:
                nearest = oht_first[half - 1 : half, :].astype(f32)
                for h in range(heads):
                    extra = get_slot(rows, n * heads + h) * (nearest * word_f(h))
                    drel = drel + extra
                    racc[...] += eight(extra)
                pacc[1] += eight(dvacc[...])
                kb[n, rows, :] = dkacc[...].astype(bf16)
                vb[n, rows, :] = dvacc[...].astype(bf16)
            relb[n, rows, : heads * buckets] = drel.astype(bf16)

        both_halves(body)
        if n == 0:
            pacc[1] += eight(vacc[...])
            kb[0] = kacc[...].astype(bf16)
            vb[0] = vacc[...].astype(bf16)

    def input_terms(n):
        @pl.loop(0, width // cols)
        def _(j):
            at = col_of(j)
            part = dot_nt(qb[n], ws[0, at, :]) + dot_nt(kb[n], ws[1, at, :])
            part = part + dot_nt(vb[n], ws[2, at, :])
            part = part + dot_nt(relb[n, :, : heads * buckets], wr[0, at, :])
            pbuf[n, j] = part.astype(bf16)

    def weight_grad(rows_ref, pieces, lane_count):
        @pl.loop(0, 4)
        def _(j):
            left = jnp.concatenate([rows_ref[n, j] for n in range(lane_count)], axis=0)
            for load, target, size in pieces:
                for start in range(0, size, cols):
                    step = min(cols, size - start)
                    right = jnp.concatenate(
                        [load(n, start, step) for n in range(lane_count)], axis=0
                    )
                    target[col_of(j), start : start + step] = dot_tn(left, right).astype(bf16)

    def of(ref):
        return lambda n, start, step: ref[n, :, start : start + step]

    words = heads * buckets

    order = list(range(lanes))
    late = order[1:] + order[:1]
    ws_copy.wait()
    wr_copy.wait()
    wa_copy.wait()
    reduces = {}
    gots = {}

    def after(n, exchange, following):
        if following is not None:
            following()
        exchange.middle()
        reduces[n] = exchange

    def ready(n, norm):
        def go():
            reduces[n].finish()
            gots[n] = norm(n)

        return go

    deals = []
    for n in order:
        x_copies[n].wait()
        x_gather[n].finish()
        if n == 0:
            par_gather.finish()
            weights.hand_on(0)
        self_forward(n)
        if n == 0:
            e_copy.wait()
            e_gather = Gather(ef, 0)
        after(n, Swap(att, n, 1), None)
        if n == 0:
            weights.hand_on(1)
        if n == 1:
            weights.across(0)
    weights.finish(0)
    wc_copy.wait()
    e_gather.finish()
    encoder_rows()
    ready(order[0], norm_first)()

    def second_of(*those):
        def go():
            if those[0] == order[0]:
                weights.finish(1)
            for n in those:
                ready(n, norm_second)()

        return go

    for k, n in enumerate(order):
        cross_forward(n, gots[n])
        og_copies[n].wait()
        following = order[k + 1] if k + 1 < lanes else None
        norm = ready(following, norm_first) if following else second_of(order[0])
        after(n, Swap(catt, n, 0), norm)
        deals.append(Deal(n))
        if k == 0:
            weights.across(1)
            weights.hand_on(2)
    for h in range(heads):
        put_head(1, order[-1], 0, h).wait()
    wi_copy.wait()
    wo_copy.wait()

    def third_of(n):
        def go():
            deals[n].finish()
            ready(n, norm_third)()

        return go

    for k, n in enumerate(order):
        ffn_forward(n, gots[n])
        if k == 0:
            norm = second_of(*order[1:])
        else:
            norm = third_of(order[0]) if k + 1 == lanes else None
        after(n, Reduce(n, 1), norm)
    for k, n in enumerate(order):
        ffn_backward(n, gots[n])
        after(n, Reduce(n, 0), third_of(order[k + 1]) if k + 1 < lanes else None)
        if k == 0:
            weights.across(2)
    weight_grad(df, [(of(act), wo.at[0], hidden)], lanes)
    share_o = Share(wo, xo, zo, go_ref, 0)
    pl.semaphore_signal(free.at[0], inc=1, device_id=c_peer, device_id_type=MESH)
    waited = set()

    def back_of(n, norm, k):
        def go():
            reduces[n].finish()
            norm(n)
            if k not in waited:
                waited.add(k)
                pl.semaphore_wait(free.at[k], 1)
            gots[n] = give(df, n)

        return go

    back_of(late[0], norm_second_back, 0)()
    weight_grad(f2, [(of(gp), wi.at[0], hidden)], lanes)
    share_i = Share(wi, xi, zi, gi_ref, 1)
    weights.finish(2)
    loads = weights.load_cross()
    for i in range(2):
        fetch(1, late[0], which_half(i), i).start()
    for k, n in enumerate(late):
        cross_backward(n, gots[n], late[k + 1] if k + 1 < lanes else None)
        after(n, Swap(cq, n, 1), back_of(late[k + 1], norm_second_back, 0) if k + 1 < lanes else None)
        if k == 1:
            share_o.middle()
    weight_grad(df, [(of(catt), ga1.at[0], cols)], lanes)
    share_a1 = Share(ga1, xa1, za1, ga1_ref, 2)
    pl.semaphore_signal(free.at[1], inc=1, device_id=c_peer, device_id_type=MESH)
    encoder_backward()
    e_scatter = Scatter(f2.at[0], ecrecv, eyrecv)
    for copy in loads:
        copy.wait()
    back_of(late[0], norm_first_back, 1)()
    e_scatter.middle()
    weight_grad(f1, [(of(cq), wc.at[0], cols)], lanes)
    weight_grad(
        ef,
        [
            (lambda n, a, b: ck[:, a : a + b], wc.at[1], cols),
            (lambda n, a, b: cv[:, a : a + b], wc.at[2], cols),
        ],
        1,
    )
    share_c = Share(wc, xc, zc, gc_ref, 4)
    share_i.middle()
    kacc[...] = jnp.zeros(kacc.shape, f32)
    vacc[...] = jnp.zeros(vacc.shape, f32)
    scatters = {}
    for k, n in enumerate(late):
        gots[n].wait()
        if k + 1 == lanes:
            weight_grad(df, [(of(att), ga0.at[0], cols)], lanes)
            share_a0 = Share(ga0, xa0, za0, ga0_ref, 3)
        self_backward(n, late[k + 1] if k + 1 < lanes else None)
        if k + 1 < lanes:
            input_terms(n)
            scatters[n] = Scatter(pbuf.at[n], crecv.at[n], yrecv.at[0, n])
            back_of(late[k + 1], norm_first_back, 1)()
            scatters[n].middle()
        if k == 0:

            def store_enc(rows, v):
                genc_ref[rows, :] = v

            e_scatter.finish(store_enc)
            share_o.last()
            share_a1.middle()
        if k == 1:
            share_i.last()
            share_c.middle()
    def last_grad(ref, k, pair, far, at):
        weight_grad(xf, [(of(ref), wc.at[k], cols)], lanes)
        return Share(wc.at[pl.ds(k, 1)], pair, far, gs_ref.at[pl.ds(k, 1)], at)

    share_v = last_grad(vb, 2, xv, zv, 6)
    share_k = last_grad(kb, 1, xk, zk, 8)
    input_terms(late[-1])
    scatters[late[-1]] = Scatter(pbuf.at[late[-1]], crecv.at[late[-1]], yrecv.at[0, late[-1]])
    share_q = last_grad(qb, 0, xq, zq, 9)
    scatters[late[-1]].middle()
    weight_grad(xf, [(of(relb), wr.at[0], words)], lanes)
    share_r = Share(wr, xr, zr, gr_ref, 5)
    share_a0.middle()
    for n in order:
        out_copies[n].wait()

        @pl.loop(0, tiles)
        def _(i, n=n):
            rows = pl.ds(pl.multiple_of((1 - cc) * half + i * TILE, TILE), TILE)
            out_ref[n, rows, :] = lrecv[n, rows_of(i), :]

    def vec_copy(src, dst, k, peer):
        return pltpu.make_async_remote_copy(
            src_ref=src,
            dst_ref=dst,
            send_sem=bsem.at[7, k],
            recv_sem=bsem.at[7, k + 1],
            device_id=peer,
            device_id_type=MESH,
        )

    for k in range(9):
        nsum[k : k + 1, :] = jnp.sum(nacc[k], axis=0, keepdims=True)
    norm_sums = send_c(nsum, nrecv)
    norm_sums.wait()
    for k in range(9):
        row = nsum[k : k + 1, :] + nrecv[k : k + 1, :]
        for q in range(4):
            vquarter[q, k : k + 1, :] = row[:, q * cols : (q + 1) * cols]
    vec[...] = jnp.zeros(vec.shape, f32)
    vec[0:9, :] = vquarter[mine, 0:9, :]
    for k in range(4):
        vec[9 + k : 10 + k, :] = jnp.sum(pacc[k], axis=0, keepdims=True)
    vec[13:14, :words] = jnp.sum(racc[...], axis=0, keepdims=True)
    row = jnp.sum(facc[...], axis=0, keepdims=True)
    for k in range(hidden // cols):
        vec[14 + k : 15 + k, :] = row[:, k * cols : (k + 1) * cols]
    vec_pair = vec_copy(vec, vrecv.at[0], 0, x_peer)
    vec_pair.start()
    share_v.middle()
    for n in late:

        def store_in(rows, v, n=n):
            gin_ref[n, rows, :] = df[n, mine, rows, :].astype(f32) + v

        scatters[n].finish(store_in)
    share_a1.last()
    share_c.last()
    share_k.middle()
    share_a0.last()
    share_q.middle()
    share_r.middle()
    vec_pair.wait()
    vec[...] += vrecv[0]

    @pl.loop(1, ring)
    def _(step):
        vec_copy(vec, vrecv.at[step], 2, z_peer(step)).start()

    share_v.last()
    share_k.last()
    share_q.last()
    share_r.last()
    every_vec = vrecv.at[pl.ds(1, ring - 1)]
    vec_copy(every_vec, every_vec, 2, z_peer(1)).wait()
    vec_ref[...] = vec[...]

    @pl.loop(1, ring)
    def _(step):
        vec_ref[...] += vrecv[step]

    for item in x_gather + [par_gather, e_gather]:
        item.done()


def finish_kernel(
    parts,
    out_i,
    gin_i,
    genc_i,
    vec_i,
    gs_i,
    gr_i,
    gc_i,
    ga0_i,
    ga1_i,
    gi_i,
    go_i,
    out_o,
    gin_o,
    genc_o,
    gs_o,
    gr_o,
    gc_o,
    gatt_o,
    gi_o,
    go_o,
    proj_o,
    rel_o,
    ffn_o,
    bias_o,
    gain_o,
    shift_o,
):
    own = lax.axis_index("batch")
    out_o[...] = out_i[...]
    gin_o[...] = gin_i[...]
    gs_o[...] = gs_i[...]
    gc_o[...] = gc_i[...]

    @pl.when(pl.program_id(0) == 0)
    def _():
        genc_o[...] = genc_i[...]
        gr_o[...] = gr_i[0]
        gi_o[...] = gi_i[0]
        go_o[...] = go_i[0].T
        gatt_o[0] = ga0_i[0].T
        gatt_o[1] = ga1_i[0].T
        cols = vec_i.shape[1]

        def chosen(rows, size):
            start = lax.rem(own * size, cols)
            at = lax.broadcasted_iota(jnp.int32, (cols, size), 0)
            at = at - lax.broadcasted_iota(jnp.int32, (cols, size), 1)
            pick = (at == start).astype(f32)
            return jnp.dot(rows, pick, precision=lax.Precision.HIGHEST, preferred_element_type=f32)

        each = cols // parts
        norms = chosen(vec_i[0:16, :], each)
        gain_o[...] = norms[0:3]
        shift_o[...] = norms[3:6]
        bias_o[...] = norms[6:9]
        proj_o[...] = norms[9:13]
        rel_o[...] = chosen(vec_i[8:16, :], rel_o.shape[1])[5:6]
        size = ffn_o.shape[1]
        row = lax.broadcasted_iota(jnp.int32, (vec_i.shape[0], 1), 0)
        line = jnp.where(row == 14 + own * size // cols, vec_i[...], 0.0)
        line = jnp.sum(line, axis=0, keepdims=True)
        ffn_o[...] = chosen(jnp.broadcast_to(line, (8, cols)), size)[0:1]


def per_device(
    layer_in,
    encoder_states,
    w_self,
    w_rel,
    w_cross,
    w_attn_out,
    w_in,
    w_out,
    proj_bias,
    rel_bias,
    ffn_in_bias,
    out_bias,
    norm_gain,
    norm_bias,
    rel_buckets,
    slot_log,
    tgt_fill,
    enc_fill,
    out_grad,
):
    lanes, span, cols = layer_in.shape
    espan = encoder_states.shape[0]
    width = w_self.shape[1]
    hidden = w_in.shape[1]
    heads = cols // HEAD_DIM
    words = w_rel.shape[1]
    buckets = words // heads
    half = span // 2
    parts = lax.axis_size("batch")
    ring = parts // 2
    block = width // parts
    shapes = [(1, cols)] * 3 + [(1, words), (3, cols), (1, cols), (1, cols), (1, hidden), (1, hidden)]
    vec_rows = -(-(14 + hidden // cols) // 8) * 8
    dims = (lanes, span, espan, cols, width, hidden, heads, buckets, parts)
    any_spec = pl.BlockSpec(memory_space=pl.ANY)
    vmem = pl.BlockSpec(memory_space=pltpu.VMEM)
    V = pltpu.VMEM
    smem = pl.BlockSpec(memory_space=pltpu.SMEM)
    scratch = [
        V((span, span), bf16),
        V((span, espan), bf16),
        V((2 * words, half), bf16),
        V((2 * words, span), bf16),
        V((half, words), bf16),
        V((span, words), bf16),
        V((4, 16, cols), f32),
        V((lanes, 4, span, cols), bf16),
        V((1, 4, espan, cols), bf16),
        V((lanes, 4, span, cols), bf16),
        V((lanes, 4, span, cols), bf16),
        V((lanes, 4, span, cols), bf16),
        V((lanes, span, hidden), bf16),
        V((lanes, span, hidden), bf16),
        V((lanes, span, cols), bf16),
        V((lanes, span, cols), bf16),
        V((lanes, span, cols), bf16),
        V((lanes, span, 2 * words), bf16),
        V((lanes, span, cols), bf16),
        V((lanes, span, cols), bf16),
        V((lanes, span, cols), bf16),
        V((espan, cols), bf16),
        V((espan, cols), bf16),
        V((span, 128), f32),
        V(w_self.shape, bf16),
        V((1,) + w_rel.shape, bf16),
        V(w_cross.shape, bf16),
        V(w_attn_out.shape, bf16),
        V((1,) + w_in.shape, bf16),
        V((1,) + w_out.shape, bf16),
        V((lanes, 4, span, cols), bf16),
        V((lanes, 4, half, cols), bf16),
        V((2, lanes, 4, half, cols), bf16),
        V((lanes, half, cols), bf16),
        V((lanes, half, cols), bf16),
        V((half, cols), f32),
        V((1, width, cols), bf16),
        V((1, width, cols), bf16),
        V((4, espan // 2, cols), bf16),
        V((2, espan // 2, cols), bf16),
        V((span, cols), f32),
        V((span, cols), f32),
        V((half, words), f32),
        V((half, cols), f32),
        V((half, cols), f32),
        V((9, 8, width), f32),
        V((4, 8, cols), f32),
        V((8, words), f32),
        V((8, hidden), f32),
        V((vec_rows, cols), f32),
        V((ring, vec_rows, cols), f32),
        V((4, 16, cols), f32),
        V((16, width), f32),
        V((16, width), f32),
        *[V((ring, m, block, w), bf16) for m, w in shapes],
        *[V((ring - 1, m, block, w), bf16) for m, w in shapes],
        pltpu.SemaphoreType.DMA((64,)),
        pltpu.SemaphoreType.DMA((64,)),
        pltpu.SemaphoreType.DMA((64,)),
        pltpu.SemaphoreType.DMA((128,)),
        pltpu.SemaphoreType.DMA((128,)),
        pltpu.SemaphoreType.DMA((10, 4)),
        pltpu.SemaphoreType.DMA((2, 16)),
        pltpu.SemaphoreType.DMA((3, 2)),
        pltpu.SemaphoreType.DMA((4,)),
        pltpu.SemaphoreType.DMA((2,)),
        pltpu.SemaphoreType.REGULAR((2,)),
    ]
    result, g_in, g_enc, vec, g_self, g_rel, g_cross, g_att0, g_att1, g_win, g_wout, _, _ = pl.pallas_call(
        functools.partial(layer_kernel, dims),
        out_shape=(
            jax.ShapeDtypeStruct((lanes, span, cols), bf16),
            jax.ShapeDtypeStruct((lanes, span, cols), f32),
            jax.ShapeDtypeStruct((espan, cols), f32),
            jax.ShapeDtypeStruct((vec_rows, cols), f32),
            jax.ShapeDtypeStruct((3, block, cols), f32),
            *[jax.ShapeDtypeStruct((m, block, w), f32) for m, w in shapes[3:]],
            jax.ShapeDtypeStruct((4, width, cols), bf16),
            jax.ShapeDtypeStruct((2, lanes, 2, span, hidden), bf16),
        ),
        in_specs=[any_spec] * 3 + [vmem] * 3 + [any_spec] * 6 + [vmem] * 4 + [smem] * 3,
        out_specs=(vmem,) * 11 + (any_spec,) * 2,
        scratch_shapes=scratch,
        compiler_params=pltpu.CompilerParams(
            collective_id=0, has_side_effects=True, vmem_limit_bytes=64 * 2**20
        ),
    )(
        layer_in,
        encoder_states,
        out_grad,
        out_bias,
        norm_gain,
        norm_bias,
        w_self,
        w_rel,
        w_cross,
        w_attn_out,
        w_in,
        w_out,
        proj_bias,
        rel_bias[None],
        ffn_in_bias[None],
        rel_buckets[None],
        slot_log,
        tgt_fill,
        enc_fill,
    )
    each = cols // parts
    flat = [
        jax.ShapeDtypeStruct(result.shape, bf16),
        jax.ShapeDtypeStruct(g_in.shape, f32),
        jax.ShapeDtypeStruct(g_enc.shape, f32),
        jax.ShapeDtypeStruct(g_self.shape, f32),
        jax.ShapeDtypeStruct((block, words), f32),
        jax.ShapeDtypeStruct(g_cross.shape, f32),
        jax.ShapeDtypeStruct((2, cols, block), f32),
        jax.ShapeDtypeStruct((block, hidden), f32),
        jax.ShapeDtypeStruct((hidden, block), f32),
        jax.ShapeDtypeStruct((4, each), f32),
        jax.ShapeDtypeStruct((1, words // parts), f32),
        jax.ShapeDtypeStruct((1, hidden // parts), f32),
        *[jax.ShapeDtypeStruct((3, each), f32)] * 3,
    ]

    def by_lane(v):
        return pl.BlockSpec((1,) + v.shape[1:], lambda i: (i, 0, 0))

    def whole(v):
        return pl.BlockSpec(v.shape, lambda i: (0,) * len(v.shape))

    stepped = (0, 1, 3, 5)
    ins = [result, g_in, g_enc, vec, g_self, g_rel, g_cross, g_att0, g_att1, g_win, g_wout]
    done = pl.pallas_call(
        functools.partial(finish_kernel, parts),
        grid=(lanes,),
        out_shape=flat,
        in_specs=[by_lane(v) if k in (0, 1, 4, 6) else whole(v) for k, v in enumerate(ins)],
        out_specs=[by_lane(v) if k in stepped else whole(v) for k, v in enumerate(flat)],
        compiler_params=pltpu.CompilerParams(vmem_limit_bytes=64 * 2**20),
    )(*ins)
    return tuple(done[:10]) + (done[10][0], done[11][0]) + tuple(done[12:])


def solution(mesh):
    return jax.shard_map(
        per_device,
        mesh=mesh,
        in_specs=(
            P(None, "batch", "tensor"),
            P("batch", "tensor"),
            P(None, None, "tensor"),
            P(None, "tensor"),
            P(None, None, "tensor"),
            P(None, "tensor", None),
            P(None, "tensor"),
            P("tensor", None),
            P(None, "tensor"),
            P("tensor"),
            P("tensor"),
            P(None, "tensor"),
            P(None, "tensor"),
            P(None, "tensor"),
            P(),
            P("batch"),
            P("batch", None),
            P("batch", None),
            P(None, "batch", "tensor"),
        ),
        out_specs=(
            P(None, "batch", "tensor"),
            P(None, "batch", "tensor"),
            P("batch", "tensor"),
            P(None, "batch", "tensor"),
            P("batch", "tensor"),
            P(None, "batch", "tensor"),
            P(None, "tensor", "batch"),
            P("batch", "tensor"),
            P("tensor", "batch"),
            P(None, ("tensor", "batch")),
            P(("tensor", "batch")),
            P(("tensor", "batch")),
            P(None, ("tensor", "batch")),
            P(None, ("tensor", "batch")),
            P(None, ("tensor", "batch")),
        ),
        check_vma=False,
    )
```

```python
import functools

import jax
import jax.numpy as jnp
from jax import lax
from jax.experimental import pallas as pl
from jax.experimental.pallas import tpu as pltpu
from jax.sharding import PartitionSpec as P

HEAD_DIM = 64
norm_eps = 1e-05
neg_big = -1e30
MESH = pl.DeviceIdType.MESH
f32 = jnp.float32
bf16 = jnp.bfloat16
TILE = 128
HEAD_UNROLL = 2


def dot(a, b):
    return jnp.dot(a, b, preferred_element_type=f32)


def dot_nt(a, b):
    return lax.dot_general(a, b, (((1,), (1,)), ((), ())), preferred_element_type=f32)


def dot_tn(a, b):
    return lax.dot_general(a, b, (((0,), (0,)), ((), ())), preferred_element_type=f32)


def total(v):
    return jnp.sum(v, axis=1, keepdims=True)


def eight(v):
    return jnp.sum(v.reshape(v.shape[0] // 8, 8, v.shape[1]), axis=0)


def gelu_both(v):
    half = 0.5 * (1.0 + lax.erf(v * (0.5**0.5)))
    bell = jnp.exp(-0.5 * v * v) * 0.3989422804014327
    return v * half, half + v * bell


def layer_kernel(
    dims,
    x_in,
    e_in,
    og_in,
    ob_in,
    ng_in,
    nb_in,
    ws_in,
    wr_in,
    wc_in,
    wa_in,
    wi_in,
    wo_in,
    pbias,
    rbias,
    fbias,
    buckets_in,
    code_in,
    fill_in,
    efill_in,
    out_ref,
    gin_ref,
    genc_ref,
    vec_ref,
    gs_ref,
    gr_ref,
    gc_ref,
    ga0_ref,
    ga1_ref,
    gi_ref,
    go_ref,
    wgc,
    pstore,
    smask,
    cmask,
    oh_first,
    oh_second,
    oht_first,
    oht_second,
    par,
    xf,
    ef,
    df,
    f1,
    f2,
    act,
    gp,
    qb,
    kb,
    vb,
    relb,
    att,
    catt,
    cq,
    ck,
    cv,
    lse,
    ws,
    wr,
    wc,
    wa,
    wi,
    wo,
    pbuf,
    crecv,
    yrecv,
    lout,
    lrecv,
    macc,
    ga0,
    ga1,
    ecrecv,
    eyrecv,
    kacc,
    vacc,
    dracc,
    dkacc,
    dvacc,
    nacc,
    pacc,
    racc,
    facc,
    vec,
    vrecv,
    vquarter,
    nsum,
    nrecv,
    xq,
    xk,
    xv,
    xr,
    xc,
    xa0,
    xa1,
    xi,
    xi_more,
    xo,
    xo_more,
    zq,
    zk,
    zv,
    zr,
    zc,
    za0,
    za1,
    zi,
    zi_more,
    zo,
    zo_more,
    lsem,
    ssem,
    rsem,
    csem,
    dsem,
    bsem,
    tsem,
    wsem,
    psem,
    qsem,
    free,
):
    lanes, span, espan, cols, width, hidden, heads, buckets, parts = dims
    half = span // 2
    tiles = half // TILE
    tensor = lax.axis_index("tensor")
    yy = tensor // 2
    cc = lax.rem(tensor, 2)
    y_peer = {"tensor": (1 - yy) * 2 + cc}
    c_peer = {"tensor": yy * 2 + (1 - cc)}
    t_peer = {"tensor": (1 - yy) * 2 + (1 - cc)}
    mine = tensor
    y_other = (1 - yy) * 2 + cc
    c_other = yy * 2 + (1 - cc)
    both_other = (1 - yy) * 2 + (1 - cc)

    batch = lax.axis_index("batch")
    ring = parts // 2
    at_ring = batch // 2
    at_pair = lax.rem(batch, 2)
    x_peer = {"batch": at_ring * 2 + (1 - at_pair)}

    def z_peer(step):
        return {"batch": lax.rem(at_ring + step, ring) * 2 + at_pair}

    barrier = pltpu.get_barrier_semaphore()
    for peer in (y_peer, c_peer, t_peer):
        pl.semaphore_signal(barrier, inc=1, device_id=peer, device_id_type=MESH)

    @pl.loop(1, parts)
    def _(step):
        peer = {"batch": lax.rem(batch + step, parts)}
        pl.semaphore_signal(barrier, inc=1, device_id=peer, device_id_type=MESH)

    counts = {"local": 0, "y": 0, "c": 0, "t": 0}

    def local(src, dst):
        at = counts["local"]
        counts["local"] += 1
        copy = pltpu.make_async_copy(src, dst, lsem.at[at])
        copy.start()
        return copy

    def send_y(src, dst):
        at = counts["y"]
        counts["y"] += 1
        copy = pltpu.make_async_remote_copy(
            src_ref=src,
            dst_ref=dst,
            send_sem=ssem.at[at],
            recv_sem=rsem.at[at],
            device_id=y_peer,
            device_id_type=MESH,
        )
        copy.start()
        return copy

    def send_c(src, dst):
        at = counts["c"]
        counts["c"] += 1
        copy = pltpu.make_async_remote_copy(
            src_ref=src,
            dst_ref=dst,
            send_sem=csem.at[at],
            recv_sem=dsem.at[at],
            device_id=c_peer,
            device_id_type=MESH,
        )
        copy.start()
        return copy

    def send_t(src, dst):
        at = counts["t"]
        counts["t"] += 1
        copy = pltpu.make_async_remote_copy(
            src_ref=src,
            dst_ref=dst,
            send_sem=tsem.at[0, at],
            recv_sem=tsem.at[1, at],
            device_id=t_peer,
            device_id_type=MESH,
        )
        copy.start()
        return copy

    own_half = pl.ds(pl.multiple_of(cc * half, half), half)
    other_half = pl.ds(pl.multiple_of((1 - cc) * half, half), half)

    x_copies = [local(x_in.at[n], xf.at[n, mine]) for n in range(lanes)]
    own_rows = pl.ds(pl.multiple_of(cc * cols, cols), cols)
    own_parts = [
        local(wa_in.at[0], act.at[yy, own_rows]),
        local(wa_in.at[1], gp.at[1 + yy, own_rows]),
    ]
    ws_copy = local(ws_in, ws)
    wr_copy = local(wr_in, wr.at[0])
    wa_copy = local(wa_in, wa)
    e_copy = local(e_in, ef.at[0, mine])
    wc_copy = local(wc_in, wc)
    og_copies = [
        local(og_in.at[n, own_half], df.at[n, mine, own_half]) for n in range(lanes)
    ]
    par[mine] = jnp.zeros(par.shape[1:], f32)
    par[mine, 0:3, :] = ob_in[...]
    par[mine, 3:6, :] = ng_in[...]
    par[mine, 6:9, :] = nb_in[...]
    pl.semaphore_wait(barrier, 2 + parts)

    class Gather:
        def __init__(self, ref, at=None, source=None):
            def block(q):
                return ref.at[q] if at is None else ref.at[at, q]

            self.block = block
            source = block(mine) if source is None else source
            self.by_y = send_y(source, block(mine))
            self.by_c = send_c(source, block(mine))

        def finish(self):
            self.by_y.wait_recv()
            self.on = send_c(self.block(y_other), self.block(y_other))
            self.by_c.wait_recv()
            self.on.wait_recv()

        def done(self):
            self.by_y.wait_send()
            self.by_c.wait_send()
            self.on.wait_send()

    class Deal:
        def __init__(self, n):
            to_own = df.at[n, mine, own_half]
            to_other = df.at[n, mine, other_half]
            self.copies = [
                send_y(og_in.at[n, own_half], to_own),
                send_t(og_in.at[n, other_half], to_other),
                send_c(og_in.at[n, other_half], to_other),
            ]

        def finish(self):
            for copy in self.copies:
                copy.wait()

    class Weights:
        def __init__(self):
            self.group = min(parts, 16)
            self.base = batch // self.group * self.group
            self.place = lax.rem(batch, self.group)
            for copy in own_parts:
                copy.wait()
            self.fetch = [
                send_y(self.piece(self.source(k), k), self.piece(self.target(k, mine), k))
                for k in range(3)
            ]
            self.near = {}
            self.far = {}

        def source(self, k):
            return wc_in.at[0] if k == 2 else self.target(k, mine)

        def target(self, k, q):
            if k == 2:
                return wgc.at[q]
            rows = pl.ds(pl.multiple_of(lax.rem(q, 2) * cols, cols), cols)
            return gp.at[1 + q // 2, rows] if k else act.at[q // 2, rows]

        def piece(self, ref, k):
            size = (width if k == 2 else cols) // self.group
            return ref.at[pl.ds(pl.multiple_of(self.place * size, size), size)]

        def hand(self, src, k, step):
            peer = {"batch": self.base + lax.rem(self.place + step, self.group)}
            return pltpu.make_async_remote_copy(
                src_ref=src,
                dst_ref=src,
                send_sem=wsem.at[k, 0],
                recv_sem=wsem.at[k, 1],
                device_id=peer,
                device_id_type=MESH,
            )

        def hand_on(self, k):
            self.near[k] = send_c(self.source(k), self.target(k, mine))
            self.fetch[k].wait_recv()

            @pl.loop(1, self.group)
            def _(step):
                self.hand(self.piece(self.target(k, y_other), k), k, step).start()

        def across(self, k):
            size = width if k == 2 else cols
            rest = self.target(k, y_other).at[pl.ds(0, size - size // self.group)]
            self.hand(rest, k, 1).wait()
            self.far[k] = send_c(self.target(k, y_other), self.target(k, y_other))

        def finish(self, k):
            self.fetch[k].wait_send()
            self.near[k].wait()
            self.far[k].wait()

        def load_cross(self):
            copies = []
            for h in range(width // span):
                rows = pl.ds(h * span, span)
                for step in range(4):
                    q = lax.rem(mine + step, 4)
                    src = wgc.at[q, rows] if step else wc_in.at[0, rows]
                    copies.append(local(src, gp.at[h, :, col_of(q)]))
            return copies

    x_gather = []
    for n in range(lanes):
        x_gather.append(Gather(xf, n, x_in.at[n]))
        if n == 0:
            par_gather = Gather(par)
            weights = Weights()

    for ref in (nacc, pacc, racc, facc, kacc, vacc):
        ref[...] = jnp.zeros(ref.shape, ref.dtype)
    act[2] = jnp.zeros(act.shape[1:], bf16)

    lane_c = lax.broadcasted_iota(jnp.int32, (1, cols), 1)

    def head_f(h):
        return (lane_c // HEAD_DIM == h).astype(f32)

    def head_b(h):
        return head_f(h).astype(bf16)

    lane_w = lax.broadcasted_iota(jnp.int32, (1, 2 * heads * buckets), 1)

    def word_b(h):
        mask = lax.rem(lane_w, heads * buckets) // buckets == h
        return mask.astype(f32).astype(bf16)

    lane_r = lax.broadcasted_iota(jnp.int32, (1, heads * buckets), 1)

    def word_f(h):
        return (lane_r // buckets == h).astype(f32)

    flip = (
        lax.broadcasted_iota(jnp.int32, (half, half), 0)
        + lax.broadcasted_iota(jnp.int32, (half, half), 1)
        == half - 1
    )
    flip = flip.astype(f32).astype(bf16)
    slot = lax.broadcasted_iota(jnp.int32, (1, 128), 1)

    def rows_of(i):
        return pl.ds(pl.multiple_of(i * TILE, TILE), TILE)

    def own_tile(i):
        return pl.ds(pl.multiple_of(cc * half + i * TILE, TILE), TILE)

    def which_half(i):
        return lax.rem(i + cc, 2)

    def half_rows(which):
        return pl.ds(pl.multiple_of(which * half, half), half)

    def col_of(j):
        return pl.ds(pl.multiple_of(j * cols, cols), cols)

    def wide(ref, n, rows):
        return jnp.concatenate([ref[n, q, rows, :] for q in range(4)], axis=1)

    def summed(n, parity, i):
        rows = own_tile(i)
        mine_part = wide(pbuf, n, rows).astype(f32)
        return mine_part + wide(yrecv.at[parity], n, rows_of(i)).astype(f32)

    def put_wide(ref, n, rows, v):
        for q in range(4):
            ref[n, q, rows, :] = v[:, q * cols : (q + 1) * cols].astype(ref.dtype)

    def param(k):
        return jnp.concatenate([par[q, k : k + 1, :] for q in range(4)], axis=1)

    def put_slot(ref, rows, k, v):
        ref[rows, :] = jnp.where(slot == k, v, ref[rows, :])

    def get_slot(rows, k):
        return total(jnp.where(slot == k, lse[rows, :], 0.0))

    code = code_in[0]

    def pick(values):
        whole, two, four = values
        return jnp.where(code == 0, whole, jnp.where(code == 1, two, four))

    def group_of(spots, length):
        return pick((spots * 0, spots // (length // 2), spots // (length // 4)))

    def key_groups(fill, length):
        spots = lax.broadcasted_iota(jnp.int32, (1, length), 1)
        group = group_of(spots, length)
        long = pick((length, length // 2, length // 4))
        ends = spots * 0
        for g in range(fill.shape[1]):
            end = long - (fill[0, g] & (long // 2 - 1))
            ends = jnp.where(group == g, end, ends)
        return jnp.where(spots - group * long < ends, group, -1)

    def build_tables():
        keys = key_groups(fill_in, span)
        ekeys = key_groups(efill_in, espan)

        word = lax.broadcasted_iota(jnp.int32, (2 * heads * buckets, 1), 0)
        hot = (lax.rem(word, buckets) == buckets_in[...]).astype(f32).astype(bf16)

        def moves(size, shift):
            @pl.loop(0, size // TILE)
            def _(k):
                place = lax.broadcasted_iota(jnp.int32, (TILE, size), 0)
                place = place + lax.broadcasted_iota(jnp.int32, (TILE, size), 1)
                place = place + (2 * size + k * TILE - shift)
                smask[rows_of(k), :size] = ((place & (size - 1)) == 0).astype(f32).astype(bf16)

        for table, turned, size, shift in (
            (oh_first, oht_first, half, 0),
            (oh_second, oht_second, span, half),
        ):
            moves(size, shift)
            table[...] = dot(hot[:, :size], smask[:size, :size]).astype(bf16)
            moves(size, shift + half - 1)
            flat = hot[: heads * buckets, :size]
            turned[...] = dot_nt(smask[:size, :size], flat).astype(bf16)

        @pl.loop(0, span // TILE)
        def _(i):
            rows = rows_of(i)
            spots = lax.broadcasted_iota(jnp.int32, (TILE, 1), 0) + i * TILE
            group = group_of(spots, span)
            allowed = (group == keys) & (spots >= lax.broadcasted_iota(jnp.int32, (1, span), 1))
            smask[rows, :] = jnp.where(allowed, 0.0, neg_big).astype(bf16)
            cmask[rows, :] = jnp.where(group == ekeys, 0.0, neg_big).astype(bf16)

    build_tables()

    wi_copy = local(wi_in, wi.at[0])
    wo_copy = local(wo_in, wo.at[0])

    class Reduce:
        def __init__(self, n, parity):
            self.n = n
            self.parity = parity
            self.first = send_c(pbuf.at[n, :, other_half], crecv.at[n])

        def middle(self):
            n = self.n
            self.first.wait_recv()

            @pl.loop(0, tiles)
            def _(i):
                rows = own_tile(i)
                for q in range(4):
                    both = pbuf[n, q, rows, :].astype(f32)
                    both = both + crecv[n, q, rows_of(i), :].astype(f32)
                    pbuf[n, q, rows, :] = both.astype(bf16)

            self.second = send_y(pbuf.at[n, :, own_half], yrecv.at[self.parity, n])

        def finish(self):
            self.first.wait_send()
            self.second.wait()

    class Swap:
        def __init__(self, ref, n, parity):
            place = yrecv.at[parity, n, mine]
            self.copies = [
                send_y(ref.at[n, own_half], place),
                send_t(ref.at[n, other_half], place),
                send_c(ref.at[n, other_half], place),
            ]

        def middle(self):
            pass

        def finish(self):
            for copy in self.copies:
                copy.wait()

    def heads_of(n, parity):
        return jnp.concatenate([yrecv[parity, n, q] for q in range(4)], axis=1)

    def project_heads(n, parity, k):
        @pl.loop(0, 4)
        def _(j):
            rows = heads_of(n, parity)
            at = col_of(j)
            low, high = (gp[1, :, at], gp[2, :, at]) if k else (act[0, :, at], act[1, :, at])
            part = dot(rows[:, : 2 * cols], low) + dot(rows[:, 2 * cols :], high)
            pbuf[n, j, own_half, :] = part.astype(bf16)

    def project_back(n, parity):
        @pl.loop(0, 4)
        def _(j):
            rows = heads_of(n, parity)
            at = pl.ds(pl.multiple_of(lax.rem(j, 2) * cols, cols), cols)
            pbuf[n, j, own_half, :] = dot_nt(rows, gp[j // 2, at, :]).astype(bf16)

    class Scatter:
        def __init__(self, part, from_c, from_y):
            self.part, self.from_c, self.from_y = part, from_c, from_y
            self.first = [
                send_c(part.at[2 * k + 1 - cc, pl.ds(r * half, half)], from_c.at[2 * k + r])
                for k in range(2)
                for r in range(2)
            ]

        def middle(self):
            for copy in self.first:
                copy.wait_recv()
            part = self.part
            for k in range(2):
                for r in range(2):

                    @pl.loop(0, tiles)
                    def _(i, k=k, r=r):
                        rows = rows_of(i + r * tiles)
                        both = part[2 * k + cc, rows, :].astype(f32)
                        both = both + self.from_c[2 * k + r, rows_of(i), :].astype(f32)
                        part[2 * k + cc, rows, :] = both.astype(bf16)

            self.second = [
                send_y(part.at[y_other, pl.ds(r * half, half)], self.from_y.at[r]) for r in range(2)
            ]

        def finish(self, store):
            for copy in self.second:
                copy.wait()
            for copy in self.first:
                copy.wait_send()
            for r in range(2):

                @pl.loop(0, tiles)
                def _(i, r=r):
                    rows = rows_of(i + r * tiles)
                    store(
                        rows,
                        self.part[mine, rows, :].astype(f32)
                        + self.from_y[r, rows_of(i), :].astype(f32),
                    )

    class Share:
        def __init__(self, grad, pair, far, out, at):
            self.grad, self.pair, self.far, self.out, self.at = grad, pair, far, out, at
            self.block = width // parts

            @pl.loop(0, ring)
            def _(z):
                self.near(self.rows(z, 1 - at_pair), pair.at[z]).start()

        def rows(self, z, x):
            start = pl.multiple_of((z * 2 + x) * self.block, self.block)
            return self.grad.at[:, pl.ds(start, self.block), :]

        def near(self, src, dst):
            return pltpu.make_async_remote_copy(
                src_ref=src,
                dst_ref=dst,
                send_sem=bsem.at[self.at, 0],
                recv_sem=bsem.at[self.at, 1],
                device_id=x_peer,
                device_id_type=MESH,
            )

        def away(self, src, dst, step):
            return pltpu.make_async_remote_copy(
                src_ref=src,
                dst_ref=dst,
                send_sem=bsem.at[self.at, 2],
                recv_sem=bsem.at[self.at, 3],
                device_id=z_peer(step),
                device_id_type=MESH,
            )

        def middle(self):
            self.near(self.pair, self.pair).wait()

            @pl.loop(0, ring)
            def _(z):
                for m in range(self.grad.shape[0]):
                    start = pl.multiple_of((z * 2 + at_pair) * self.block, self.block)
                    own = self.grad[m, pl.ds(start, self.block), :].astype(f32)
                    self.pair[z, m] = (own + self.pair[z, m].astype(f32)).astype(bf16)

            @pl.loop(1, ring)
            def _(step):
                self.away(
                    self.pair.at[lax.rem(at_ring + step, ring)], self.far.at[step - 1], step
                ).start()

        def last(self):
            self.away(self.far, self.far, 1).wait()
            self.out[...] = self.pair[at_ring].astype(f32)

            @pl.loop(1, ring)
            def _(step):
                self.out[...] += self.far[step - 1].astype(f32)

    def norm_rows(resid):
        mean = total(resid) * (1.0 / width)
        centred = resid - mean
        var = total(centred * centred) * (1.0 / width)
        rs = lax.rsqrt(var + norm_eps)
        return centred * rs, rs

    def norm_grad(grad, xh, rs, gain, k):
        q = grad * gain
        m1 = total(q) * (1.0 / width)
        m2 = total(q * xh) * (1.0 / width)
        back = rs * (q - m1 - xh * m2)
        nacc[k] += eight(grad * xh)
        nacc[3 + k] += eight(grad)
        nacc[6 + k] += eight(back)
        return back

    at_scale = 2 * lanes * heads

    def give(ref, n):
        return send_c(ref.at[n, :, own_half], ref.at[n, :, own_half])

    def norm_first(n):
        project_heads(n, 1, 0)

        @pl.loop(0, tiles)
        def _(i):
            rows = own_tile(i)
            resid = wide(xf, n, rows).astype(f32) + wide(pbuf, n, rows).astype(f32) + param(0)
            xh, rs = norm_rows(resid)
            put_slot(lse, rows, at_scale + n, rs)
            put_wide(f1, n, rows, xh * param(3) + param(6))

        return give(f1, n)

    def norm_second(n):
        project_heads(n, 0, 1)

        @pl.loop(0, tiles)
        def _(i):
            rows = own_tile(i)
            resid = wide(f1, n, rows).astype(f32) + wide(pbuf, n, rows).astype(f32) + param(1)
            xh, rs = norm_rows(resid)
            put_slot(lse, rows, at_scale + lanes + n, rs)
            put_wide(f2, n, rows, xh * param(4) + param(7))

        return give(f2, n)

    out_copies = []

    def norm_third(n):
        @pl.loop(0, tiles)
        def _(i):
            rows = own_tile(i)
            resid = wide(f2, n, rows).astype(f32) + summed(n, 1, i) + param(2)
            xh, rs = norm_rows(resid)
            out = xh * param(5) + param(8)
            put_wide(pbuf, n, rows, out)
            out_ref[n, rows, :] = pbuf[n, mine, rows, :]
            lout[n, rows_of(i), :] = pbuf[n, c_other, rows, :]
            grad = wide(df, n, rows).astype(f32)
            put_wide(df, n, rows, norm_grad(grad, xh, rs, param(5), 2))

        out_copies.append(send_c(lout.at[n], lrecv.at[n]))
        return give(df, n)

    def norm_second_back(n):
        @pl.loop(0, tiles)
        def _(i):
            rows = own_tile(i)
            grad = wide(df, n, rows).astype(f32) + summed(n, 0, i)
            gain = param(4)
            xh = (wide(f2, n, rows).astype(f32) - param(7)) * (1.0 / gain)
            rs = get_slot(rows, at_scale + lanes + n)
            put_wide(df, n, rows, norm_grad(grad, xh, rs, gain, 1))

    def norm_first_back(n):
        project_back(n, 1)

        @pl.loop(0, tiles)
        def _(i):
            rows = own_tile(i)
            grad = wide(df, n, rows).astype(f32) + wide(pbuf, n, rows).astype(f32)
            gain = param(3)
            xh = (wide(f1, n, rows).astype(f32) - param(6)) * (1.0 / gain)
            rs = get_slot(rows, at_scale + n)
            put_wide(df, n, rows, norm_grad(grad, xh, rs, gain, 0))

    def halves(got, body):
        @pl.loop(0, 2)
        def _(i):
            if got is not None:

                @pl.when(i == 1)
                def _():
                    got.wait()

            which = which_half(i)
            body(which, half_rows(which), i)

    def keep_own(parity, n, which, v):
        @pl.when(which == cc)
        def _():
            yrecv[parity, n, mine] = v

    def each_head(body):
        pl.loop(0, heads, unroll=HEAD_UNROLL)(body)

    def spot(k, h, size, wide=None):
        row = pl.ds(pl.multiple_of(lax.rem(h, 2) * half, half), half)
        col = pl.ds(pl.multiple_of(k * span + (h // 2) * size, size), wide or size)
        return row, col

    def put_head(kind, n, which, h):
        place = spot(0, h, span)
        return pltpu.make_async_copy(
            act.at[(2,) + place], pstore.at[(kind, n, which) + place], psem.at[h]
        )

    def fetch(kind, n, which, at):
        return pltpu.make_async_copy(pstore.at[kind, n, which], act.at[at], qsem.at[at])

    def self_score(n, which, rows, h, diag):
        reach = (which + 1) * half
        qh = qb[n, rows, :] * head_b(h)
        table = oh_second if which else oh_first
        spread = dot(relb[n, rows, :] * word_b(h), table[...])
        bias = pltpu.roll(spread, 0, 1, stride=1, stride_axis=0)
        s = dot_nt(qh, kb[0, :reach, :]) + smask[rows, :reach].astype(f32)
        if n > 0:
            s = jnp.where(diag, total(qh.astype(f32) * kb[n, rows, :].astype(f32)), s)
        return qh, s + bias

    def diagonal(which):
        r = lax.broadcasted_iota(jnp.int32, (half, (which + 1) * half), 0)
        s = lax.broadcasted_iota(jnp.int32, (half, (which + 1) * half), 1)
        return s == r + which * half

    def both_halves(body):
        for which in range(2):
            body(which, pl.ds(which * half, half), (which + 1) * half)

    def project_rows(n):
        def body(which, rows, i):
            x = wide(xf, n, rows)
            q = (dot(x, ws[0]) + pbias[0:1, :]).astype(bf16)
            qb[n, rows, :] = (q.astype(f32) * 0.125).astype(bf16)
            kb[n, rows, :] = dot(x, ws[1]).astype(bf16)
            vb[n, rows, :] = (dot(x, ws[2]) + pbias[1:2, :]).astype(bf16)
            rel = dot(x, wr[0]) + rbias[...]
            high = rel.astype(bf16)
            relb[n, rows, : heads * buckets] = high
            relb[n, rows, heads * buckets :] = (rel - high.astype(f32)).astype(bf16)

        halves(None, body)

    def self_forward(n):
        project_rows(n)

        def body(which, rows, reach):
            macc[...] = jnp.zeros(macc.shape, f32)

            @each_head
            def _(h):
                if n > 0 or which > 0:
                    put_head(0, n, which, h).wait()
                diag = diagonal(which) if n > 0 else None
                qh, s = self_score(n, which, rows, h, diag)
                w = jnp.exp(s - jnp.max(s, axis=1, keepdims=True))
                inverse = 1.0 / total(w)
                if n > 0:
                    own = total(jnp.where(diag, w, 0.0)) * inverse
                    put_slot(lse, rows, n * heads + h, own)
                    w = jnp.where(diag, 0.0, w)
                prob = (w * inverse).astype(bf16)
                act[(2,) + spot(0, h, span, reach)] = prob
                put_head(0, n, which, h).start()
                part = dot(prob, vb[0, :reach, :])
                if n > 0:
                    part = part + own.astype(bf16).astype(f32) * vb[n, rows, :].astype(f32)
                macc[...] += part * head_f(h)

            low = macc[...].astype(bf16)
            att[n, rows, :] = low
            keep_own(1, n, which, low)

        both_halves(body)

    def encoder_rows():
        @pl.loop(0, espan // TILE)
        def _(i):
            rows = rows_of(i)
            e = wide(ef, 0, rows)
            ck[rows, :] = dot(e, wc[1]).astype(bf16)
            cv[rows, :] = (dot(e, wc[2]) + pbias[3:4, :]).astype(bf16)

    def cross_forward(n, got):
        def body(which, rows, i):
            q = (dot(wide(f1, n, rows), wc[0]) + pbias[2:3, :]).astype(bf16)
            cq[n, rows, :] = (q.astype(f32) * 0.125).astype(bf16)
            macc[...] = jnp.zeros(macc.shape, f32)

            @each_head
            def _(h):
                put_head(1, n, which, h).wait()
                s = dot_nt(cq[n, rows, :] * head_b(h), ck[...]) + cmask[rows, :].astype(f32)
                w = jnp.exp(s - jnp.max(s, axis=1, keepdims=True))
                prob = (w * (1.0 / total(w))).astype(bf16)
                act[(2,) + spot(0, h, span)] = prob
                put_head(1, n, which, h).start()
                macc[...] += dot(prob, cv[...]) * head_f(h)

            low = macc[...].astype(bf16)
            catt[n, rows, :] = low
            keep_own(0, n, which, low)

        halves(got, body)

    def ffn_forward(n, got):
        def body(which, rows, i):
            @pl.loop(0, hidden // cols)
            def _(j):
                at = col_of(j)
                pre = dot(wide(f2, n, rows), wi[0, :, at]) + fbias[:, at]
                value, slope = gelu_both(pre)
                act[n, rows, at] = value.astype(bf16)
                gp[n, rows, at] = slope.astype(bf16)

            @pl.loop(0, width // cols)
            def _(j):
                pbuf[n, j, rows, :] = dot(act[n, rows, :], wo[0, :, col_of(j)]).astype(bf16)

        halves(got, body)

    def ffn_backward(n, got):
        def body(which, rows, i):
            @pl.loop(0, hidden // cols)
            def _(j):
                at = col_of(j)
                grad = dot_nt(wide(df, n, rows), wo[0, at, :]) * gp[n, rows, at].astype(f32)
                facc[:, at] += eight(grad)
                gp[n, rows, at] = grad.astype(bf16)

            @pl.loop(0, width // cols)
            def _(j):
                pbuf[n, j, rows, :] = dot_nt(gp[n, rows, :], wi[0, col_of(j), :]).astype(bf16)

        halves(got, body)

    def stacked(ref, n, k, size, wide=None):
        parts = [ref[(n,) + spot(k, h, size, wide)] for h in range(heads)]
        return jnp.concatenate(parts, axis=0)

    def keep_head(h, ds, dh, qh, reach):
        gp[(2,) + spot(0, h, span, reach)] = ds
        act[(2,) + spot(0, h, cols)] = dh
        act[(2,) + spot(1, h, cols)] = qh

    def add_heads(at, reach):
        vacc[:reach, :] += dot_tn(stacked(act, at, 0, span, reach), stacked(act, 2, 0, cols))
        kacc[:reach, :] += dot_tn(stacked(gp, 2, 0, span, reach), stacked(act, 2, 1, cols))

    def cross_backward(n, got, following):
        def body(which, rows, i):
            fetch(1, n, which, i).wait()
            da = dot_nt(wide(df, n, rows), wa[1]).astype(bf16)
            macc[...] = jnp.zeros(macc.shape, f32)

            @each_head
            def _(h):
                qh = cq[n, rows, :] * head_b(h)
                dh = da * head_b(h)
                p = act[(i,) + spot(0, h, span)].astype(f32)
                both = p * dot_nt(dh, cv[...])
                ds = (both - p * total(both)).astype(bf16)
                keep_head(h, ds, dh, qh, espan)
                macc[...] += dot(ds, ck[...]) * head_f(h)

            add_heads(i, espan)
            if following is None:
                fetch(0, late[0], i, i).start()
            else:
                fetch(1, following, which, i).start()
            dq = macc[...] * 0.125
            pacc[2] += eight(dq)
            low = dq.astype(bf16)
            cq[n, rows, :] = low
            keep_own(1, n, which, low)

        halves(got, body)

    def encoder_backward():
        pacc[3] += eight(vacc[...])

        @pl.loop(0, espan // TILE)
        def _(i):
            rows = rows_of(i)
            dk = kacc[rows, :].astype(bf16)
            dv = vacc[rows, :].astype(bf16)
            ck[rows, :] = dk
            cv[rows, :] = dv
            part = dot_nt(dk, wc[1]) + dot_nt(dv, wc[2])
            for q in range(4):
                f2[0, q, rows, :] = part[:, q * cols : (q + 1) * cols].astype(bf16)

    def self_backward(n, following):
        def body(which, rows, reach):
            fetch(0, n, which, which).wait()
            da = dot_nt(wide(df, n, rows), wa[0]).astype(bf16)
            macc[...] = jnp.zeros(macc.shape, f32)
            dracc[...] = jnp.zeros(dracc.shape, f32)
            if n > 0:
                dkacc[...] = jnp.zeros(dkacc.shape, f32)
                dvacc[...] = jnp.zeros(dvacc.shape, f32)

            @each_head
            def _(h):
                qh = qb[n, rows, :] * head_b(h)
                dh = da * head_b(h)
                p = act[(which,) + spot(0, h, span, reach)].astype(f32)
                both = p * dot_nt(dh, vb[0, :reach, :])
                delta = total(both)
                if n > 0:
                    own = get_slot(rows, n * heads + h)
                    own_dp = total(dh.astype(f32) * vb[n, rows, :].astype(f32))
                    delta = delta + own * own_dp
                    own_ds = own * (own_dp - delta)
                    put_slot(lse, rows, n * heads + h, own_ds)
                low = (both - p * delta).astype(bf16)
                keep_head(h, low, dh, qh, reach)
                turned = pltpu.roll(dot(flip, low), 0, 1, stride=1, stride_axis=0)
                table = oht_second if which else oht_first
                dracc[...] += dot(turned.astype(bf16), table[...]) * word_f(h)
                part = dot(low, kb[0, :reach, :])
                if n > 0:
                    own_s = own_ds.astype(bf16).astype(f32)
                    dkacc[...] += own_s * qh.astype(f32)
                    dvacc[...] += own.astype(bf16).astype(f32) * dh.astype(f32)
                    part = part + own_s * kb[n, rows, :].astype(f32)
                macc[...] += part * head_f(h)

            add_heads(which, reach)
            if following is not None:
                fetch(0, following, which, which).start()
            dq = macc[...] * 0.125
            pacc[0] += eight(dq)
            qb[n, rows, :] = dq.astype(bf16)
            drel = dot(flip, dracc[...].astype(bf16))
            racc[...] += eight(dracc[...])
            if n > 0:
                nearest = oht_first[half - 1 : half, :].astype(f32)
                for h in range(heads):
                    extra = get_slot(rows, n * heads + h) * (nearest * word_f(h))
                    drel = drel + extra
                    racc[...] += eight(extra)
                pacc[1] += eight(dvacc[...])
                kb[n, rows, :] = dkacc[...].astype(bf16)
                vb[n, rows, :] = dvacc[...].astype(bf16)
            relb[n, rows, : heads * buckets] = drel.astype(bf16)

        both_halves(body)
        if n == 0:
            pacc[1] += eight(vacc[...])
            kb[0] = kacc[...].astype(bf16)
            vb[0] = vacc[...].astype(bf16)

    def input_terms(n):
        @pl.loop(0, width // cols)
        def _(j):
            at = col_of(j)
            part = dot_nt(qb[n], ws[0, at, :]) + dot_nt(kb[n], ws[1, at, :])
            part = part + dot_nt(vb[n], ws[2, at, :])
            part = part + dot_nt(relb[n, :, : heads * buckets], wr[0, at, :])
            pbuf[n, j] = part.astype(bf16)

    def weight_grad(rows_ref, pieces, lane_count):
        @pl.loop(0, 4)
        def _(j):
            left = jnp.concatenate([rows_ref[n, j] for n in range(lane_count)], axis=0)
            for load, target, size in pieces:
                for start in range(0, size, cols):
                    step = min(cols, size - start)
                    right = jnp.concatenate(
                        [load(n, start, step) for n in range(lane_count)], axis=0
                    )
                    target[col_of(j), start : start + step] = dot_tn(left, right).astype(bf16)

    def of(ref):
        return lambda n, start, step: ref[n, :, start : start + step]

    words = heads * buckets

    order = list(range(lanes))
    late = order[1:] + order[:1]
    ws_copy.wait()
    wr_copy.wait()
    wa_copy.wait()
    reduces = {}
    gots = {}

    def after(n, exchange, following):
        if following is not None:
            following()
        exchange.middle()
        reduces[n] = exchange

    def ready(n, norm):
        def go():
            reduces[n].finish()
            gots[n] = norm(n)

        return go

    deals = []
    for n in order:
        x_copies[n].wait()
        x_gather[n].finish()
        if n == 0:
            par_gather.finish()
            weights.hand_on(0)
        self_forward(n)
        if n == 0:
            e_copy.wait()
            e_gather = Gather(ef, 0)
        after(n, Swap(att, n, 1), None)
        if n == 0:
            weights.hand_on(1)
        if n == 1:
            weights.across(0)
    weights.finish(0)
    wc_copy.wait()
    e_gather.finish()
    encoder_rows()
    ready(order[0], norm_first)()

    def second_of(*those):
        def go():
            if those[0] == order[0]:
                weights.finish(1)
            for n in those:
                ready(n, norm_second)()

        return go

    for k, n in enumerate(order):
        cross_forward(n, gots[n])
        og_copies[n].wait()
        following = order[k + 1] if k + 1 < lanes else None
        norm = ready(following, norm_first) if following else second_of(order[0])
        after(n, Swap(catt, n, 0), norm)
        deals.append(Deal(n))
        if k == 0:
            weights.across(1)
            weights.hand_on(2)
    for h in range(heads):
        put_head(1, order[-1], 0, h).wait()
    wi_copy.wait()
    wo_copy.wait()

    def third_of(n):
        def go():
            deals[n].finish()
            ready(n, norm_third)()

        return go

    for k, n in enumerate(order):
        ffn_forward(n, gots[n])
        if k == 0:
            norm = second_of(*order[1:])
        else:
            norm = third_of(order[0]) if k + 1 == lanes else None
        after(n, Reduce(n, 1), norm)
    for k, n in enumerate(order):
        ffn_backward(n, gots[n])
        after(n, Reduce(n, 0), third_of(order[k + 1]) if k + 1 < lanes else None)
        if k == 0:
            weights.across(2)
    weight_grad(df, [(of(act), wo.at[0], hidden)], lanes)
    def share_part(grad, pair, far, out, part, at):
        columns = pl.ds(part * (hidden // 2), hidden // 2)
        return Share(grad.at[:, :, columns], pair, far, out.at[:, :, columns], at)

    share_o = share_part(wo, xo, zo, go_ref, 0, 0)
    share_o_more = share_part(wo, xo_more, zo_more, go_ref, 1, 10)
    pl.semaphore_signal(free.at[0], inc=1, device_id=c_peer, device_id_type=MESH)
    waited = set()

    def back_of(n, norm, k):
        def go():
            reduces[n].finish()
            norm(n)
            if k not in waited:
                waited.add(k)
                pl.semaphore_wait(free.at[k], 1)
            gots[n] = give(df, n)

        return go

    back_of(late[0], norm_second_back, 0)()
    weight_grad(f2, [(of(gp), wi.at[0], hidden)], lanes)
    share_i = share_part(wi, xi, zi, gi_ref, 0, 1)
    share_i_more = share_part(wi, xi_more, zi_more, gi_ref, 1, 11)
    weights.finish(2)
    loads = weights.load_cross()
    for i in range(2):
        fetch(1, late[0], which_half(i), i).start()
    for k, n in enumerate(late):
        cross_backward(n, gots[n], late[k + 1] if k + 1 < lanes else None)
        after(n, Swap(cq, n, 1), back_of(late[k + 1], norm_second_back, 0) if k + 1 < lanes else None)
        if k == 0:
            share_o.middle()
        if k == 1:
            share_o_more.middle()
        if k == 2:
            share_i.middle()
    weight_grad(df, [(of(catt), ga1.at[0], cols)], lanes)
    share_a1 = Share(ga1, xa1, za1, ga1_ref, 2)
    pl.semaphore_signal(free.at[1], inc=1, device_id=c_peer, device_id_type=MESH)
    encoder_backward()
    e_scatter = Scatter(f2.at[0], ecrecv, eyrecv)
    for copy in loads:
        copy.wait()
    back_of(late[0], norm_first_back, 1)()
    e_scatter.middle()
    weight_grad(f1, [(of(cq), wc.at[0], cols)], lanes)
    weight_grad(
        ef,
        [
            (lambda n, a, b: ck[:, a : a + b], wc.at[1], cols),
            (lambda n, a, b: cv[:, a : a + b], wc.at[2], cols),
        ],
        1,
    )
    share_c = Share(wc, xc, zc, gc_ref, 4)
    share_i_more.middle()
    kacc[...] = jnp.zeros(kacc.shape, f32)
    vacc[...] = jnp.zeros(vacc.shape, f32)
    scatters = {}
    for k, n in enumerate(late):
        gots[n].wait()
        if k + 1 == lanes:
            weight_grad(df, [(of(att), ga0.at[0], cols)], lanes)
            share_a0 = Share(ga0, xa0, za0, ga0_ref, 3)
        self_backward(n, late[k + 1] if k + 1 < lanes else None)
        if k + 1 < lanes:
            input_terms(n)
            scatters[n] = Scatter(pbuf.at[n], crecv.at[n], yrecv.at[0, n])
            back_of(late[k + 1], norm_first_back, 1)()
            scatters[n].middle()
        if k == 0:

            def store_enc(rows, v):
                genc_ref[rows, :] = v

            e_scatter.finish(store_enc)
            share_o.last()
            share_o_more.last()
            share_a1.middle()
        if k == 1:
            share_i.last()
            share_c.middle()
    def last_grad(ref, k, pair, far, at):
        weight_grad(xf, [(of(ref), wc.at[k], cols)], lanes)
        return Share(wc.at[pl.ds(k, 1)], pair, far, gs_ref.at[pl.ds(k, 1)], at)

    last = late[-1]
    share_a0.middle()
    share_v = last_grad(vb, 2, xv, zv, 6)
    share_k = last_grad(kb, 1, xk, zk, 8)
    input_terms(last)
    scatters[last] = Scatter(pbuf.at[last], crecv.at[last], yrecv.at[0, last])
    share_q = last_grad(qb, 0, xq, zq, 9)
    share_v.middle()
    weight_grad(xf, [(of(relb), wr.at[0], words)], lanes)
    share_r = Share(wr, xr, zr, gr_ref, 5)
    scatters[last].middle()
    share_i_more.last()
    share_a1.last()
    def vec_copy(src, dst, k, peer):
        return pltpu.make_async_remote_copy(
            src_ref=src,
            dst_ref=dst,
            send_sem=bsem.at[7, k],
            recv_sem=bsem.at[7, k + 1],
            device_id=peer,
            device_id_type=MESH,
        )

    for k in range(9):
        nsum[k : k + 1, :] = jnp.sum(nacc[k], axis=0, keepdims=True)
    norm_sums = send_c(nsum, nrecv)
    norm_sums.wait()
    for k in range(9):
        row = nsum[k : k + 1, :] + nrecv[k : k + 1, :]
        for q in range(4):
            vquarter[q, k : k + 1, :] = row[:, q * cols : (q + 1) * cols]
    vec[...] = jnp.zeros(vec.shape, f32)
    vec[0:9, :] = vquarter[mine, 0:9, :]
    for k in range(4):
        vec[9 + k : 10 + k, :] = jnp.sum(pacc[k], axis=0, keepdims=True)
    vec[13:14, :words] = jnp.sum(racc[...], axis=0, keepdims=True)
    row = jnp.sum(facc[...], axis=0, keepdims=True)
    for k in range(hidden // cols):
        vec[14 + k : 15 + k, :] = row[:, k * cols : (k + 1) * cols]
    vec_pair = vec_copy(vec, vrecv.at[0], 0, x_peer)
    vec_pair.start()
    share_k.middle()
    for n in order:
        out_copies[n].wait()

        @pl.loop(0, tiles)
        def _(i, n=n):
            rows = pl.ds(pl.multiple_of((1 - cc) * half + i * TILE, TILE), TILE)
            out_ref[n, rows, :] = lrecv[n, rows_of(i), :]

    share_c.last()
    share_q.middle()
    vec_pair.wait()
    vec[...] += vrecv[0]

    @pl.loop(1, ring)
    def _(step):
        vec_copy(vec, vrecv.at[step], 2, z_peer(step)).start()

    for n in late:

        def store_in(rows, v, n=n):
            gin_ref[n, rows, :] = df[n, mine, rows, :].astype(f32) + v

        scatters[n].finish(store_in)
    share_r.middle()
    share_a0.last()
    share_v.last()
    share_k.last()
    share_q.last()
    share_r.last()
    every_vec = vrecv.at[pl.ds(1, ring - 1)]
    vec_copy(every_vec, every_vec, 2, z_peer(1)).wait()
    vec_ref[...] = vec[...]

    @pl.loop(1, ring)
    def _(step):
        vec_ref[...] += vrecv[step]

    for item in x_gather + [par_gather, e_gather]:
        item.done()


def finish_kernel(
    parts,
    out_i,
    gin_i,
    genc_i,
    vec_i,
    gs_i,
    gr_i,
    gc_i,
    ga0_i,
    ga1_i,
    gi_i,
    go_i,
    out_o,
    gin_o,
    genc_o,
    gs_o,
    gr_o,
    gc_o,
    gatt_o,
    gi_o,
    go_o,
    proj_o,
    rel_o,
    ffn_o,
    bias_o,
    gain_o,
    shift_o,
):
    own = lax.axis_index("batch")
    out_o[...] = out_i[...]
    gin_o[...] = gin_i[...]
    gs_o[...] = gs_i[...]
    gc_o[...] = gc_i[...]

    @pl.when(pl.program_id(0) == 0)
    def _():
        genc_o[...] = genc_i[...]
        gr_o[...] = gr_i[0]
        gi_o[...] = gi_i[0]
        go_o[...] = go_i[0].T
        gatt_o[0] = ga0_i[0].T
        gatt_o[1] = ga1_i[0].T
        cols = vec_i.shape[1]

        def chosen(rows, size):
            start = lax.rem(own * size, cols)
            at = lax.broadcasted_iota(jnp.int32, (cols, size), 0)
            at = at - lax.broadcasted_iota(jnp.int32, (cols, size), 1)
            pick = (at == start).astype(f32)
            return jnp.dot(rows, pick, precision=lax.Precision.HIGHEST, preferred_element_type=f32)

        each = cols // parts
        norms = chosen(vec_i[0:16, :], each)
        gain_o[...] = norms[0:3]
        shift_o[...] = norms[3:6]
        bias_o[...] = norms[6:9]
        proj_o[...] = norms[9:13]
        rel_o[...] = chosen(vec_i[8:16, :], rel_o.shape[1])[5:6]
        size = ffn_o.shape[1]
        row = lax.broadcasted_iota(jnp.int32, (vec_i.shape[0], 1), 0)
        line = jnp.where(row == 14 + own * size // cols, vec_i[...], 0.0)
        line = jnp.sum(line, axis=0, keepdims=True)
        ffn_o[...] = chosen(jnp.broadcast_to(line, (8, cols)), size)[0:1]


def per_device(
    layer_in,
    encoder_states,
    w_self,
    w_rel,
    w_cross,
    w_attn_out,
    w_in,
    w_out,
    proj_bias,
    rel_bias,
    ffn_in_bias,
    out_bias,
    norm_gain,
    norm_bias,
    rel_buckets,
    slot_log,
    tgt_fill,
    enc_fill,
    out_grad,
):
    lanes, span, cols = layer_in.shape
    espan = encoder_states.shape[0]
    width = w_self.shape[1]
    hidden = w_in.shape[1]
    heads = cols // HEAD_DIM
    words = w_rel.shape[1]
    buckets = words // heads
    half = span // 2
    parts = lax.axis_size("batch")
    ring = parts // 2
    block = width // parts
    shapes = [(1, cols)] * 3 + [(1, words), (3, cols), (1, cols), (1, cols)]
    shapes += [(1, hidden // 2)] * 4
    vec_rows = -(-(14 + hidden // cols) // 8) * 8
    dims = (lanes, span, espan, cols, width, hidden, heads, buckets, parts)
    any_spec = pl.BlockSpec(memory_space=pl.ANY)
    vmem = pl.BlockSpec(memory_space=pltpu.VMEM)
    V = pltpu.VMEM
    smem = pl.BlockSpec(memory_space=pltpu.SMEM)
    scratch = [
        V((span, span), bf16),
        V((span, espan), bf16),
        V((2 * words, half), bf16),
        V((2 * words, span), bf16),
        V((half, words), bf16),
        V((span, words), bf16),
        V((4, 16, cols), f32),
        V((lanes, 4, span, cols), bf16),
        V((1, 4, espan, cols), bf16),
        V((lanes, 4, span, cols), bf16),
        V((lanes, 4, span, cols), bf16),
        V((lanes, 4, span, cols), bf16),
        V((lanes, span, hidden), bf16),
        V((lanes, span, hidden), bf16),
        V((lanes, span, cols), bf16),
        V((lanes, span, cols), bf16),
        V((lanes, span, cols), bf16),
        V((lanes, span, 2 * words), bf16),
        V((lanes, span, cols), bf16),
        V((lanes, span, cols), bf16),
        V((lanes, span, cols), bf16),
        V((espan, cols), bf16),
        V((espan, cols), bf16),
        V((span, 128), f32),
        V(w_self.shape, bf16),
        V((1,) + w_rel.shape, bf16),
        V(w_cross.shape, bf16),
        V(w_attn_out.shape, bf16),
        V((1,) + w_in.shape, bf16),
        V((1,) + w_out.shape, bf16),
        V((lanes, 4, span, cols), bf16),
        V((lanes, 4, half, cols), bf16),
        V((2, lanes, 4, half, cols), bf16),
        V((lanes, half, cols), bf16),
        V((lanes, half, cols), bf16),
        V((half, cols), f32),
        V((1, width, cols), bf16),
        V((1, width, cols), bf16),
        V((4, espan // 2, cols), bf16),
        V((2, espan // 2, cols), bf16),
        V((span, cols), f32),
        V((span, cols), f32),
        V((half, words), f32),
        V((half, cols), f32),
        V((half, cols), f32),
        V((9, 8, width), f32),
        V((4, 8, cols), f32),
        V((8, words), f32),
        V((8, hidden), f32),
        V((vec_rows, cols), f32),
        V((ring, vec_rows, cols), f32),
        V((4, 16, cols), f32),
        V((16, width), f32),
        V((16, width), f32),
        *[V((ring, m, block, w), bf16) for m, w in shapes],
        *[V((ring - 1, m, block, w), bf16) for m, w in shapes],
        pltpu.SemaphoreType.DMA((64,)),
        pltpu.SemaphoreType.DMA((64,)),
        pltpu.SemaphoreType.DMA((64,)),
        pltpu.SemaphoreType.DMA((128,)),
        pltpu.SemaphoreType.DMA((128,)),
        pltpu.SemaphoreType.DMA((12, 4)),
        pltpu.SemaphoreType.DMA((2, 16)),
        pltpu.SemaphoreType.DMA((3, 2)),
        pltpu.SemaphoreType.DMA((4,)),
        pltpu.SemaphoreType.DMA((2,)),
        pltpu.SemaphoreType.REGULAR((2,)),
    ]
    result, g_in, g_enc, vec, g_self, g_rel, g_cross, g_att0, g_att1, g_win, g_wout, _, _ = pl.pallas_call(
        functools.partial(layer_kernel, dims),
        out_shape=(
            jax.ShapeDtypeStruct((lanes, span, cols), bf16),
            jax.ShapeDtypeStruct((lanes, span, cols), f32),
            jax.ShapeDtypeStruct((espan, cols), f32),
            jax.ShapeDtypeStruct((vec_rows, cols), f32),
            jax.ShapeDtypeStruct((3, block, cols), f32),
            *[jax.ShapeDtypeStruct((m, block, w), f32) for m, w in shapes[3:7]],
            *[jax.ShapeDtypeStruct((1, block, hidden), f32)] * 2,
            jax.ShapeDtypeStruct((4, width, cols), bf16),
            jax.ShapeDtypeStruct((2, lanes, 2, span, hidden), bf16),
        ),
        in_specs=[any_spec] * 3 + [vmem] * 3 + [any_spec] * 6 + [vmem] * 4 + [smem] * 3,
        out_specs=(vmem,) * 11 + (any_spec,) * 2,
        scratch_shapes=scratch,
        compiler_params=pltpu.CompilerParams(
            collective_id=0, has_side_effects=True, vmem_limit_bytes=64 * 2**20
        ),
    )(
        layer_in,
        encoder_states,
        out_grad,
        out_bias,
        norm_gain,
        norm_bias,
        w_self,
        w_rel,
        w_cross,
        w_attn_out,
        w_in,
        w_out,
        proj_bias,
        rel_bias[None],
        ffn_in_bias[None],
        rel_buckets[None],
        slot_log,
        tgt_fill,
        enc_fill,
    )
    each = cols // parts
    flat = [
        jax.ShapeDtypeStruct(result.shape, bf16),
        jax.ShapeDtypeStruct(g_in.shape, f32),
        jax.ShapeDtypeStruct(g_enc.shape, f32),
        jax.ShapeDtypeStruct(g_self.shape, f32),
        jax.ShapeDtypeStruct((block, words), f32),
        jax.ShapeDtypeStruct(g_cross.shape, f32),
        jax.ShapeDtypeStruct((2, cols, block), f32),
        jax.ShapeDtypeStruct((block, hidden), f32),
        jax.ShapeDtypeStruct((hidden, block), f32),
        jax.ShapeDtypeStruct((4, each), f32),
        jax.ShapeDtypeStruct((1, words // parts), f32),
        jax.ShapeDtypeStruct((1, hidden // parts), f32),
        *[jax.ShapeDtypeStruct((3, each), f32)] * 3,
    ]

    def by_lane(v):
        return pl.BlockSpec((1,) + v.shape[1:], lambda i: (i, 0, 0))

    def whole(v):
        return pl.BlockSpec(v.shape, lambda i: (0,) * len(v.shape))

    stepped = (0, 1, 3, 5)
    ins = [result, g_in, g_enc, vec, g_self, g_rel, g_cross, g_att0, g_att1, g_win, g_wout]
    done = pl.pallas_call(
        functools.partial(finish_kernel, parts),
        grid=(lanes,),
        out_shape=flat,
        in_specs=[by_lane(v) if k in (0, 1, 4, 6) else whole(v) for k, v in enumerate(ins)],
        out_specs=[by_lane(v) if k in stepped else whole(v) for k, v in enumerate(flat)],
        compiler_params=pltpu.CompilerParams(vmem_limit_bytes=64 * 2**20),
    )(*ins)
    return tuple(done[:10]) + (done[10][0], done[11][0]) + tuple(done[12:])


def solution(mesh):
    return jax.shard_map(
        per_device,
        mesh=mesh,
        in_specs=(
            P(None, "batch", "tensor"),
            P("batch", "tensor"),
            P(None, None, "tensor"),
            P(None, "tensor"),
            P(None, None, "tensor"),
            P(None, "tensor", None),
            P(None, "tensor"),
            P("tensor", None),
            P(None, "tensor"),
            P("tensor"),
            P("tensor"),
            P(None, "tensor"),
            P(None, "tensor"),
            P(None, "tensor"),
            P(),
            P("batch"),
            P("batch", None),
            P("batch", None),
            P(None, "batch", "tensor"),
        ),
        out_specs=(
            P(None, "batch", "tensor"),
            P(None, "batch", "tensor"),
            P("batch", "tensor"),
            P(None, "batch", "tensor"),
            P("batch", "tensor"),
            P(None, "batch", "tensor"),
            P(None, "tensor", "batch"),
            P("batch", "tensor"),
            P("tensor", "batch"),
            P(None, ("tensor", "batch")),
            P(("tensor", "batch")),
            P(("tensor", "batch")),
            P(None, ("tensor", "batch")),
            P(None, ("tensor", "batch")),
            P(None, ("tensor", "batch")),
        ),
        check_vma=False,
    )
```

```python
import functools

import jax
import jax.numpy as jnp
from jax import lax
from jax.experimental import pallas as pl
from jax.experimental.pallas import tpu as pltpu
from jax.sharding import PartitionSpec as P

HEAD_DIM = 64
norm_eps = 1e-05
neg_big = -1e30
MESH = pl.DeviceIdType.MESH
f32 = jnp.float32
bf16 = jnp.bfloat16
TILE = 128
HEAD_UNROLL = 2


def dot(a, b):
    return jnp.dot(a, b, preferred_element_type=f32)


def dot_nt(a, b):
    return lax.dot_general(a, b, (((1,), (1,)), ((), ())), preferred_element_type=f32)


def dot_tn(a, b):
    return lax.dot_general(a, b, (((0,), (0,)), ((), ())), preferred_element_type=f32)


def total(v):
    return jnp.sum(v, axis=1, keepdims=True)


def eight(v):
    return jnp.sum(v.reshape(v.shape[0] // 8, 8, v.shape[1]), axis=0)


def gelu_both(v):
    half = 0.5 * (1.0 + lax.erf(v * (0.5**0.5)))
    bell = jnp.exp(-0.5 * v * v) * 0.3989422804014327
    return v * half, half + v * bell


def layer_kernel(
    dims,
    x_in,
    e_in,
    og_in,
    ob_in,
    ng_in,
    nb_in,
    ws_in,
    wr_in,
    wc_in,
    wa_in,
    wi_in,
    wo_in,
    pbias,
    rbias,
    fbias,
    buckets_in,
    code_in,
    fill_in,
    efill_in,
    out_ref,
    gin_ref,
    genc_ref,
    vec_ref,
    gs_ref,
    gr_ref,
    gc_ref,
    ga0_ref,
    ga1_ref,
    gi_ref,
    go_ref,
    wgc,
    pstore,
    smask,
    cmask,
    oh_first,
    oh_second,
    oht_first,
    oht_second,
    par,
    xf,
    ef,
    df,
    f1,
    f2,
    act,
    gp,
    qb,
    kb,
    vb,
    relb,
    att,
    catt,
    cq,
    ck,
    cv,
    lse,
    ws,
    wr,
    wc,
    wa,
    wi,
    wo,
    pbuf,
    crecv,
    yrecv,
    lout,
    lrecv,
    macc,
    ga0,
    ga1,
    ecrecv,
    eyrecv,
    kacc,
    vacc,
    dracc,
    dkacc,
    dvacc,
    nacc,
    pacc,
    racc,
    facc,
    vec,
    vrecv,
    vquarter,
    nsum,
    nrecv,
    xq,
    xk,
    xv,
    xr,
    xc,
    xa0,
    xa1,
    xi,
    xi_more,
    xo,
    xo_more,
    zq,
    zk,
    zv,
    zr,
    zc,
    za0,
    za1,
    zi,
    zi_more,
    zo,
    zo_more,
    lsem,
    ssem,
    rsem,
    csem,
    dsem,
    bsem,
    tsem,
    wsem,
    psem,
    qsem,
    free,
):
    lanes, span, espan, cols, width, hidden, heads, buckets, parts = dims
    half = span // 2
    tiles = half // TILE
    tensor = lax.axis_index("tensor")
    yy = tensor // 2
    cc = lax.rem(tensor, 2)
    y_peer = {"tensor": (1 - yy) * 2 + cc}
    c_peer = {"tensor": yy * 2 + (1 - cc)}
    t_peer = {"tensor": (1 - yy) * 2 + (1 - cc)}
    mine = tensor
    y_other = (1 - yy) * 2 + cc
    c_other = yy * 2 + (1 - cc)
    both_other = (1 - yy) * 2 + (1 - cc)

    batch = lax.axis_index("batch")
    ring = parts // 2
    at_ring = batch // 2
    at_pair = lax.rem(batch, 2)
    x_peer = {"batch": at_ring * 2 + (1 - at_pair)}

    def z_peer(step):
        return {"batch": lax.rem(at_ring + step, ring) * 2 + at_pair}

    barrier = pltpu.get_barrier_semaphore()
    for peer in (y_peer, c_peer, t_peer):
        pl.semaphore_signal(barrier, inc=1, device_id=peer, device_id_type=MESH)

    @pl.loop(1, parts)
    def _(step):
        peer = {"batch": lax.rem(batch + step, parts)}
        pl.semaphore_signal(barrier, inc=1, device_id=peer, device_id_type=MESH)

    counts = {"local": 0, "y": 0, "c": 0, "t": 0}

    def local(src, dst):
        at = counts["local"]
        counts["local"] += 1
        copy = pltpu.make_async_copy(src, dst, lsem.at[at])
        copy.start()
        return copy

    def send_y(src, dst):
        at = counts["y"]
        counts["y"] += 1
        copy = pltpu.make_async_remote_copy(
            src_ref=src,
            dst_ref=dst,
            send_sem=ssem.at[at],
            recv_sem=rsem.at[at],
            device_id=y_peer,
            device_id_type=MESH,
        )
        copy.start()
        return copy

    def send_c(src, dst):
        at = counts["c"]
        counts["c"] += 1
        copy = pltpu.make_async_remote_copy(
            src_ref=src,
            dst_ref=dst,
            send_sem=csem.at[at],
            recv_sem=dsem.at[at],
            device_id=c_peer,
            device_id_type=MESH,
        )
        copy.start()
        return copy

    def send_t(src, dst):
        at = counts["t"]
        counts["t"] += 1
        copy = pltpu.make_async_remote_copy(
            src_ref=src,
            dst_ref=dst,
            send_sem=tsem.at[0, at],
            recv_sem=tsem.at[1, at],
            device_id=t_peer,
            device_id_type=MESH,
        )
        copy.start()
        return copy

    own_half = pl.ds(pl.multiple_of(cc * half, half), half)
    other_half = pl.ds(pl.multiple_of((1 - cc) * half, half), half)

    x_copies = [local(x_in.at[n], xf.at[n, mine]) for n in range(lanes)]
    own_rows = pl.ds(pl.multiple_of(cc * cols, cols), cols)
    own_parts = [
        local(wa_in.at[0], act.at[yy, own_rows]),
        local(wa_in.at[1], gp.at[1 + yy, own_rows]),
    ]
    ws_copy = local(ws_in, ws)
    wr_copy = local(wr_in, wr.at[0])
    wa_copy = local(wa_in, wa)
    e_copy = local(e_in, ef.at[0, mine])
    wc_copy = local(wc_in, wc)
    og_copies = [
        local(og_in.at[n, own_half], df.at[n, mine, own_half]) for n in range(lanes)
    ]
    par[mine] = jnp.zeros(par.shape[1:], f32)
    par[mine, 0:3, :] = ob_in[...]
    par[mine, 3:6, :] = ng_in[...]
    par[mine, 6:9, :] = nb_in[...]
    pl.semaphore_wait(barrier, 2 + parts)

    class Gather:
        def __init__(self, ref, at=None, source=None):
            def block(q):
                return ref.at[q] if at is None else ref.at[at, q]

            self.block = block
            source = block(mine) if source is None else source
            self.by_y = send_y(source, block(mine))
            self.by_c = send_c(source, block(mine))

        def finish(self):
            self.by_y.wait_recv()
            self.on = send_c(self.block(y_other), self.block(y_other))
            self.by_c.wait_recv()
            self.on.wait_recv()

        def done(self):
            self.by_y.wait_send()
            self.by_c.wait_send()
            self.on.wait_send()

    class Deal:
        def __init__(self, n):
            to_own = df.at[n, mine, own_half]
            to_other = df.at[n, mine, other_half]
            self.copies = [
                send_y(og_in.at[n, own_half], to_own),
                send_t(og_in.at[n, other_half], to_other),
                send_c(og_in.at[n, other_half], to_other),
            ]

        def finish(self):
            for copy in self.copies:
                copy.wait()

    class Weights:
        def __init__(self):
            self.group = min(parts, 16)
            self.base = batch // self.group * self.group
            self.place = lax.rem(batch, self.group)
            for copy in own_parts:
                copy.wait()
            self.fetch = [
                send_y(self.piece(self.source(k), k), self.piece(self.target(k, mine), k))
                for k in range(3)
            ]
            self.near = {}
            self.far = {}

        def source(self, k):
            return wc_in.at[0] if k == 2 else self.target(k, mine)

        def target(self, k, q):
            if k == 2:
                return wgc.at[q]
            rows = pl.ds(pl.multiple_of(lax.rem(q, 2) * cols, cols), cols)
            return gp.at[1 + q // 2, rows] if k else act.at[q // 2, rows]

        def piece(self, ref, k):
            size = (width if k == 2 else cols) // self.group
            return ref.at[pl.ds(pl.multiple_of(self.place * size, size), size)]

        def hand(self, src, k, step):
            peer = {"batch": self.base + lax.rem(self.place + step, self.group)}
            return pltpu.make_async_remote_copy(
                src_ref=src,
                dst_ref=src,
                send_sem=wsem.at[k, 0],
                recv_sem=wsem.at[k, 1],
                device_id=peer,
                device_id_type=MESH,
            )

        def hand_on(self, k):
            self.near[k] = send_c(self.source(k), self.target(k, mine))
            self.fetch[k].wait_recv()

            @pl.loop(1, self.group)
            def _(step):
                self.hand(self.piece(self.target(k, y_other), k), k, step).start()

        def across(self, k):
            size = width if k == 2 else cols
            rest = self.target(k, y_other).at[pl.ds(0, size - size // self.group)]
            self.hand(rest, k, 1).wait()
            self.far[k] = send_c(self.target(k, y_other), self.target(k, y_other))

        def finish(self, k):
            self.fetch[k].wait_send()
            self.near[k].wait()
            self.far[k].wait()

        def load_cross(self):
            copies = []
            for h in range(width // span):
                rows = pl.ds(h * span, span)
                for step in range(4):
                    q = lax.rem(mine + step, 4)
                    src = wgc.at[q, rows] if step else wc_in.at[0, rows]
                    copies.append(local(src, gp.at[h, :, col_of(q)]))
            return copies

    x_gather = []
    for n in range(lanes):
        x_gather.append(Gather(xf, n, x_in.at[n]))
        if n == 0:
            par_gather = Gather(par)
            weights = Weights()

    for ref in (nacc, pacc, racc, facc, kacc, vacc):
        ref[...] = jnp.zeros(ref.shape, ref.dtype)
    act[2] = jnp.zeros(act.shape[1:], bf16)

    lane_c = lax.broadcasted_iota(jnp.int32, (1, cols), 1)

    def head_f(h):
        return (lane_c // HEAD_DIM == h).astype(f32)

    def head_b(h):
        return head_f(h).astype(bf16)

    lane_w = lax.broadcasted_iota(jnp.int32, (1, 2 * heads * buckets), 1)

    def word_b(h):
        mask = lax.rem(lane_w, heads * buckets) // buckets == h
        return mask.astype(f32).astype(bf16)

    lane_r = lax.broadcasted_iota(jnp.int32, (1, heads * buckets), 1)

    def word_f(h):
        return (lane_r // buckets == h).astype(f32)

    flip = (
        lax.broadcasted_iota(jnp.int32, (half, half), 0)
        + lax.broadcasted_iota(jnp.int32, (half, half), 1)
        == half - 1
    )
    flip = flip.astype(f32).astype(bf16)
    slot = lax.broadcasted_iota(jnp.int32, (1, 128), 1)

    def rows_of(i):
        return pl.ds(pl.multiple_of(i * TILE, TILE), TILE)

    def own_tile(i):
        return pl.ds(pl.multiple_of(cc * half + i * TILE, TILE), TILE)

    def which_half(i):
        return lax.rem(i + cc, 2)

    def half_rows(which):
        return pl.ds(pl.multiple_of(which * half, half), half)

    def col_of(j):
        return pl.ds(pl.multiple_of(j * cols, cols), cols)

    def wide(ref, n, rows):
        return jnp.concatenate([ref[n, q, rows, :] for q in range(4)], axis=1)

    def summed(n, parity, i):
        rows = own_tile(i)
        mine_part = wide(pbuf, n, rows).astype(f32)
        return mine_part + wide(yrecv.at[parity], n, rows_of(i)).astype(f32)

    def put_wide(ref, n, rows, v):
        for q in range(4):
            ref[n, q, rows, :] = v[:, q * cols : (q + 1) * cols].astype(ref.dtype)

    def param(k):
        return jnp.concatenate([par[q, k : k + 1, :] for q in range(4)], axis=1)

    def put_slot(ref, rows, k, v):
        ref[rows, :] = jnp.where(slot == k, v, ref[rows, :])

    def get_slot(rows, k):
        return total(jnp.where(slot == k, lse[rows, :], 0.0))

    code = code_in[0]

    def pick(values):
        whole, two, four = values
        return jnp.where(code == 0, whole, jnp.where(code == 1, two, four))

    def group_of(spots, length):
        return pick((spots * 0, spots // (length // 2), spots // (length // 4)))

    def key_groups(fill, length):
        spots = lax.broadcasted_iota(jnp.int32, (1, length), 1)
        group = group_of(spots, length)
        long = pick((length, length // 2, length // 4))
        ends = spots * 0
        for g in range(fill.shape[1]):
            end = long - (fill[0, g] & (long // 2 - 1))
            ends = jnp.where(group == g, end, ends)
        return jnp.where(spots - group * long < ends, group, -1)

    def build_tables():
        keys = key_groups(fill_in, span)
        ekeys = key_groups(efill_in, espan)

        word = lax.broadcasted_iota(jnp.int32, (2 * heads * buckets, 1), 0)
        hot = (lax.rem(word, buckets) == buckets_in[...]).astype(f32).astype(bf16)

        def moves(size, shift):
            @pl.loop(0, size // TILE)
            def _(k):
                place = lax.broadcasted_iota(jnp.int32, (TILE, size), 0)
                place = place + lax.broadcasted_iota(jnp.int32, (TILE, size), 1)
                place = place + (2 * size + k * TILE - shift)
                smask[rows_of(k), :size] = ((place & (size - 1)) == 0).astype(f32).astype(bf16)

        for table, turned, size, shift in (
            (oh_first, oht_first, half, 0),
            (oh_second, oht_second, span, half),
        ):
            moves(size, shift)
            table[...] = dot(hot[:, :size], smask[:size, :size]).astype(bf16)
            moves(size, shift + half - 1)
            flat = hot[: heads * buckets, :size]
            turned[...] = dot_nt(smask[:size, :size], flat).astype(bf16)

        @pl.loop(0, span // TILE)
        def _(i):
            rows = rows_of(i)
            spots = lax.broadcasted_iota(jnp.int32, (TILE, 1), 0) + i * TILE
            group = group_of(spots, span)
            allowed = (group == keys) & (spots >= lax.broadcasted_iota(jnp.int32, (1, span), 1))
            smask[rows, :] = jnp.where(allowed, 0.0, neg_big).astype(bf16)
            cmask[rows, :] = jnp.where(group == ekeys, 0.0, neg_big).astype(bf16)

    build_tables()

    wi_copy = local(wi_in, wi.at[0])
    wo_copy = local(wo_in, wo.at[0])

    class Reduce:
        def __init__(self, n, parity):
            self.n = n
            self.parity = parity
            self.first = send_c(pbuf.at[n, :, other_half], crecv.at[n])

        def middle(self):
            n = self.n
            self.first.wait_recv()

            @pl.loop(0, tiles)
            def _(i):
                rows = own_tile(i)
                for q in range(4):
                    both = pbuf[n, q, rows, :].astype(f32)
                    both = both + crecv[n, q, rows_of(i), :].astype(f32)
                    pbuf[n, q, rows, :] = both.astype(bf16)

            self.second = send_y(pbuf.at[n, :, own_half], yrecv.at[self.parity, n])

        def finish(self):
            self.first.wait_send()
            self.second.wait()

    class Swap:
        def __init__(self, ref, n, parity):
            place = yrecv.at[parity, n, mine]
            self.copies = [
                send_y(ref.at[n, own_half], place),
                send_t(ref.at[n, other_half], place),
                send_c(ref.at[n, other_half], place),
            ]

        def middle(self):
            pass

        def finish(self):
            for copy in self.copies:
                copy.wait()

    def heads_of(n, parity):
        return jnp.concatenate([yrecv[parity, n, q] for q in range(4)], axis=1)

    def project_heads(n, parity, k):
        @pl.loop(0, 4)
        def _(j):
            rows = heads_of(n, parity)
            at = col_of(j)
            low, high = (gp[1, :, at], gp[2, :, at]) if k else (act[0, :, at], act[1, :, at])
            part = dot(rows[:, : 2 * cols], low) + dot(rows[:, 2 * cols :], high)
            pbuf[n, j, own_half, :] = part.astype(bf16)

    def project_back(n, parity):
        @pl.loop(0, 4)
        def _(j):
            rows = heads_of(n, parity)
            at = pl.ds(pl.multiple_of(lax.rem(j, 2) * cols, cols), cols)
            pbuf[n, j, own_half, :] = dot_nt(rows, gp[j // 2, at, :]).astype(bf16)

    class Scatter:
        def __init__(self, part, from_c, from_y):
            self.part, self.from_c, self.from_y = part, from_c, from_y
            self.first = [
                send_c(part.at[2 * k + 1 - cc, pl.ds(r * half, half)], from_c.at[2 * k + r])
                for k in range(2)
                for r in range(2)
            ]

        def middle(self):
            for copy in self.first:
                copy.wait_recv()
            part = self.part
            for k in range(2):
                for r in range(2):

                    @pl.loop(0, tiles)
                    def _(i, k=k, r=r):
                        rows = rows_of(i + r * tiles)
                        both = part[2 * k + cc, rows, :].astype(f32)
                        both = both + self.from_c[2 * k + r, rows_of(i), :].astype(f32)
                        part[2 * k + cc, rows, :] = both.astype(bf16)

            self.second = [
                send_y(part.at[y_other, pl.ds(r * half, half)], self.from_y.at[r]) for r in range(2)
            ]

        def finish(self, store):
            for copy in self.second:
                copy.wait()
            for copy in self.first:
                copy.wait_send()
            for r in range(2):

                @pl.loop(0, tiles)
                def _(i, r=r):
                    rows = rows_of(i + r * tiles)
                    store(
                        rows,
                        self.part[mine, rows, :].astype(f32)
                        + self.from_y[r, rows_of(i), :].astype(f32),
                    )

    class Share:
        def __init__(self, grad, pair, far, out, at):
            self.grad, self.pair, self.far, self.out, self.at = grad, pair, far, out, at
            self.block = width // parts

            @pl.loop(0, ring)
            def _(z):
                self.near(self.rows(z, 1 - at_pair), pair.at[z]).start()

        def rows(self, z, x):
            start = pl.multiple_of((z * 2 + x) * self.block, self.block)
            return self.grad.at[:, pl.ds(start, self.block), :]

        def near(self, src, dst):
            return pltpu.make_async_remote_copy(
                src_ref=src,
                dst_ref=dst,
                send_sem=bsem.at[self.at, 0],
                recv_sem=bsem.at[self.at, 1],
                device_id=x_peer,
                device_id_type=MESH,
            )

        def away(self, src, dst, step):
            return pltpu.make_async_remote_copy(
                src_ref=src,
                dst_ref=dst,
                send_sem=bsem.at[self.at, 2],
                recv_sem=bsem.at[self.at, 3],
                device_id=z_peer(step),
                device_id_type=MESH,
            )

        def middle(self):
            self.near(self.pair, self.pair).wait()

            @pl.loop(0, ring)
            def _(z):
                for m in range(self.grad.shape[0]):
                    start = pl.multiple_of((z * 2 + at_pair) * self.block, self.block)
                    own = self.grad[m, pl.ds(start, self.block), :].astype(f32)
                    self.pair[z, m] = (own + self.pair[z, m].astype(f32)).astype(bf16)

            @pl.loop(1, ring)
            def _(step):
                self.away(
                    self.pair.at[lax.rem(at_ring + step, ring)], self.far.at[step - 1], step
                ).start()

        def last(self):
            self.away(self.far, self.far, 1).wait()
            self.out[...] = self.pair[at_ring].astype(f32)

            @pl.loop(1, ring)
            def _(step):
                self.out[...] += self.far[step - 1].astype(f32)

    def norm_rows(resid):
        mean = total(resid) * (1.0 / width)
        centred = resid - mean
        var = total(centred * centred) * (1.0 / width)
        rs = lax.rsqrt(var + norm_eps)
        return centred * rs, rs

    def norm_grad(grad, xh, rs, gain, k):
        q = grad * gain
        m1 = total(q) * (1.0 / width)
        m2 = total(q * xh) * (1.0 / width)
        back = rs * (q - m1 - xh * m2)
        nacc[k] += eight(grad * xh)
        nacc[3 + k] += eight(grad)
        nacc[6 + k] += eight(back)
        return back

    at_scale = 2 * lanes * heads

    def give(ref, n):
        return send_c(ref.at[n, :, own_half], ref.at[n, :, own_half])

    def norm_first(n):
        project_heads(n, 1, 0)

        @pl.loop(0, tiles)
        def _(i):
            rows = own_tile(i)
            resid = wide(xf, n, rows).astype(f32) + wide(pbuf, n, rows).astype(f32) + param(0)
            xh, rs = norm_rows(resid)
            put_slot(lse, rows, at_scale + n, rs)
            put_wide(f1, n, rows, xh * param(3) + param(6))

        return give(f1, n)

    def norm_second(n):
        project_heads(n, 0, 1)

        @pl.loop(0, tiles)
        def _(i):
            rows = own_tile(i)
            resid = wide(f1, n, rows).astype(f32) + wide(pbuf, n, rows).astype(f32) + param(1)
            xh, rs = norm_rows(resid)
            put_slot(lse, rows, at_scale + lanes + n, rs)
            put_wide(f2, n, rows, xh * param(4) + param(7))

        return give(f2, n)

    out_copies = []

    def norm_third(n):
        @pl.loop(0, tiles)
        def _(i):
            rows = own_tile(i)
            resid = wide(f2, n, rows).astype(f32) + summed(n, 1, i) + param(2)
            xh, rs = norm_rows(resid)
            out = xh * param(5) + param(8)
            put_wide(pbuf, n, rows, out)
            out_ref[n, rows, :] = pbuf[n, mine, rows, :]
            lout[n, rows_of(i), :] = pbuf[n, c_other, rows, :]
            grad = wide(df, n, rows).astype(f32)
            put_wide(df, n, rows, norm_grad(grad, xh, rs, param(5), 2))

        out_copies.append(send_c(lout.at[n], lrecv.at[n]))
        return give(df, n)

    def norm_second_back(n):
        @pl.loop(0, tiles)
        def _(i):
            rows = own_tile(i)
            grad = wide(df, n, rows).astype(f32) + summed(n, 0, i)
            gain = param(4)
            xh = (wide(f2, n, rows).astype(f32) - param(7)) * (1.0 / gain)
            rs = get_slot(rows, at_scale + lanes + n)
            put_wide(df, n, rows, norm_grad(grad, xh, rs, gain, 1))

    def norm_first_back(n):
        project_back(n, 1)

        @pl.loop(0, tiles)
        def _(i):
            rows = own_tile(i)
            grad = wide(df, n, rows).astype(f32) + wide(pbuf, n, rows).astype(f32)
            gain = param(3)
            xh = (wide(f1, n, rows).astype(f32) - param(6)) * (1.0 / gain)
            rs = get_slot(rows, at_scale + n)
            put_wide(df, n, rows, norm_grad(grad, xh, rs, gain, 0))

    def halves(got, body):
        @pl.loop(0, 2)
        def _(i):
            if got is not None:

                @pl.when(i == 1)
                def _():
                    got.wait()

            which = which_half(i)
            body(which, half_rows(which), i)

    def keep_own(parity, n, which, v):
        @pl.when(which == cc)
        def _():
            yrecv[parity, n, mine] = v

    def each_head(body):
        pl.loop(0, heads, unroll=HEAD_UNROLL)(body)

    def spot(k, h, size, wide=None):
        row = pl.ds(pl.multiple_of(lax.rem(h, 2) * half, half), half)
        col = pl.ds(pl.multiple_of(k * span + (h // 2) * size, size), wide or size)
        return row, col

    def put_head(kind, n, which, h):
        place = spot(0, h, span)
        return pltpu.make_async_copy(
            act.at[(2,) + place], pstore.at[(kind, n, which) + place], psem.at[h]
        )

    def fetch(kind, n, which, at):
        return pltpu.make_async_copy(pstore.at[kind, n, which], act.at[at], qsem.at[at])

    def self_score(n, which, rows, h, diag):
        reach = (which + 1) * half
        qh = qb[n, rows, :] * head_b(h)
        table = oh_second if which else oh_first
        spread = dot(relb[n, rows, :] * word_b(h), table[...])
        bias = pltpu.roll(spread, 0, 1, stride=1, stride_axis=0)
        s = dot_nt(qh, kb[0, :reach, :]) + smask[rows, :reach].astype(f32)
        if n > 0:
            s = jnp.where(diag, total(qh.astype(f32) * kb[n, rows, :].astype(f32)), s)
        return qh, s + bias

    def diagonal(which):
        r = lax.broadcasted_iota(jnp.int32, (half, (which + 1) * half), 0)
        s = lax.broadcasted_iota(jnp.int32, (half, (which + 1) * half), 1)
        return s == r + which * half

    def both_halves(body):
        for which in range(2):
            body(which, pl.ds(which * half, half), (which + 1) * half)

    def project_rows(n):
        def body(which, rows, i):
            x = wide(xf, n, rows)
            q = (dot(x, ws[0]) + pbias[0:1, :]).astype(bf16)
            qb[n, rows, :] = (q.astype(f32) * 0.125).astype(bf16)
            kb[n, rows, :] = dot(x, ws[1]).astype(bf16)
            vb[n, rows, :] = (dot(x, ws[2]) + pbias[1:2, :]).astype(bf16)
            rel = dot(x, wr[0]) + rbias[...]
            high = rel.astype(bf16)
            relb[n, rows, : heads * buckets] = high
            relb[n, rows, heads * buckets :] = (rel - high.astype(f32)).astype(bf16)

        halves(None, body)

    def self_forward(n):
        project_rows(n)

        def body(which, rows, reach):
            macc[...] = jnp.zeros(macc.shape, f32)

            @each_head
            def _(h):
                if n > 0 or which > 0:
                    put_head(0, n, which, h).wait()
                diag = diagonal(which) if n > 0 else None
                qh, s = self_score(n, which, rows, h, diag)
                w = jnp.exp(s - jnp.max(s, axis=1, keepdims=True))
                inverse = 1.0 / total(w)
                if n > 0:
                    own = total(jnp.where(diag, w, 0.0)) * inverse
                    put_slot(lse, rows, n * heads + h, own)
                    w = jnp.where(diag, 0.0, w)
                prob = (w * inverse).astype(bf16)
                act[(2,) + spot(0, h, span, reach)] = prob
                put_head(0, n, which, h).start()
                part = dot(prob, vb[0, :reach, :])
                if n > 0:
                    part = part + own.astype(bf16).astype(f32) * vb[n, rows, :].astype(f32)
                macc[...] += part * head_f(h)

            low = macc[...].astype(bf16)
            att[n, rows, :] = low
            keep_own(1, n, which, low)

        both_halves(body)

    def encoder_rows():
        @pl.loop(0, espan // TILE)
        def _(i):
            rows = rows_of(i)
            e = wide(ef, 0, rows)
            ck[rows, :] = dot(e, wc[1]).astype(bf16)
            cv[rows, :] = (dot(e, wc[2]) + pbias[3:4, :]).astype(bf16)

    def cross_forward(n, got):
        def body(which, rows, i):
            q = (dot(wide(f1, n, rows), wc[0]) + pbias[2:3, :]).astype(bf16)
            cq[n, rows, :] = (q.astype(f32) * 0.125).astype(bf16)
            macc[...] = jnp.zeros(macc.shape, f32)

            @each_head
            def _(h):
                put_head(1, n, which, h).wait()
                s = dot_nt(cq[n, rows, :] * head_b(h), ck[...]) + cmask[rows, :].astype(f32)
                w = jnp.exp(s - jnp.max(s, axis=1, keepdims=True))
                prob = (w * (1.0 / total(w))).astype(bf16)
                act[(2,) + spot(0, h, span)] = prob
                put_head(1, n, which, h).start()
                macc[...] += dot(prob, cv[...]) * head_f(h)

            low = macc[...].astype(bf16)
            catt[n, rows, :] = low
            keep_own(0, n, which, low)

        halves(got, body)

    def ffn_forward(n, got):
        def body(which, rows, i):
            @pl.loop(0, hidden // cols)
            def _(j):
                at = col_of(j)
                pre = dot(wide(f2, n, rows), wi[0, :, at]) + fbias[:, at]
                value, slope = gelu_both(pre)
                act[n, rows, at] = value.astype(bf16)
                gp[n, rows, at] = slope.astype(bf16)

            @pl.loop(0, width // cols)
            def _(j):
                pbuf[n, j, rows, :] = dot(act[n, rows, :], wo[0, :, col_of(j)]).astype(bf16)

        halves(got, body)

    def ffn_backward(n, got):
        def body(which, rows, i):
            @pl.loop(0, hidden // cols)
            def _(j):
                at = col_of(j)
                grad = dot_nt(wide(df, n, rows), wo[0, at, :]) * gp[n, rows, at].astype(f32)
                facc[:, at] += eight(grad)
                gp[n, rows, at] = grad.astype(bf16)

            @pl.loop(0, width // cols)
            def _(j):
                pbuf[n, j, rows, :] = dot_nt(gp[n, rows, :], wi[0, col_of(j), :]).astype(bf16)

        halves(got, body)

    def stacked(ref, n, k, size, wide=None):
        parts = [ref[(n,) + spot(k, h, size, wide)] for h in range(heads)]
        return jnp.concatenate(parts, axis=0)

    def keep_head(h, ds, dh, qh, reach):
        gp[(2,) + spot(0, h, span, reach)] = ds
        act[(2,) + spot(0, h, cols)] = dh
        act[(2,) + spot(1, h, cols)] = qh

    def add_heads(at, reach):
        vacc[:reach, :] += dot_tn(stacked(act, at, 0, span, reach), stacked(act, 2, 0, cols))
        kacc[:reach, :] += dot_tn(stacked(gp, 2, 0, span, reach), stacked(act, 2, 1, cols))

    def cross_backward(n, got, following):
        def body(which, rows, i):
            fetch(1, n, which, i).wait()
            da = dot_nt(wide(df, n, rows), wa[1]).astype(bf16)
            macc[...] = jnp.zeros(macc.shape, f32)

            @each_head
            def _(h):
                qh = cq[n, rows, :] * head_b(h)
                dh = da * head_b(h)
                p = act[(i,) + spot(0, h, span)].astype(f32)
                both = p * dot_nt(dh, cv[...])
                ds = (both - p * total(both)).astype(bf16)
                keep_head(h, ds, dh, qh, espan)
                macc[...] += dot(ds, ck[...]) * head_f(h)

            add_heads(i, espan)
            if following is None:
                fetch(0, late[0], i, i).start()
            else:
                fetch(1, following, which, i).start()
            dq = macc[...] * 0.125
            pacc[2] += eight(dq)
            low = dq.astype(bf16)
            cq[n, rows, :] = low
            keep_own(1, n, which, low)

        halves(got, body)

    def encoder_backward():
        pacc[3] += eight(vacc[...])

        @pl.loop(0, espan // TILE)
        def _(i):
            rows = rows_of(i)
            dk = kacc[rows, :].astype(bf16)
            dv = vacc[rows, :].astype(bf16)
            ck[rows, :] = dk
            cv[rows, :] = dv
            part = dot_nt(dk, wc[1]) + dot_nt(dv, wc[2])
            for q in range(4):
                f2[0, q, rows, :] = part[:, q * cols : (q + 1) * cols].astype(bf16)

    def self_backward(n, following):
        def body(which, rows, reach):
            fetch(0, n, which, which).wait()
            da = dot_nt(wide(df, n, rows), wa[0]).astype(bf16)
            macc[...] = jnp.zeros(macc.shape, f32)
            dracc[...] = jnp.zeros(dracc.shape, f32)
            if n > 0:
                dkacc[...] = jnp.zeros(dkacc.shape, f32)
                dvacc[...] = jnp.zeros(dvacc.shape, f32)

            @each_head
            def _(h):
                qh = qb[n, rows, :] * head_b(h)
                dh = da * head_b(h)
                p = act[(which,) + spot(0, h, span, reach)].astype(f32)
                both = p * dot_nt(dh, vb[0, :reach, :])
                delta = total(both)
                if n > 0:
                    own = get_slot(rows, n * heads + h)
                    own_dp = total(dh.astype(f32) * vb[n, rows, :].astype(f32))
                    delta = delta + own * own_dp
                    own_ds = own * (own_dp - delta)
                    put_slot(lse, rows, n * heads + h, own_ds)
                low = (both - p * delta).astype(bf16)
                keep_head(h, low, dh, qh, reach)
                turned = pltpu.roll(dot(flip, low), 0, 1, stride=1, stride_axis=0)
                table = oht_second if which else oht_first
                dracc[...] += dot(turned.astype(bf16), table[...]) * word_f(h)
                part = dot(low, kb[0, :reach, :])
                if n > 0:
                    own_s = own_ds.astype(bf16).astype(f32)
                    dkacc[...] += own_s * qh.astype(f32)
                    dvacc[...] += own.astype(bf16).astype(f32) * dh.astype(f32)
                    part = part + own_s * kb[n, rows, :].astype(f32)
                macc[...] += part * head_f(h)

            add_heads(which, reach)
            if following is not None:
                fetch(0, following, which, which).start()
            dq = macc[...] * 0.125
            pacc[0] += eight(dq)
            qb[n, rows, :] = dq.astype(bf16)
            drel = dot(flip, dracc[...].astype(bf16))
            racc[...] += eight(dracc[...])
            if n > 0:
                nearest = oht_first[half - 1 : half, :].astype(f32)
                for h in range(heads):
                    extra = get_slot(rows, n * heads + h) * (nearest * word_f(h))
                    drel = drel + extra
                    racc[...] += eight(extra)
                pacc[1] += eight(dvacc[...])
                kb[n, rows, :] = dkacc[...].astype(bf16)
                vb[n, rows, :] = dvacc[...].astype(bf16)
            relb[n, rows, : heads * buckets] = drel.astype(bf16)

        both_halves(body)
        if n == 0:
            pacc[1] += eight(vacc[...])
            kb[0] = kacc[...].astype(bf16)
            vb[0] = vacc[...].astype(bf16)

    def input_terms(n):
        @pl.loop(0, width // cols)
        def _(j):
            at = col_of(j)
            part = dot_nt(qb[n], ws[0, at, :]) + dot_nt(kb[n], ws[1, at, :])
            part = part + dot_nt(vb[n], ws[2, at, :])
            part = part + dot_nt(relb[n, :, : heads * buckets], wr[0, at, :])
            pbuf[n, j] = part.astype(bf16)

    def weight_grad(rows_ref, pieces, lane_count):
        @pl.loop(0, 4)
        def _(j):
            left = jnp.concatenate([rows_ref[n, j] for n in range(lane_count)], axis=0)
            for load, target, size in pieces:
                for start in range(0, size, cols):
                    step = min(cols, size - start)
                    right = jnp.concatenate(
                        [load(n, start, step) for n in range(lane_count)], axis=0
                    )
                    target[col_of(j), start : start + step] = dot_tn(left, right).astype(bf16)

    def of(ref):
        return lambda n, start, step: ref[n, :, start : start + step]

    words = heads * buckets

    order = list(range(lanes))
    late = order[1:] + order[:1]
    ws_copy.wait()
    wr_copy.wait()
    wa_copy.wait()
    reduces = {}
    gots = {}

    def after(n, exchange, following):
        if following is not None:
            following()
        exchange.middle()
        reduces[n] = exchange

    def ready(n, norm):
        def go():
            reduces[n].finish()
            gots[n] = norm(n)

        return go

    deals = []
    for n in order:
        x_copies[n].wait()
        x_gather[n].finish()
        if n == 0:
            par_gather.finish()
            weights.hand_on(0)
        self_forward(n)
        if n == 0:
            e_copy.wait()
            e_gather = Gather(ef, 0)
        after(n, Swap(att, n, 1), None)
        if n == 0:
            weights.hand_on(1)
        if n == 1:
            weights.across(0)
    weights.finish(0)
    wc_copy.wait()
    e_gather.finish()
    encoder_rows()
    ready(order[0], norm_first)()

    def second_of(*those):
        def go():
            if those[0] == order[0]:
                weights.finish(1)
            for n in those:
                ready(n, norm_second)()

        return go

    for k, n in enumerate(order):
        cross_forward(n, gots[n])
        og_copies[n].wait()
        following = order[k + 1] if k + 1 < lanes else None
        norm = ready(following, norm_first) if following else second_of(order[0])
        after(n, Swap(catt, n, 0), norm)
        deals.append(Deal(n))
        if k == 0:
            weights.across(1)
            weights.hand_on(2)
    for h in range(heads):
        put_head(1, order[-1], 0, h).wait()
    wi_copy.wait()
    wo_copy.wait()

    def third_of(n):
        def go():
            deals[n].finish()
            ready(n, norm_third)()

        return go

    for k, n in enumerate(order):
        ffn_forward(n, gots[n])
        if k == 0:
            norm = second_of(*order[1:])
        else:
            norm = third_of(order[0]) if k + 1 == lanes else None
        after(n, Reduce(n, 1), norm)
    for k, n in enumerate(order):
        ffn_backward(n, gots[n])
        after(n, Reduce(n, 0), third_of(order[k + 1]) if k + 1 < lanes else None)
        if k == 0:
            weights.across(2)
    weight_grad(df, [(of(act), wo.at[0], hidden)], lanes)
    def share_part(grad, pair, far, out, part, at):
        columns = pl.ds(part * (hidden // 2), hidden // 2)
        return Share(grad.at[:, :, columns], pair, far, out.at[:, :, columns], at)

    share_o = share_part(wo, xo, zo, go_ref, 0, 0)
    share_o_more = share_part(wo, xo_more, zo_more, go_ref, 1, 10)
    pl.semaphore_signal(free.at[0], inc=1, device_id=c_peer, device_id_type=MESH)
    waited = set()

    def back_of(n, norm, k):
        def go():
            reduces[n].finish()
            norm(n)
            if k not in waited:
                waited.add(k)
                pl.semaphore_wait(free.at[k], 1)
            gots[n] = give(df, n)

        return go

    back_of(late[0], norm_second_back, 0)()
    weight_grad(f2, [(of(gp), wi.at[0], hidden)], lanes)
    share_i = share_part(wi, xi, zi, gi_ref, 0, 1)
    share_i_more = share_part(wi, xi_more, zi_more, gi_ref, 1, 11)
    weights.finish(2)
    loads = weights.load_cross()
    for i in range(2):
        fetch(1, late[0], which_half(i), i).start()
    for k, n in enumerate(late):
        cross_backward(n, gots[n], late[k + 1] if k + 1 < lanes else None)
        after(n, Swap(cq, n, 1), back_of(late[k + 1], norm_second_back, 0) if k + 1 < lanes else None)
        if k == 0:
            share_o.middle()
        if k == 1:
            share_o_more.middle()
        if k == 2:
            share_i.middle()
    weight_grad(df, [(of(catt), ga1.at[0], cols)], lanes)
    share_a1 = Share(ga1, xa1, za1, ga1_ref, 2)
    pl.semaphore_signal(free.at[1], inc=1, device_id=c_peer, device_id_type=MESH)
    encoder_backward()
    e_scatter = Scatter(f2.at[0], ecrecv, eyrecv)
    for copy in loads:
        copy.wait()
    back_of(late[0], norm_first_back, 1)()
    e_scatter.middle()
    weight_grad(f1, [(of(cq), wc.at[0], cols)], lanes)
    weight_grad(
        ef,
        [
            (lambda n, a, b: ck[:, a : a + b], wc.at[1], cols),
            (lambda n, a, b: cv[:, a : a + b], wc.at[2], cols),
        ],
        1,
    )
    share_c = Share(wc, xc, zc, gc_ref, 4)
    share_i_more.middle()
    kacc[...] = jnp.zeros(kacc.shape, f32)
    vacc[...] = jnp.zeros(vacc.shape, f32)
    scatters = {}
    for k, n in enumerate(late):
        gots[n].wait()
        if k + 1 == lanes:
            weight_grad(df, [(of(att), ga0.at[0], cols)], lanes)
            share_a0 = Share(ga0, xa0, za0, ga0_ref, 3)
        self_backward(n, late[k + 1] if k + 1 < lanes else None)
        if k + 1 < lanes:
            input_terms(n)
            scatters[n] = Scatter(pbuf.at[n], crecv.at[n], yrecv.at[0, n])
            back_of(late[k + 1], norm_first_back, 1)()
            scatters[n].middle()
        if k == 0:

            def store_enc(rows, v):
                genc_ref[rows, :] = v

            e_scatter.finish(store_enc)
            share_o.last()
            share_o_more.last()
            share_a1.middle()
        if k == 1:
            share_i.last()
            share_c.middle()
    def last_grad(ref, k, pair, far, at):
        weight_grad(xf, [(of(ref), wc.at[k], cols)], lanes)
        return Share(wc.at[pl.ds(k, 1)], pair, far, gs_ref.at[pl.ds(k, 1)], at)

    last = late[-1]
    share_a0.middle()
    share_v = last_grad(vb, 2, xv, zv, 6)
    share_k = last_grad(kb, 1, xk, zk, 8)
    input_terms(last)
    scatters[last] = Scatter(pbuf.at[last], crecv.at[last], yrecv.at[0, last])
    share_q = last_grad(qb, 0, xq, zq, 9)
    share_v.middle()
    weight_grad(xf, [(of(relb), wr.at[0], words)], lanes)
    share_r = Share(wr, xr, zr, gr_ref, 5)
    scatters[last].middle()
    share_i_more.last()
    share_a1.last()
    def vec_copy(src, dst, k, peer):
        return pltpu.make_async_remote_copy(
            src_ref=src,
            dst_ref=dst,
            send_sem=bsem.at[7, k],
            recv_sem=bsem.at[7, k + 1],
            device_id=peer,
            device_id_type=MESH,
        )

    for k in range(9):
        nsum[k : k + 1, :] = jnp.sum(nacc[k], axis=0, keepdims=True)
    norm_sums = send_c(nsum, nrecv)
    norm_sums.wait()
    for k in range(9):
        row = nsum[k : k + 1, :] + nrecv[k : k + 1, :]
        for q in range(4):
            vquarter[q, k : k + 1, :] = row[:, q * cols : (q + 1) * cols]
    vec[...] = jnp.zeros(vec.shape, f32)
    vec[0:9, :] = vquarter[mine, 0:9, :]
    for k in range(4):
        vec[9 + k : 10 + k, :] = jnp.sum(pacc[k], axis=0, keepdims=True)
    vec[13:14, :words] = jnp.sum(racc[...], axis=0, keepdims=True)
    row = jnp.sum(facc[...], axis=0, keepdims=True)
    for k in range(hidden // cols):
        vec[14 + k : 15 + k, :] = row[:, k * cols : (k + 1) * cols]
    vec_pair = vec_copy(vec, vrecv.at[0], 0, x_peer)
    vec_pair.start()
    share_k.middle()
    for n in order:
        out_copies[n].wait()

        @pl.loop(0, tiles)
        def _(i, n=n):
            rows = pl.ds(pl.multiple_of((1 - cc) * half + i * TILE, TILE), TILE)
            out_ref[n, rows, :] = lrecv[n, rows_of(i), :]

    share_c.last()
    share_q.middle()
    vec_pair.wait()
    vec[...] += vrecv[0]

    @pl.loop(1, ring)
    def _(step):
        vec_copy(vec, vrecv.at[step], 2, z_peer(step)).start()

    for n in late:

        def store_in(rows, v, n=n):
            gin_ref[n, rows, :] = df[n, mine, rows, :].astype(f32) + v

        scatters[n].finish(store_in)
    share_r.middle()
    share_a0.last()
    share_v.last()
    share_k.last()
    share_q.last()
    share_r.last()
    every_vec = vrecv.at[pl.ds(1, ring - 1)]
    vec_copy(every_vec, every_vec, 2, z_peer(1)).wait()
    vec_ref[...] = vec[...]

    @pl.loop(1, ring)
    def _(step):
        vec_ref[...] += vrecv[step]

    for item in x_gather + [par_gather, e_gather]:
        item.done()


def finish_kernel(
    parts,
    out_i,
    gin_i,
    genc_i,
    vec_i,
    gs_i,
    gr_i,
    gc_i,
    ga0_i,
    ga1_i,
    gi_i,
    go_i,
    out_o,
    gin_o,
    genc_o,
    gs_o,
    gr_o,
    gc_o,
    gatt_o,
    gi_o,
    go_o,
    proj_o,
    rel_o,
    ffn_o,
    bias_o,
    gain_o,
    shift_o,
):
    own = lax.axis_index("batch")
    out_o[...] = out_i[...]
    gin_o[...] = gin_i[...]
    gs_o[...] = gs_i[...]
    gc_o[...] = gc_i[...]

    def rest():
        genc_o[...] = genc_i[...]
        gr_o[...] = gr_i[0]
        gi_o[...] = gi_i[0]
        go_o[...] = go_i[0].T
        gatt_o[0] = ga0_i[0].T
        gatt_o[1] = ga1_i[0].T
        cols = vec_i.shape[1]

        def chosen(rows, size):
            start = lax.rem(own * size, cols)
            at = lax.broadcasted_iota(jnp.int32, (cols, size), 0)
            at = at - lax.broadcasted_iota(jnp.int32, (cols, size), 1)
            pick = (at == start).astype(f32)
            return jnp.dot(rows, pick, precision=lax.Precision.HIGHEST, preferred_element_type=f32)

        each = cols // parts
        norms = chosen(vec_i[0:16, :], each)
        gain_o[...] = norms[0:3]
        shift_o[...] = norms[3:6]
        bias_o[...] = norms[6:9]
        proj_o[...] = norms[9:13]
        rel_o[...] = chosen(vec_i[8:16, :], rel_o.shape[1])[5:6]
        size = ffn_o.shape[1]
        row = lax.broadcasted_iota(jnp.int32, (vec_i.shape[0], 1), 0)
        line = jnp.where(row == 14 + own * size // cols, vec_i[...], 0.0)
        line = jnp.sum(line, axis=0, keepdims=True)
        ffn_o[...] = chosen(jnp.broadcast_to(line, (8, cols)), size)[0:1]

    rest()


def per_device(
    layer_in,
    encoder_states,
    w_self,
    w_rel,
    w_cross,
    w_attn_out,
    w_in,
    w_out,
    proj_bias,
    rel_bias,
    ffn_in_bias,
    out_bias,
    norm_gain,
    norm_bias,
    rel_buckets,
    slot_log,
    tgt_fill,
    enc_fill,
    out_grad,
):
    lanes, span, cols = layer_in.shape
    espan = encoder_states.shape[0]
    width = w_self.shape[1]
    hidden = w_in.shape[1]
    heads = cols // HEAD_DIM
    words = w_rel.shape[1]
    buckets = words // heads
    half = span // 2
    parts = lax.axis_size("batch")
    ring = parts // 2
    block = width // parts
    shapes = [(1, cols)] * 3 + [(1, words), (3, cols), (1, cols), (1, cols)]
    shapes += [(1, hidden // 2)] * 4
    vec_rows = -(-(14 + hidden // cols) // 8) * 8
    dims = (lanes, span, espan, cols, width, hidden, heads, buckets, parts)
    any_spec = pl.BlockSpec(memory_space=pl.ANY)
    vmem = pl.BlockSpec(memory_space=pltpu.VMEM)
    V = pltpu.VMEM
    smem = pl.BlockSpec(memory_space=pltpu.SMEM)
    scratch = [
        V((span, span), bf16),
        V((span, espan), bf16),
        V((2 * words, half), bf16),
        V((2 * words, span), bf16),
        V((half, words), bf16),
        V((span, words), bf16),
        V((4, 16, cols), f32),
        V((lanes, 4, span, cols), bf16),
        V((1, 4, espan, cols), bf16),
        V((lanes, 4, span, cols), bf16),
        V((lanes, 4, span, cols), bf16),
        V((lanes, 4, span, cols), bf16),
        V((lanes, span, hidden), bf16),
        V((lanes, span, hidden), bf16),
        V((lanes, span, cols), bf16),
        V((lanes, span, cols), bf16),
        V((lanes, span, cols), bf16),
        V((lanes, span, 2 * words), bf16),
        V((lanes, span, cols), bf16),
        V((lanes, span, cols), bf16),
        V((lanes, span, cols), bf16),
        V((espan, cols), bf16),
        V((espan, cols), bf16),
        V((span, 128), f32),
        V(w_self.shape, bf16),
        V((1,) + w_rel.shape, bf16),
        V(w_cross.shape, bf16),
        V(w_attn_out.shape, bf16),
        V((1,) + w_in.shape, bf16),
        V((1,) + w_out.shape, bf16),
        V((lanes, 4, span, cols), bf16),
        V((lanes, 4, half, cols), bf16),
        V((2, lanes, 4, half, cols), bf16),
        V((lanes, half, cols), bf16),
        V((lanes, half, cols), bf16),
        V((half, cols), f32),
        V((1, width, cols), bf16),
        V((1, width, cols), bf16),
        V((4, espan // 2, cols), bf16),
        V((2, espan // 2, cols), bf16),
        V((span, cols), f32),
        V((span, cols), f32),
        V((half, words), f32),
        V((half, cols), f32),
        V((half, cols), f32),
        V((9, 8, width), f32),
        V((4, 8, cols), f32),
        V((8, words), f32),
        V((8, hidden), f32),
        V((vec_rows, cols), f32),
        V((ring, vec_rows, cols), f32),
        V((4, 16, cols), f32),
        V((16, width), f32),
        V((16, width), f32),
        *[V((ring, m, block, w), bf16) for m, w in shapes],
        *[V((ring - 1, m, block, w), bf16) for m, w in shapes],
        pltpu.SemaphoreType.DMA((64,)),
        pltpu.SemaphoreType.DMA((64,)),
        pltpu.SemaphoreType.DMA((64,)),
        pltpu.SemaphoreType.DMA((128,)),
        pltpu.SemaphoreType.DMA((128,)),
        pltpu.SemaphoreType.DMA((12, 4)),
        pltpu.SemaphoreType.DMA((2, 16)),
        pltpu.SemaphoreType.DMA((3, 2)),
        pltpu.SemaphoreType.DMA((4,)),
        pltpu.SemaphoreType.DMA((2,)),
        pltpu.SemaphoreType.REGULAR((2,)),
    ]
    result, g_in, g_enc, vec, g_self, g_rel, g_cross, g_att0, g_att1, g_win, g_wout, _, _ = pl.pallas_call(
        functools.partial(layer_kernel, dims),
        out_shape=(
            jax.ShapeDtypeStruct((lanes, span, cols), bf16),
            jax.ShapeDtypeStruct((lanes, span, cols), f32),
            jax.ShapeDtypeStruct((espan, cols), f32),
            jax.ShapeDtypeStruct((vec_rows, cols), f32),
            jax.ShapeDtypeStruct((3, block, cols), f32),
            *[jax.ShapeDtypeStruct((m, block, w), f32) for m, w in shapes[3:7]],
            *[jax.ShapeDtypeStruct((1, block, hidden), f32)] * 2,
            jax.ShapeDtypeStruct((4, width, cols), bf16),
            jax.ShapeDtypeStruct((2, lanes, 2, span, hidden), bf16),
        ),
        in_specs=[any_spec] * 3 + [vmem] * 3 + [any_spec] * 6 + [vmem] * 4 + [smem] * 3,
        out_specs=(vmem,) * 11 + (any_spec,) * 2,
        scratch_shapes=scratch,
        compiler_params=pltpu.CompilerParams(
            collective_id=0, has_side_effects=True, vmem_limit_bytes=64 * 2**20
        ),
    )(
        layer_in,
        encoder_states,
        out_grad,
        out_bias,
        norm_gain,
        norm_bias,
        w_self,
        w_rel,
        w_cross,
        w_attn_out,
        w_in,
        w_out,
        proj_bias,
        rel_bias[None],
        ffn_in_bias[None],
        rel_buckets[None],
        slot_log,
        tgt_fill,
        enc_fill,
    )
    each = cols // parts
    flat = [
        jax.ShapeDtypeStruct(result.shape, bf16),
        jax.ShapeDtypeStruct(g_in.shape, f32),
        jax.ShapeDtypeStruct(g_enc.shape, f32),
        jax.ShapeDtypeStruct(g_self.shape, f32),
        jax.ShapeDtypeStruct((block, words), f32),
        jax.ShapeDtypeStruct(g_cross.shape, f32),
        jax.ShapeDtypeStruct((2, cols, block), f32),
        jax.ShapeDtypeStruct((block, hidden), f32),
        jax.ShapeDtypeStruct((hidden, block), f32),
        jax.ShapeDtypeStruct((4, each), f32),
        jax.ShapeDtypeStruct((1, words // parts), f32),
        jax.ShapeDtypeStruct((1, hidden // parts), f32),
        *[jax.ShapeDtypeStruct((3, each), f32)] * 3,
    ]

    def by_lane(v):
        return pl.BlockSpec((1,) + v.shape[1:], lambda i: (i, 0, 0))

    def whole(v):
        return pl.BlockSpec(v.shape, lambda i: (0,) * len(v.shape))

    stepped = (0, 1, 3, 5)
    ins = [result, g_in, g_enc, vec, g_self, g_rel, g_cross, g_att0, g_att1, g_win, g_wout]
    done = pl.pallas_call(
        functools.partial(finish_kernel, parts),
        out_shape=flat,
        in_specs=[vmem] * len(ins),
        out_specs=[vmem] * len(flat),
        compiler_params=pltpu.CompilerParams(vmem_limit_bytes=64 * 2**20),
    )(*ins)
    return tuple(done[:10]) + (done[10][0], done[11][0]) + tuple(done[12:])


def solution(mesh):
    return jax.shard_map(
        per_device,
        mesh=mesh,
        in_specs=(
            P(None, "batch", "tensor"),
            P("batch", "tensor"),
            P(None, None, "tensor"),
            P(None, "tensor"),
            P(None, None, "tensor"),
            P(None, "tensor", None),
            P(None, "tensor"),
            P("tensor", None),
            P(None, "tensor"),
            P("tensor"),
            P("tensor"),
            P(None, "tensor"),
            P(None, "tensor"),
            P(None, "tensor"),
            P(),
            P("batch"),
            P("batch", None),
            P("batch", None),
            P(None, "batch", "tensor"),
        ),
        out_specs=(
            P(None, "batch", "tensor"),
            P(None, "batch", "tensor"),
            P("batch", "tensor"),
            P(None, "batch", "tensor"),
            P("batch", "tensor"),
            P(None, "batch", "tensor"),
            P(None, "tensor", "batch"),
            P("batch", "tensor"),
            P("tensor", "batch"),
            P(None, ("tensor", "batch")),
            P(("tensor", "batch")),
            P(("tensor", "batch")),
            P(None, ("tensor", "batch")),
            P(None, ("tensor", "batch")),
            P(None, ("tensor", "batch")),
        ),
        check_vma=False,
    )
```
